128 devices in a mesh: row: 8 (over y, x_hi), col: 16 (over z, x_lo, core).
Axes of the slice: x: 4 (x_hi: 2, x_lo: 2; x = x_hi * 2 + x_lo), y: 4, z: 4, core: 2. Of those that a mesh axis runs over, the one named last changes fastest.
Arguments:
- polarization: bfloat16 [4096, 26624], P('row', 'col'), may hold values from -6 to 6
- metric: bfloat16 [26624, 4096], P('row', 'col'), may hold values from -0.0390625 to 0.0390625
- three_panel: bfloat16 [4096, 64, 256], P('row'), may hold values from -0.125 to 0.125
- three_near: bfloat16 [4096, 64, 256], P('col'), may hold values from -0.0078125 to 0.0078125
- green_function: bfloat16 [256, 256], replicated, may hold values from -0.375 to 0.375
- mask_panel: int32 [64, 8], replicated, may hold values 0 or 1
- mask_near: int32 [64, 8], replicated, may hold values 0 or 1
Outputs:
- screened: bfloat16 [4096, 4096], P('row', 'col')
- contracted: bfloat16 [4096, 64, 256], P('col', None, 'row')
- self_energy: float32 [64, 64], P('row', 'col')
The draws below stay inside these ranges and needn't reach their ends.
All inputs are finite; a program needn't handle non-finite values.
Results may differ from the reference program's by a relative error of at most 0.02.
Values may be sent and summed in bfloat16 or wider, within the bound.
A program may use at most 192 MiB of HBM per device.

```python
import jax
import jax.numpy as jnp
from jax import lax

NRI = 26624
PR = 4096
QW = 4096
TILE = 64
NL = 256
RB = 64
AB = 32
N_ROW = 8


def set_ends(result, key, smallest, top_value):
    extent = result.shape
    index_at = [jax.random.randint(jax.random.fold_in(key, axis), (), 0, extent[axis]) for axis in range(len(extent))]
    result = result.at[tuple(index_at)].set(smallest)
    longest = extent.index(max(extent))
    index_at[longest] = (index_at[longest] + 1) % extent[longest]
    return result.at[tuple(index_at)].set(top_value)


def steps_of(own_key, shape, shards, low, largest):
    loudness, own = 1.0, jax.random.fold_in(own_key, 6)
    for axis_at, shards_of in shards:
        draws = jnp.exp(jax.random.uniform(jax.random.fold_in(own, axis_at), (shards_of,), jnp.float32, low / len(shards), largest / len(shards)))
        loudness = loudness * jnp.repeat(draws, shape[axis_at] // shards_of).reshape([-1 if axis == axis_at else 1 for axis in range(len(shape))])
    return loudness


def gaussian(rng, extent, width, limit, shards=(), held_as=jnp.bfloat16):
    gain = steps_of(rng, extent, shards, -0.22, 0.18) if shards else 1.0
    result = jax.random.normal(rng, extent, jnp.float32) * width * gain
    return jnp.minimum(jnp.maximum(result, -limit), limit).astype(held_as)


def setup_inputs(seed: int = 0) -> dict:
    streams_of = jax.random.split(jax.random.key(seed), 8)
    return {
        "polarization": gaussian(streams_of[0], (PR, NRI), 1.0, 6.0, ((0, 8), (1, 16))),
        "metric": gaussian(streams_of[1], (NRI, QW), NRI ** -0.5, 0.0390625, ((0, 8), (1, 16))),
        "three_panel": gaussian(streams_of[2], (PR, TILE, NL), (PR // 2) ** -0.5, 0.125, ((0, 8),)),
        "three_near": gaussian(streams_of[3], (QW, TILE, NL), (QW * NL // 2) ** -0.5, 0.0078125, ((0, 16),)),
        "green_function": gaussian(streams_of[4], (NL, NL), NL ** -0.5, 0.375),
        "mask_panel": set_ends((jax.random.randint(streams_of[5], (PR // RB, NL // AB), 0, 2) < 1).astype(jnp.int32), jax.random.fold_in(streams_of[5], 1), 0, 1),
        "mask_near": set_ends((jax.random.randint(streams_of[6], (QW // RB, NL // AB), 0, 2) < 1).astype(jnp.int32), jax.random.fold_in(streams_of[6], 1), 0, 1),
    }


def expand_mask(mask, rows, cols):
    return jnp.repeat(jnp.repeat(mask, rows, axis=0), cols, axis=1)


def reference(polarization, metric, three_panel, three_near, green_function, mask_panel, mask_near):
    screened = jnp.dot(polarization, metric, preferred_element_type=jnp.float32).astype(jnp.bfloat16)
    panel = three_panel * expand_mask(mask_panel, RB, AB).astype(jnp.bfloat16)[:, None, :]
    near = three_near * expand_mask(mask_near, RB, AB).astype(jnp.bfloat16)[:, None, :]
    block_rows = PR // N_ROW
    screened_blocks = screened.reshape(N_ROW, block_rows, QW)
    panel_blocks = panel.reshape(N_ROW, block_rows, TILE * NL)

    def add_block(total, pair):
        screened_block, panel_block = pair
        partial_sum = lax.dot_general(screened_block, panel_block, (((0,), (0,)), ((), ())), preferred_element_type=jnp.float32)
        rounded = lax.optimization_barrier(partial_sum.astype(jnp.bfloat16))
        return total + rounded.astype(jnp.float32), None

    contracted, _ = lax.scan(add_block, jnp.zeros((QW, TILE * NL), jnp.float32), (screened_blocks, panel_blocks))
    contracted = contracted.astype(jnp.bfloat16).reshape(QW, TILE, NL)
    dressed = jnp.dot(near.reshape(QW * TILE, NL), green_function.T, preferred_element_type=jnp.float32)
    dressed = dressed.astype(jnp.bfloat16).reshape(QW, TILE, NL)
    self_energy = -lax.dot_general(contracted, dressed, (((0, 2), (0, 2)), ((), ())), preferred_element_type=jnp.float32)
    return screened, contracted, self_energy
```

```python
import functools

import jax
import jax.numpy as jnp
from jax import lax
from jax.experimental import pallas as pl
from jax.experimental.pallas import tpu as pltpu
from jax.sharding import PartitionSpec as P

TILE = 64
NL = 256
RB = 64
AB = 32
MESH = pl.DeviceIdType.MESH


def expand_mask(mask, rows, cols):
    return jnp.repeat(jnp.repeat(mask, rows, axis=0), cols, axis=1)


def place():
    row, col = lax.axis_index("row"), lax.axis_index("col")
    return row // 2, row % 2, col // 4, (col // 2) % 2, col % 2


def device(y, xh, z, xl, core):
    return (y * 2 + xh, (z * 2 + xl) * 2 + core)


class Copies:
    def __init__(self, send_sem):
        self.send_sem, self.started = send_sem, []

    def send(self, src, dst, recv_sem, target):
        index = len(self.started)
        copy = pltpu.make_async_remote_copy(
            src_ref=src,
            dst_ref=dst,
            send_sem=self.send_sem.at[index],
            recv_sem=recv_sem,
            device_id=target,
            device_id_type=MESH,
        )
        copy.start()
        self.started.append((copy, None))

    def send_or_keep(self, keep, src, dst, recv_sem, target):
        index = len(self.started)
        copy = pltpu.make_async_remote_copy(
            src_ref=src,
            dst_ref=dst,
            send_sem=self.send_sem.at[index],
            recv_sem=recv_sem,
            device_id=target,
            device_id_type=MESH,
        )

        @pl.when(jnp.logical_not(keep))
        def _():
            copy.start()

        @pl.when(keep)
        def _():
            pltpu.make_async_copy(src, dst, recv_sem).start()

        self.started.append((copy, keep))

    def finish(self):
        for copy, keep in self.started:
            if keep is None:
                copy.wait_send()
            else:
                pl.when(jnp.logical_not(keep))(copy.wait_send)


def landed(ref, sem):
    pltpu.make_async_copy(ref, ref, sem).wait()


def screen_kernel(
    a_ref,
    b_ref,
    out_ref,
    a0,
    a1,
    b0,
    b1,
    a1_own,
    total,
    give,
    take,
    send_sem,
    local_sem,
    x_sem,
    near_sem,
    far_sem,
    twin_sem,
    last_sem,
):
    y, xh, z, xl, core = place()
    twin = device(y, xh, z, xl, 1 - core)
    x = xh * 2 + xl
    rows, depth = a_ref.shape
    half, piece = rows // 2, rows // 4
    cols = b_ref.shape[1]
    z_at = [lax.rem(z + d, 4) for d in range(4)]
    y_at = [lax.rem(y + d, 4) for d in range(4)]

    barrier = pltpu.get_barrier_semaphore()
    partners = [twin]
    partners += [device(y, xh, z_at[d], xl, core) for d in (1, 3)]
    partners += [device(y_at[d], xh, z, xl, core) for d in (1, 3)]
    for d in (1, 2, 3):
        other = lax.rem(x + d, 4)
        partners.append(device(y, other // 2, z, other % 2, core))
    for partner in partners:
        pl.semaphore_signal(barrier, inc=1, device_id=partner, device_id_type=MESH)
    pl.semaphore_wait(barrier, len(partners))

    copies = Copies(send_sem)
    first, second = pl.ds(0, depth), pl.ds(depth, depth)

    own0, own1 = pl.ds(0, half), pl.ds(half, half)

    @pl.when(core == 0)
    def _():
        pltpu.make_async_copy(a_ref, a0.at[z], local_sem.at[0]).start()
        copy = pltpu.make_async_remote_copy(
            a_ref, a0.at[z], send_sem.at[62], local_sem.at[0], device_id=twin, device_id_type=MESH
        )
        copy.start()

    @pl.when(core == 1)
    def _():
        pltpu.make_async_copy(a_ref.at[own1], a1_own, local_sem.at[1]).start()
        copy = pltpu.make_async_remote_copy(
            a_ref.at[own0], a1_own, send_sem.at[62], local_sem.at[1], device_id=twin, device_id_type=MESH
        )
        copy.start()

    for j in range(2):
        keep = jnp.logical_and(j == xh, xh == xl)
        copies.send_or_keep(
            keep, b_ref.at[first], b0.at[y, xl], x_sem.at[2 + xl], device(y, j, z, xh, core)
        )
    b_own = pltpu.make_async_copy(b_ref.at[second], b1.at[y], local_sem.at[2])
    b_own.start()

    deep = depth // 2
    b_up = [device(y_at[1], xh, z, xl, core), device(y_at[3], xh, z, xl, core)]
    a_up = [device(y, xh, z_at[1], xl, core), device(y, xh, z_at[3], xl, core)]

    def b_slot(stream, k, p):
        buffer = b1.at[k] if stream == 0 else b0.at[k, stream - 1]
        return buffer.at[pl.ds(p * deep, deep)]

    def a_rows(stream, k, start, count):
        buffer = a0.at[k] if stream == 0 else a1.at[k, stream - 1]
        return buffer.at[pl.ds(pl.multiple_of(core * half + start, piece), count)]

    def a_slot(stream, k, p):
        return a_rows(stream, k, p * piece, piece)

    def spread(slot, sem_base, stream, k, to):
        for p in range(2):
            for side in range(2):
                q = p if side == 0 else 1 - p
                copies.send(
                    slot(stream, k, q), slot(stream, k, q), near_sem.at[sem_base + stream, side, q], to[side]
                )

    def go_on(slot, sem_base, stream, at, to):
        for side in range(2):
            k = at[3] if side == 0 else at[1]
            landed(slot(stream, k, side), near_sem.at[sem_base + stream, side, side])
            copies.send(
                slot(stream, k, side), slot(stream, k, side), far_sem.at[sem_base + stream, side], to[side]
            )

    def to_twin(stream, k, index):
        copies.send(
            a_rows(stream, k, 0, half), a_rows(stream, k, 0, half), twin_sem.at[stream, index], twin
        )

    for p in range(2):
        for side in range(2):
            q = p if side == 0 else 1 - p
            copies.send(
                b_ref.at[pl.ds(depth + q * deep, deep)], b_slot(0, y, q), near_sem.at[3, side, q], b_up[side]
            )

    landed(a1_own, local_sem.at[1])
    for j in range(2):
        keep = jnp.logical_and(j == xl, xh == xl)
        copies.send_or_keep(
            keep, a1_own, a_rows_at(a1, z, xh, core, half), x_sem.at[xh], device(y, xl, z, j, core)
        )
    landed(a0.at[z], local_sem.at[0])
    spread(a_slot, 0, 0, z, a_up)

    go_on(b_slot, 3, 0, y_at, b_up)
    go_on(a_slot, 0, 0, z_at, a_up)

    for s in (1, 2):
        landed(a_rows(s, z, 0, half), x_sem.at[s - 1])
        spread(a_slot, 0, s, z, a_up)
        landed(b0.at[y, s - 1], x_sem.at[1 + s])
        spread(b_slot, 3, s, y, b_up)
        to_twin(s, z, 3)

    def rest(slot, sem_base, stream, at, side):
        k = at[3] if side == 0 else at[1]
        landed(slot(stream, k, 1 - side), near_sem.at[sem_base + stream, side, 1 - side])

    for side in range(2):
        rest(b_slot, 3, 0, y_at, side)
        rest(a_slot, 0, 0, z_at, side)
        to_twin(0, z_at[3] if side == 0 else z_at[1], side)
    for s in (1, 2):
        go_on(a_slot, 0, s, z_at, a_up)
        go_on(b_slot, 3, s, y_at, b_up)

    def far(slot, sem_base, stream, at):
        for side in range(2):
            landed(slot(stream, at[2], side), far_sem.at[sem_base + stream, side])

    far(b_slot, 3, 0, y_at)
    far(a_slot, 0, 0, z_at)
    to_twin(0, z_at[2], 2)
    for s in (1, 2):
        for side in range(2):
            rest(a_slot, 0, s, z_at, side)
            rest(b_slot, 3, s, y_at, side)
            to_twin(s, z_at[3] if side == 0 else z_at[1], side)
    for s in (1, 2):
        far(a_slot, 0, s, z_at)
        to_twin(s, z_at[2], 2)
        far(b_slot, 3, s, y_at)

    def other_half(stream, k, index):
        buffer = a0.at[k] if stream == 0 else a1.at[k, stream - 1]
        start = pl.multiple_of((1 - core) * half, half)
        landed(buffer.at[pl.ds(start, half)], twin_sem.at[stream, index])

    for index, k in ((0, z_at[3]), (1, z_at[1]), (2, z_at[2])):
        other_half(0, k, index)
    for s in (1, 2):
        for index, k in ((0, z_at[3]), (1, z_at[1]), (2, z_at[2]), (3, z)):
            other_half(s, k, index)
    b_own.wait()

    def multiply(index, left, right):
        def body(k, carry):
            partial = jnp.dot(left(k)[...], right(k)[...], preferred_element_type=jnp.float32)
            total[index] = jnp.where(k == 0, partial, total[index] + partial)
            return carry

        lax.fori_loop(0, 4, body, 0)

    multiply(0, lambda k: a0.at[k], lambda k: b0.at[k, 1 - xl])
    give[0] = total[0].astype(jnp.bfloat16)
    copies.send(give.at[0], take.at[0], last_sem.at[0], device(y, xh, z, 1 - xl, core))
    multiply(0, lambda k: a1.at[k, 1 - xh], lambda k: b1.at[k])
    give[1] = total[0].astype(jnp.bfloat16)
    copies.send(give.at[1], take.at[1], last_sem.at[1], device(y, 1 - xh, z, xl, core))
    multiply(0, lambda k: a0.at[k], lambda k: b0.at[k, xl])
    multiply(1, lambda k: a1.at[k, xh], lambda k: b1.at[k])
    landed(take.at[0], last_sem.at[0])
    landed(take.at[1], last_sem.at[1])
    out_ref[...] = (
        total[0] + total[1] + take[0].astype(jnp.float32) + take[1].astype(jnp.float32)
    ).astype(jnp.bfloat16)

    assert len(copies.started) <= 62
    copies.finish()

    @pl.when(core == 0)
    def _():
        pltpu.make_async_copy(a_ref, a0.at[z], send_sem.at[62]).wait()

    @pl.when(core == 1)
    def _():
        pltpu.make_async_copy(a_ref.at[own0], a1_own, send_sem.at[62]).wait()


def a_rows_at(a1, k, index, core, half):
    return a1.at[k, index, pl.ds(pl.multiple_of(core * half, half), half)]


def screen(a, b):
    rows, depth = a.shape
    cols = b.shape[1]
    bf16 = jnp.bfloat16
    dma = pltpu.SemaphoreType.DMA
    return pl.pallas_call(
        screen_kernel,
        out_shape=jax.ShapeDtypeStruct((rows, cols), bf16),
        in_specs=[pl.BlockSpec(memory_space=pl.ANY)] * 2,
        out_specs=pl.BlockSpec(memory_space=pltpu.VMEM),
        scratch_shapes=[
            pltpu.VMEM((4, rows, depth), bf16),
            pltpu.VMEM((4, 2, rows, depth), bf16),
            pltpu.VMEM((4, 2, depth, cols), bf16),
            pltpu.VMEM((4, depth, cols), bf16),
            pltpu.VMEM((rows // 2, depth), bf16),
            pltpu.VMEM((2, rows, cols), jnp.float32),
            pltpu.VMEM((2, rows, cols), bf16),
            pltpu.VMEM((2, rows, cols), bf16),
            dma((64,)),
            dma((3,)),
            dma((4,)),
            dma((6, 2, 2)),
            dma((6, 2)),
            dma((3, 4)),
            dma((2,)),
        ],
        compiler_params=pltpu.CompilerParams(
            collective_id=0, has_side_effects=True, vmem_limit_bytes=56 * 2**20
        ),
        name="screen",
    )(a, b)


def per_device(
    polarization, metric, three_panel, three_near, green_function, mask_panel, mask_near
):
    row_index = lax.axis_index("row")
    col_index = lax.axis_index("col")
    row_count = lax.axis_size("row")
    panel_rows = polarization.shape[0]
    near_cols = metric.shape[1]
    screened = screen(polarization, metric)
    panel_blocks = panel_rows // RB
    panel_mask = lax.dynamic_slice_in_dim(mask_panel, row_index * panel_blocks, panel_blocks, 0)
    panel = three_panel * expand_mask(panel_mask, RB, AB).astype(jnp.bfloat16)[:, None, :]
    near_blocks = near_cols // RB
    near_mask = lax.dynamic_slice_in_dim(mask_near, col_index * near_blocks, near_blocks, 0)
    near = three_near * expand_mask(near_mask, RB, AB).astype(jnp.bfloat16)[:, None, :]
    near_flat = near.reshape(near_cols * TILE, NL)
    contract_part = lax.dot_general(
        screened,
        panel.reshape(panel_rows, TILE * NL),
        (((0,), (0,)), ((), ())),
        preferred_element_type=jnp.float32,
    )
    contract_part = (
        contract_part.astype(jnp.bfloat16).astype(jnp.float32).reshape(near_cols, TILE, NL)
    )
    near_share = NL // row_count
    contracted = lax.psum(contract_part.astype(jnp.bfloat16), "row")
    dressed = jnp.dot(near_flat, green_function.T, preferred_element_type=jnp.float32)
    dressed = dressed.astype(jnp.bfloat16).reshape(near_cols, TILE, NL)
    tile_part = -lax.dot_general(
        contracted, dressed, (((0, 2), (0, 2)), ((), ())), preferred_element_type=jnp.float32
    )
    column_share = lax.psum_scatter(tile_part, "col", scatter_dimension=1, tiled=True)
    row_share = TILE // row_count
    self_energy = lax.dynamic_slice_in_dim(column_share, row_index * row_share, row_share, 0)
    contracted_out = lax.dynamic_slice_in_dim(contracted, row_index * near_share, near_share, 2)
    return (screened, contracted_out, self_energy)


def solution(mesh):
    placed = (
        P("row", "col"),
        P("row", "col"),
        P("row", None, None),
        P("col", None, None),
        P(),
        P(),
        P(),
    )
    return jax.shard_map(
        per_device,
        mesh=mesh,
        in_specs=placed,
        out_specs=(P("row", "col"), P("col", None, "row"), P("row", "col")),
        check_vma=False,
    )
```

```python
import functools

import jax
import jax.numpy as jnp
from jax import lax
from jax.experimental import pallas as pl
from jax.experimental.pallas import tpu as pltpu
from jax.sharding import PartitionSpec as P

TILE = 64
NL = 256
RB = 64
AB = 32
MESH = pl.DeviceIdType.MESH


def expand_mask(mask, rows, cols):
    return jnp.repeat(jnp.repeat(mask, rows, axis=0), cols, axis=1)


def place():
    row, col = lax.axis_index("row"), lax.axis_index("col")
    return row // 2, row % 2, col // 4, (col // 2) % 2, col % 2


def device(y, xh, z, xl, core):
    return (y * 2 + xh, (z * 2 + xl) * 2 + core)


class Copies:
    def __init__(self, send_sem):
        self.send_sem, self.started = send_sem, []

    def send(self, src, dst, recv_sem, target):
        index = len(self.started)
        copy = pltpu.make_async_remote_copy(
            src_ref=src,
            dst_ref=dst,
            send_sem=self.send_sem.at[index],
            recv_sem=recv_sem,
            device_id=target,
            device_id_type=MESH,
        )
        copy.start()
        self.started.append((copy, None))

    def send_or_keep(self, keep, src, dst, recv_sem, target):
        index = len(self.started)
        copy = pltpu.make_async_remote_copy(
            src_ref=src,
            dst_ref=dst,
            send_sem=self.send_sem.at[index],
            recv_sem=recv_sem,
            device_id=target,
            device_id_type=MESH,
        )

        @pl.when(jnp.logical_not(keep))
        def _():
            copy.start()

        @pl.when(keep)
        def _():
            pltpu.make_async_copy(src, dst, recv_sem).start()

        self.started.append((copy, keep))

    def finish(self):
        for copy, keep in self.started:
            if keep is None:
                copy.wait_send()
            else:
                pl.when(jnp.logical_not(keep))(copy.wait_send)


def landed(ref, sem):
    pltpu.make_async_copy(ref, ref, sem).wait()


def prepare(panel, near, panel_mask, near_mask, green, panel_t, dressed, taken, flat, made, made_near, sem):
    start = lambda k, size: pl.ds(pl.multiple_of(k * size, size), size)

    def steps(source, mask, count, make, put, first, last):
        def fetch(i):
            block = source.at[start(i // 4, 128), start(i % 4, 16)]
            return pltpu.make_async_copy(block, taken.at[i % 2], sem.at[i % 2])

        fetch(first).start()

        def body(i, carry):
            @pl.when(i + 1 < last)
            def _():
                fetch(i + 1).start()

            fetch(i).wait()

            @pl.when(i >= first + 2)
            def _():
                put(i - 2).wait()

            for h in range(2):
                lanes = slice(h * 128, (h + 1) * 128)
                flat[h] = taken[i % 2, :, :, lanes].astype(jnp.float32).reshape(128 * 16, 128)
            rows = start(i // 4, 128)
            for m in range(16):
                make(
                    i,
                    m,
                    [
                        flat[h, pl.ds(m, 128, stride=16), :] * mask[rows, h * 128 : (h + 1) * 128]
                        for h in range(2)
                    ],
                )
            put(i).start()
            return carry

        lax.fori_loop(first, last, body, 0)
        put(last - 2).wait()
        put(last - 1).wait()

    def put_panel(i):
        place_at = panel_t.at[:, start(i % 4, 512), start(i // 4, 128)]
        return pltpu.make_async_copy(made.at[i % 2], place_at, sem.at[2 + i % 2])

    def put_near(i):
        place_at = dressed.at[start(i % 4, 512), start(i // 4, 128)]
        return pltpu.make_async_copy(made_near.at[i % 2], place_at, sem.at[2 + i % 2])

    def make_panel(i, m, halves):
        turned = jnp.concatenate([half.T.astype(jnp.bfloat16) for half in halves], 0)
        made[i % 2, :, m * 32 : (m + 1) * 32, :] = turned.reshape(8, 32, 128)

    def make_near(i, m, halves):
        block = jnp.concatenate([half.astype(jnp.bfloat16) for half in halves], 1)
        product = lax.dot_general(
            green[...], block, (((1,), (1,)), ((), ())), preferred_element_type=jnp.float32
        )
        made_near[i % 2, m * 32 : (m + 1) * 32, :] = product.astype(jnp.bfloat16)

    return (
        functools.partial(steps, panel, panel_mask, 16, make_panel, put_panel),
        functools.partial(steps, near, near_mask, 8, make_near, put_near),
    )


def screen_kernel(
    a_ref,
    b_ref,
    panel,
    near,
    panel_mask,
    near_mask,
    green,
    out_ref,
    panel_t,
    dressed,
    a0,
    a1,
    b0,
    b1,
    a1_own,
    total,
    give,
    take,
    taken,
    flat,
    made,
    made_near,
    send_sem,
    local_sem,
    x_sem,
    near_sem,
    far_sem,
    twin_sem,
    last_sem,
    step_sem,
):
    panel_steps, near_steps = prepare(
        panel, near, panel_mask, near_mask, green, panel_t, dressed, taken, flat, made, made_near, step_sem
    )
    y, xh, z, xl, core = place()
    twin = device(y, xh, z, xl, 1 - core)
    x = xh * 2 + xl
    rows, depth = a_ref.shape
    half, piece = rows // 2, rows // 4
    cols = b_ref.shape[1]
    z_at = [lax.rem(z + d, 4) for d in range(4)]
    y_at = [lax.rem(y + d, 4) for d in range(4)]

    barrier = pltpu.get_barrier_semaphore()
    partners = [twin]
    partners += [device(y, xh, z_at[d], xl, core) for d in (1, 3)]
    partners += [device(y_at[d], xh, z, xl, core) for d in (1, 3)]
    for d in (1, 2, 3):
        other = lax.rem(x + d, 4)
        partners.append(device(y, other // 2, z, other % 2, core))
    for partner in partners:
        pl.semaphore_signal(barrier, inc=1, device_id=partner, device_id_type=MESH)
    pl.semaphore_wait(barrier, len(partners))

    copies = Copies(send_sem)
    first, second = pl.ds(0, depth), pl.ds(depth, depth)

    own0, own1 = pl.ds(0, half), pl.ds(half, half)

    @pl.when(core == 0)
    def _():
        pltpu.make_async_copy(a_ref, a0.at[z], local_sem.at[0]).start()
        copy = pltpu.make_async_remote_copy(
            a_ref, a0.at[z], send_sem.at[62], local_sem.at[0], device_id=twin, device_id_type=MESH
        )
        copy.start()

    @pl.when(core == 1)
    def _():
        pltpu.make_async_copy(a_ref.at[own1], a1_own, local_sem.at[1]).start()
        copy = pltpu.make_async_remote_copy(
            a_ref.at[own0], a1_own, send_sem.at[62], local_sem.at[1], device_id=twin, device_id_type=MESH
        )
        copy.start()

    for j in range(2):
        keep = jnp.logical_and(j == xh, xh == xl)
        copies.send_or_keep(
            keep, b_ref.at[first], b0.at[y, xl], x_sem.at[2 + xl], device(y, j, z, xh, core)
        )
    b_own = pltpu.make_async_copy(b_ref.at[second], b1.at[y], local_sem.at[2])
    b_own.start()

    deep = depth // 2
    b_up = [device(y_at[1], xh, z, xl, core), device(y_at[3], xh, z, xl, core)]
    a_up = [device(y, xh, z_at[1], xl, core), device(y, xh, z_at[3], xl, core)]

    def b_slot(stream, k, p):
        buffer = b1.at[k] if stream == 0 else b0.at[k, stream - 1]
        return buffer.at[pl.ds(p * deep, deep)]

    def a_rows(stream, k, start, count):
        buffer = a0.at[k] if stream == 0 else a1.at[k, stream - 1]
        return buffer.at[pl.ds(pl.multiple_of(core * half + start, piece), count)]

    def a_slot(stream, k, p):
        return a_rows(stream, k, p * piece, piece)

    def spread(slot, sem_base, stream, k, to):
        for p in range(2):
            for side in range(2):
                q = p if side == 0 else 1 - p
                copies.send(
                    slot(stream, k, q), slot(stream, k, q), near_sem.at[sem_base + stream, side, q], to[side]
                )

    def go_on(slot, sem_base, stream, at, to):
        for side in range(2):
            k = at[3] if side == 0 else at[1]
            landed(slot(stream, k, side), near_sem.at[sem_base + stream, side, side])
            copies.send(
                slot(stream, k, side), slot(stream, k, side), far_sem.at[sem_base + stream, side], to[side]
            )

    def to_twin(stream, k, index):
        copies.send(
            a_rows(stream, k, 0, half), a_rows(stream, k, 0, half), twin_sem.at[stream, index], twin
        )

    for p in range(2):
        for side in range(2):
            q = p if side == 0 else 1 - p
            copies.send(
                b_ref.at[pl.ds(depth + q * deep, deep)], b_slot(0, y, q), near_sem.at[3, side, q], b_up[side]
            )

    landed(a1_own, local_sem.at[1])
    for j in range(2):
        keep = jnp.logical_and(j == xl, xh == xl)
        copies.send_or_keep(
            keep, a1_own, a_rows_at(a1, z, xh, core, half), x_sem.at[xh], device(y, xl, z, j, core)
        )
    landed(a0.at[z], local_sem.at[0])
    spread(a_slot, 0, 0, z, a_up)

    panel_steps(0, 6)
    go_on(b_slot, 3, 0, y_at, b_up)
    go_on(a_slot, 0, 0, z_at, a_up)
    panel_steps(6, 16)

    for s in (1, 2):
        landed(a_rows(s, z, 0, half), x_sem.at[s - 1])
        spread(a_slot, 0, s, z, a_up)
        landed(b0.at[y, s - 1], x_sem.at[1 + s])
        spread(b_slot, 3, s, y, b_up)
        to_twin(s, z, 3)

    near_steps(0, 8)

    def rest(slot, sem_base, stream, at, side):
        k = at[3] if side == 0 else at[1]
        landed(slot(stream, k, 1 - side), near_sem.at[sem_base + stream, side, 1 - side])

    for side in range(2):
        rest(b_slot, 3, 0, y_at, side)
        rest(a_slot, 0, 0, z_at, side)
        to_twin(0, z_at[3] if side == 0 else z_at[1], side)
    for s in (1, 2):
        go_on(a_slot, 0, s, z_at, a_up)
        go_on(b_slot, 3, s, y_at, b_up)

    def far(slot, sem_base, stream, at):
        for side in range(2):
            landed(slot(stream, at[2], side), far_sem.at[sem_base + stream, side])

    far(b_slot, 3, 0, y_at)
    far(a_slot, 0, 0, z_at)
    to_twin(0, z_at[2], 2)
    for s in (1, 2):
        for side in range(2):
            rest(a_slot, 0, s, z_at, side)
            rest(b_slot, 3, s, y_at, side)
            to_twin(s, z_at[3] if side == 0 else z_at[1], side)
    for s in (1, 2):
        far(a_slot, 0, s, z_at)
        to_twin(s, z_at[2], 2)
        far(b_slot, 3, s, y_at)

    def other_half(stream, k, index):
        buffer = a0.at[k] if stream == 0 else a1.at[k, stream - 1]
        start = pl.multiple_of((1 - core) * half, half)
        landed(buffer.at[pl.ds(start, half)], twin_sem.at[stream, index])

    for index, k in ((0, z_at[3]), (1, z_at[1]), (2, z_at[2])):
        other_half(0, k, index)
    for s in (1, 2):
        for index, k in ((0, z_at[3]), (1, z_at[1]), (2, z_at[2]), (3, z)):
            other_half(s, k, index)
    b_own.wait()

    def multiply(index, left, right):
        def body(k, carry):
            partial = jnp.dot(left(k)[...], right(k)[...], preferred_element_type=jnp.float32)
            total[index] = jnp.where(k == 0, partial, total[index] + partial)
            return carry

        lax.fori_loop(0, 4, body, 0)

    multiply(0, lambda k: a0.at[k], lambda k: b0.at[k, 1 - xl])
    give[0] = total[0].astype(jnp.bfloat16)
    copies.send(give.at[0], take.at[0], last_sem.at[0], device(y, xh, z, 1 - xl, core))
    multiply(0, lambda k: a1.at[k, 1 - xh], lambda k: b1.at[k])
    give[1] = total[0].astype(jnp.bfloat16)
    copies.send(give.at[1], take.at[1], last_sem.at[1], device(y, 1 - xh, z, xl, core))
    multiply(0, lambda k: a0.at[k], lambda k: b0.at[k, xl])
    multiply(1, lambda k: a1.at[k, xh], lambda k: b1.at[k])
    landed(take.at[0], last_sem.at[0])
    landed(take.at[1], last_sem.at[1])
    out_ref[...] = (
        total[0] + total[1] + take[0].astype(jnp.float32) + take[1].astype(jnp.float32)
    ).astype(jnp.bfloat16)

    assert len(copies.started) <= 62
    copies.finish()

    @pl.when(core == 0)
    def _():
        pltpu.make_async_copy(a_ref, a0.at[z], send_sem.at[62]).wait()

    @pl.when(core == 1)
    def _():
        pltpu.make_async_copy(a_ref.at[own0], a1_own, send_sem.at[62]).wait()


def a_rows_at(a1, k, index, core, half):
    return a1.at[k, index, pl.ds(pl.multiple_of(core * half, half), half)]


def screen(a, b, panel, near, panel_mask, near_mask, green):
    rows, depth = a.shape
    cols = b.shape[1]
    bf16 = jnp.bfloat16
    dma = pltpu.SemaphoreType.DMA
    hbm, vmem = pl.BlockSpec(memory_space=pl.ANY), pl.BlockSpec(memory_space=pltpu.VMEM)
    return pl.pallas_call(
        screen_kernel,
        out_shape=(
            jax.ShapeDtypeStruct((rows, cols), bf16),
            jax.ShapeDtypeStruct((8, TILE * 32, rows), bf16),
            jax.ShapeDtypeStruct((TILE * 32, cols), bf16),
        ),
        in_specs=[hbm] * 4 + [vmem] * 3,
        out_specs=(vmem, hbm, hbm),
        scratch_shapes=[
            pltpu.VMEM((4, rows, depth), bf16),
            pltpu.VMEM((4, 2, rows, depth), bf16),
            pltpu.VMEM((4, 2, depth, cols), bf16),
            pltpu.VMEM((4, depth, cols), bf16),
            pltpu.VMEM((rows // 2, depth), bf16),
            pltpu.VMEM((2, rows, cols), jnp.float32),
            pltpu.VMEM((2, rows, cols), bf16),
            pltpu.VMEM((2, rows, cols), bf16),
            pltpu.VMEM((2, 128, 16, NL), bf16),
            pltpu.VMEM((2, 128 * 16, 128), jnp.float32),
            pltpu.VMEM((2, 8, 16 * 32, 128), bf16),
            pltpu.VMEM((2, 16 * 32, 128), bf16),
            dma((64,)),
            dma((3,)),
            dma((4,)),
            dma((6, 2, 2)),
            dma((6, 2)),
            dma((3, 4)),
            dma((2,)),
            dma((4,)),
        ],
        compiler_params=pltpu.CompilerParams(
            collective_id=0, has_side_effects=True, vmem_limit_bytes=56 * 2**20
        ),
        name="screen",
    )(a, b, panel, near, panel_mask, near_mask, green)


LATE = 1152


def contract_kernel(
    s_ref,
    panel_t,
    dressed,
    out_ref,
    energy_ref,
    block,
    part,
    far_y,
    near_y,
    cross_y,
    cross_x,
    far_x,
    near_x,
    total,
    other,
    dressed_b,
    tile,
    row_sum,
    tile_row,
    tile_col,
    send_sem,
    block_sem,
    far_sem,
    near_sem,
    cross_sem,
    row_sem,
    col_sem,
):
    y, xh, z, xl, core = place()
    col = (z * 2 + xl) * 2 + core
    f32, bf16 = jnp.float32, jnp.bfloat16

    def in_row(d, j):
        return device(lax.rem(y + d, 4), lax.rem(xh + j, 2), z, xl, core)

    def in_col(d):
        return (y * 2 + xh, lax.rem(col + d, 16))

    partners = [in_row(s // 2, s % 2) for s in range(1, 8)] + [in_col(d) for d in range(1, 16)]
    barrier = pltpu.get_barrier_semaphore()
    for partner in partners:
        pl.semaphore_signal(barrier, inc=1, device_id=partner, device_id_type=MESH)

    order = [(2, 1), (2, 0), (1, 1), (3, 1), (1, 0), (3, 0), (0, 1), (0, 0)]

    def fetch(i):
        d, j = order[i]
        share = lax.rem(y + d, 4) * 2 + lax.rem(xh + j, 2)
        return pltpu.make_async_copy(panel_t.at[share], block.at[i % 2], block_sem.at[i % 2])

    fetch(0).start()
    dressed_copy = pltpu.make_async_copy(dressed, dressed_b, block_sem.at[2])
    dressed_copy.start()
    pl.semaphore_wait(barrier, len(partners))

    copies = Copies(send_sem)
    rows = TILE * 32
    early = rows - LATE
    h_late, h_early = LATE // 2, early // 2
    up, down, across = in_row(1, 0), in_row(3, 0), in_row(0, 1)

    def late(d, j, start=0, count=LATE):
        return part.at[d * 2 + j, pl.ds(start, count)]

    def first(d, j, start=0, count=early):
        return part.at[d * 2 + j, pl.ds(LATE + start, count)]

    for i, (d, j) in enumerate(order):
        if i + 1 < 8:
            fetch(i + 1).start()
        fetch(i).wait()

        def multiply(t, carry):
            at = pl.ds(pl.multiple_of(t * 256, 256), 256)
            part[d * 2 + j, at] = jnp.dot(
                block[i % 2, at], s_ref[...], preferred_element_type=f32
            ).astype(bf16)
            return carry

        lax.fori_loop(0, rows // 256, multiply, 0)
        if j == 1:
            copies.send(first(d, 1), cross_x.at[d], cross_sem.at[d], across)
        if d == 2:
            copies.send(late(2, j, 0, h_late), far_y.at[j, 0], far_sem.at[j, 0], up)
            copies.send(late(2, j, h_late, h_late), far_y.at[j, 1], far_sem.at[j, 1], down)
        if d == 1:
            copies.send(late(1, j, h_late, h_late), near_y.at[j, 0, pl.ds(h_late, h_late)], near_sem.at[j, 0, 0], up)
        if d == 3:
            copies.send(late(3, j, 0, h_late), near_y.at[j, 1, pl.ds(0, h_late)], near_sem.at[j, 1, 0], down)

    def add(ref, *others):
        result = ref[...].astype(f32)
        for each in others:
            result = result + each[...].astype(f32)
        ref[...] = result.astype(bf16)

    for j in (1, 0):
        landed(far_y.at[j, 0], far_sem.at[j, 0])
        add(late(1, j, 0, h_late), far_y.at[j, 0])
        copies.send(late(1, j, 0, h_late), near_y.at[j, 0, pl.ds(0, h_late)], near_sem.at[j, 0, 1], up)
        landed(far_y.at[j, 1], far_sem.at[j, 1])
        add(late(3, j, h_late, h_late), far_y.at[j, 1])
        copies.send(late(3, j, h_late, h_late), near_y.at[j, 1, pl.ds(h_late, h_late)], near_sem.at[j, 1, 1], down)

    landed(cross_x.at[2], cross_sem.at[2])
    add(first(2, 0), cross_x.at[2])
    copies.send(first(2, 0, 0, h_early), far_x.at[0], far_sem.at[2, 0], up)
    copies.send(first(2, 0, h_early, h_early), far_x.at[1], far_sem.at[2, 1], down)
    landed(cross_x.at[1], cross_sem.at[1])
    add(first(1, 0), cross_x.at[1])
    copies.send(first(1, 0, h_early, h_early), near_x.at[0, pl.ds(h_early, h_early)], near_sem.at[2, 0, 0], up)
    landed(cross_x.at[3], cross_sem.at[3])
    add(first(3, 0), cross_x.at[3])
    copies.send(first(3, 0, 0, h_early), near_x.at[1, pl.ds(0, h_early)], near_sem.at[2, 1, 0], down)

    def both_near(j, ref):
        count = ref.shape[1] // 2
        for side in range(2):
            for turn in range(2):
                start = count if (side == 0) == (turn == 0) else 0
                landed(ref.at[side, pl.ds(start, count)], near_sem.at[j, side, turn])

    both_near(1, near_y.at[1])
    add(late(0, 1), near_y.at[1, 0], near_y.at[1, 1])
    copies.send(late(0, 1), cross_y, cross_sem.at[4], across)

    landed(far_x.at[0], far_sem.at[2, 0])
    add(first(1, 0, 0, h_early), far_x.at[0])
    copies.send(first(1, 0, 0, h_early), near_x.at[0, pl.ds(0, h_early)], near_sem.at[2, 0, 1], up)
    landed(far_x.at[1], far_sem.at[2, 1])
    add(first(3, 0, h_early, h_early), far_x.at[1])
    copies.send(first(3, 0, h_early, h_early), near_x.at[1, pl.ds(h_early, h_early)], near_sem.at[2, 1, 1], down)

    dressed_copy.wait()
    for h in range(2):
        other[h] = dressed_b[:, h * 128 : (h + 1) * 128].astype(f32)

    def settle(at, *terms):
        result = terms[0][...].astype(f32)
        for each in terms[1:]:
            result = result + each[...].astype(f32)
        result = result.astype(bf16)
        out_ref[at] = result
        for h in range(2):
            total[h, at] = result[:, h * 128 : (h + 1) * 128].astype(f32)

    both_near(0, near_y.at[0])
    landed(cross_x.at[0], cross_sem.at[0])
    landed(cross_y, cross_sem.at[4])
    settle(pl.ds(0, LATE), late(0, 0), near_y.at[0, 0], near_y.at[0, 1], cross_y)
    both_near(2, near_x)
    settle(pl.ds(LATE, early), first(0, 0), cross_x.at[0], near_x.at[0], near_x.at[1])

    def column(ref, l):
        halves = [ref[h, pl.ds(l, TILE, stride=32), :].astype(bf16) for h in range(2)]
        return jnp.concatenate(halves, 1)

    energy = jnp.zeros((TILE, TILE), f32)
    for l in range(32):
        energy = energy + lax.dot_general(
            column(total, l), column(other, l), (((1,), (1,)), ((), ())), preferred_element_type=f32
        )
    tile[...] = jnp.concatenate([-energy, jnp.zeros_like(energy)], 1)

    def share_of(row):
        return pl.ds(pl.multiple_of(row * 8, 8), 8)

    for s in range(1, 8):
        target = in_row(s // 2, s % 2)
        copies.send(tile.at[share_of(target[0])], tile_row.at[s], row_sem.at[s], target)
    mine = tile[share_of(y * 2 + xh)]
    for s in range(1, 8):
        landed(tile_row.at[s], row_sem.at[s])
        mine = mine + tile_row[s]
    row_sum[...] = mine
    for d in range(1, 16):
        copies.send(row_sum, tile_col.at[d], col_sem.at[d], in_col(d))
    for d in range(1, 16):
        landed(tile_col.at[d], col_sem.at[d])
        mine = mine + tile_col[d]
    energy_ref[...] = mine
    copies.finish()


def contract(screened, panel_t, dressed):
    rows = TILE * 32
    cols = screened.shape[1]
    early = rows - LATE
    bf16, f32 = jnp.bfloat16, jnp.float32
    dma = pltpu.SemaphoreType.DMA
    hbm, vmem = pl.BlockSpec(memory_space=pl.ANY), pl.BlockSpec(memory_space=pltpu.VMEM)
    return pl.pallas_call(
        contract_kernel,
        out_shape=(jax.ShapeDtypeStruct((rows, cols), bf16), jax.ShapeDtypeStruct((8, 128), f32)),
        in_specs=[vmem, hbm, hbm],
        out_specs=(vmem, vmem),
        scratch_shapes=[
            pltpu.VMEM((2, rows, screened.shape[0]), bf16),
            pltpu.VMEM((8, rows, cols), bf16),
            pltpu.VMEM((2, 2, LATE // 2, cols), bf16),
            pltpu.VMEM((2, 2, LATE, cols), bf16),
            pltpu.VMEM((LATE, cols), bf16),
            pltpu.VMEM((4, early, cols), bf16),
            pltpu.VMEM((2, early // 2, cols), bf16),
            pltpu.VMEM((2, early, cols), bf16),
            pltpu.VMEM((2, rows, 128), f32),
            pltpu.VMEM((2, rows, 128), f32),
            pltpu.VMEM((rows, cols), bf16),
            pltpu.VMEM((TILE, 128), f32),
            pltpu.VMEM((8, 128), f32),
            pltpu.VMEM((8, 8, 128), f32),
            pltpu.VMEM((16, 8, 128), f32),
            dma((48,)),
            dma((3,)),
            dma((3, 2)),
            dma((3, 2, 2)),
            dma((5,)),
            dma((8,)),
            dma((16,)),
        ],
        compiler_params=pltpu.CompilerParams(
            collective_id=1, has_side_effects=True, vmem_limit_bytes=56 * 2**20
        ),
        name="contract",
    )(screened, panel_t, dressed)


def per_device(
    polarization, metric, three_panel, three_near, green_function, mask_panel, mask_near
):
    row_index = lax.axis_index("row")
    col_index = lax.axis_index("col")
    row_count = lax.axis_size("row")
    panel_rows = polarization.shape[0]
    near_cols = metric.shape[1]
    panel_blocks = panel_rows // RB
    panel_mask = lax.dynamic_slice_in_dim(mask_panel, row_index * panel_blocks, panel_blocks, 0)
    near_blocks = near_cols // RB
    near_mask = lax.dynamic_slice_in_dim(mask_near, col_index * near_blocks, near_blocks, 0)
    near_share = NL // row_count
    green = lax.dynamic_slice_in_dim(green_function, row_index * near_share, near_share, 0)
    screened, panel_t, dressed = screen(
        polarization,
        metric,
        three_panel,
        three_near,
        expand_mask(panel_mask, RB, AB).astype(jnp.float32),
        expand_mask(near_mask, RB, AB).astype(jnp.float32),
        green,
    )
    contracted, energy = contract(screened, panel_t, dressed)
    contracted = contracted.T.reshape(near_cols, TILE, near_share)
    self_energy = lax.dynamic_slice_in_dim(energy, col_index * 4, 4, 1)
    return (screened, contracted, self_energy)


def solution(mesh):
    placed = (
        P("row", "col"),
        P("row", "col"),
        P("row", None, None),
        P("col", None, None),
        P(),
        P(),
        P(),
    )
    return jax.shard_map(
        per_device,
        mesh=mesh,
        in_specs=placed,
        out_specs=(P("row", "col"), P("col", None, "row"), P("row", "col")),
        check_vma=False,
    )
```

```python
import functools

import jax
import jax.numpy as jnp
from jax import lax
from jax.experimental import pallas as pl
from jax.experimental.pallas import tpu as pltpu
from jax.sharding import PartitionSpec as P

TILE = 64
NL = 256
RB = 64
AB = 32
MESH = pl.DeviceIdType.MESH


def expand_mask(mask, rows, cols):
    return jnp.repeat(jnp.repeat(mask, rows, axis=0), cols, axis=1)


def place():
    row, col = lax.axis_index("row"), lax.axis_index("col")
    return row // 2, row % 2, col // 4, (col // 2) % 2, col % 2


def device(y, xh, z, xl, core):
    return (y * 2 + xh, (z * 2 + xl) * 2 + core)


class Copies:
    def __init__(self, send_sem):
        self.send_sem, self.started = send_sem, []

    def send(self, src, dst, recv_sem, target):
        index = len(self.started)
        copy = pltpu.make_async_remote_copy(
            src_ref=src,
            dst_ref=dst,
            send_sem=self.send_sem.at[index],
            recv_sem=recv_sem,
            device_id=target,
            device_id_type=MESH,
        )
        copy.start()
        self.started.append((copy, None))

    def send_or_keep(self, keep, src, dst, recv_sem, target):
        index = len(self.started)
        copy = pltpu.make_async_remote_copy(
            src_ref=src,
            dst_ref=dst,
            send_sem=self.send_sem.at[index],
            recv_sem=recv_sem,
            device_id=target,
            device_id_type=MESH,
        )

        @pl.when(jnp.logical_not(keep))
        def _():
            copy.start()

        @pl.when(keep)
        def _():
            pltpu.make_async_copy(src, dst, recv_sem).start()

        self.started.append((copy, keep))

    def finish(self):
        for copy, keep in self.started:
            if keep is None:
                copy.wait_send()
            else:
                pl.when(jnp.logical_not(keep))(copy.wait_send)


def landed(ref, sem):
    pltpu.make_async_copy(ref, ref, sem).wait()


def prepare(panel, near, panel_mask, near_mask, green, panel_t, dressed, taken, flat, made, made_near, sem):
    start = lambda k, size: pl.ds(pl.multiple_of(k * size, size), size)

    def steps(source, mask, count, make, put, first, last):
        def fetch(i):
            block = source.at[start(i // 4, 128), start(i % 4, 16)]
            return pltpu.make_async_copy(block, taken.at[i % 2], sem.at[i % 2])

        fetch(first).start()

        def body(i, carry):
            @pl.when(i + 1 < last)
            def _():
                fetch(i + 1).start()

            fetch(i).wait()

            @pl.when(i >= first + 2)
            def _():
                put(i - 2).wait()

            for h in range(2):
                lanes = slice(h * 128, (h + 1) * 128)
                flat[h] = taken[i % 2, :, :, lanes].astype(jnp.float32).reshape(128 * 16, 128)
            rows = start(i // 4, 128)
            for m in range(16):
                make(
                    i,
                    m,
                    [
                        flat[h, pl.ds(m, 128, stride=16), :] * mask[rows, h * 128 : (h + 1) * 128]
                        for h in range(2)
                    ],
                )
            put(i).start()
            return carry

        lax.fori_loop(first, last, body, 0)
        put(last - 2).wait()
        put(last - 1).wait()

    def put_panel(i):
        place_at = panel_t.at[:, start(i % 4, 512), start(i // 4, 128)]
        return pltpu.make_async_copy(made.at[i % 2], place_at, sem.at[2 + i % 2])

    def put_near(i):
        place_at = dressed.at[start(i % 4, 512), start(i // 4, 128)]
        return pltpu.make_async_copy(made_near.at[i % 2], place_at, sem.at[2 + i % 2])

    def make_panel(i, m, halves):
        turned = jnp.concatenate([half.T.astype(jnp.bfloat16) for half in halves], 0)
        made[i % 2, :, m * 32 : (m + 1) * 32, :] = turned.reshape(8, 32, 128)

    def make_near(i, m, halves):
        block = jnp.concatenate([half.astype(jnp.bfloat16) for half in halves], 1)
        product = lax.dot_general(
            green[...], block, (((1,), (1,)), ((), ())), preferred_element_type=jnp.float32
        )
        made_near[i % 2, m * 32 : (m + 1) * 32, :] = product.astype(jnp.bfloat16)

    return (
        functools.partial(steps, panel, panel_mask, 16, make_panel, put_panel),
        functools.partial(steps, near, near_mask, 8, make_near, put_near),
    )


def screen_kernel(
    a_ref,
    b_ref,
    panel,
    near,
    panel_mask,
    near_mask,
    green,
    out_ref,
    panel_t,
    dressed,
    a0,
    a1,
    b0,
    b1,
    a1_own,
    total,
    give,
    take,
    taken,
    flat,
    made,
    made_near,
    send_sem,
    own_sem,
    local_sem,
    x_sem,
    near_sem,
    far_sem,
    twin_sem,
    last_sem,
    step_sem,
):
    panel_steps, near_steps = prepare(
        panel, near, panel_mask, near_mask, green, panel_t, dressed, taken, flat, made, made_near, step_sem
    )
    y, xh, z, xl, core = place()
    twin = device(y, xh, z, xl, 1 - core)
    x = xh * 2 + xl
    rows, depth = a_ref.shape
    half, piece = rows // 2, rows // 4
    z_at = [lax.rem(z + d, 4) for d in range(4)]
    y_at = [lax.rem(y + d, 4) for d in range(4)]

    barrier = pltpu.get_barrier_semaphore()
    partners = [twin]
    partners += [device(y, xh, z_at[d], xl, core) for d in (1, 3)]
    partners += [device(y_at[d], xh, z, xl, core) for d in (1, 3)]
    for d in (1, 2, 3):
        other = lax.rem(x + d, 4)
        partners.append(device(y, other // 2, z, other % 2, core))
    for partner in partners:
        pl.semaphore_signal(barrier, inc=1, device_id=partner, device_id_type=MESH)
    pl.semaphore_wait(barrier, len(partners))

    copies = Copies(send_sem)

    own0, own1 = pl.ds(0, half), pl.ds(half, half)

    @pl.when(core == 0)
    def _():
        pltpu.make_async_copy(a_ref, a0.at[z], local_sem.at[0]).start()
        copy = pltpu.make_async_remote_copy(
            a_ref, a0.at[z], own_sem, local_sem.at[0], device_id=twin, device_id_type=MESH
        )
        copy.start()

    @pl.when(core == 1)
    def _():
        pltpu.make_async_copy(a_ref.at[own1], a1_own, local_sem.at[1]).start()
        copy = pltpu.make_async_remote_copy(
            a_ref.at[own0], a1_own, own_sem, local_sem.at[1], device_id=twin, device_id_type=MESH
        )
        copy.start()

    deep = (depth // 256 * 128 + 128, depth // 256 * 128)

    def b_slot(stream, k, p, part=None):
        buffer = b1.at[k] if stream == 0 else b0.at[k, stream - 1]
        start, count = p * deep[0], deep[p]
        if part is not None:
            start, count = start + part * (count // 2), count // 2
        return buffer.at[pl.ds(start, count)]

    def a_rows(stream, k, start, count):
        buffer = a0.at[k] if stream == 0 else a1.at[k, stream - 1]
        return buffer.at[pl.ds(start, count)]

    def a_slot(stream, k, p, part=None, of=core):
        start, count = of * half + p * piece, piece
        if part is not None:
            start, count = start + part * (count // 2), count // 2
        return a_rows(stream, k, pl.multiple_of(start, piece // 2), count)

    b_up = [device(y_at[1], xh, z, xl, core), device(y_at[3], xh, z, xl, core)]
    a_up = [device(y, xh, z_at[1], xl, core), device(y, xh, z_at[3], xl, core)]
    A, B = (a_slot, 0, z_at, a_up), (b_slot, 3, y_at, b_up)

    def b_own(p, base=0):
        return b_ref.at[pl.ds(base + p * deep[0], deep[p])]

    def b_along_x(p):
        for j in range(2):
            keep = jnp.logical_and(j == xh, xh == xl)
            at = b0.at[y, xl, pl.ds(p * deep[0], deep[p])]
            copies.send_or_keep(keep, b_own(p), at, x_sem.at[1, xl, p], device(y, j, z, xh, core))

    def a_along_x(p):
        for j in range(2):
            keep = jnp.logical_and(j == xl, xh == xl)
            at = a1.at[z, xh, pl.ds(pl.multiple_of(core * half + p * piece, piece), piece)]
            source = a1_own.at[pl.ds(p * piece, piece)]
            copies.send_or_keep(keep, source, at, x_sem.at[0, xh, p], device(y, xl, z, j, core))

    def spread(array, stream, p, source=None):
        slot, base, at, to = array
        for side in range(2):
            here = slot(stream, at[0], p)
            copies.send(here if source is None else source, here, near_sem.at[base + stream, side, p], to[side])

    def to_twin(stream, k, p, index):
        here = a_slot(stream, k, p)
        copies.send(here, here, twin_sem.at[stream, index, p], twin)

    def go_on(array, stream, p):
        slot, base, at, to = array
        for side in range(2):
            k = at[3 - 2 * side]
            landed(slot(stream, k, p), near_sem.at[base + stream, side, p])
            half_of = slot(stream, k, p, side)
            copies.send(half_of, half_of, far_sem.at[base + stream, side, p], to[side])
        if base == 0:
            for side in range(2):
                to_twin(stream, at[3 - 2 * side], p, 3 - 2 * side)

    def far(array, stream, p):
        slot, base, at, to = array
        for side in range(2):
            landed(slot(stream, at[2], p, side), far_sem.at[base + stream, side, p])
        if base == 0:
            to_twin(stream, at[2], p, 2)

    def from_twin(stream, p, indices):
        for d in indices:
            landed(a_slot(stream, z_at[d], p, of=1 - core), twin_sem.at[stream, d, p])

    def arrive(p):
        for s in (1, 2):
            landed(a_slot(s, z, p), x_sem.at[0, s - 1, p])
            spread(A, s, p)
            to_twin(s, z, p, 0)
            landed(b_slot(s, y, p), x_sem.at[1, s - 1, p])
            spread(B, s, p)

    def keep_rows(k, p, j):
        lanes = slice(p * deep[0], p * deep[0] + deep[p])

        def body(t, carry):
            at = pl.ds(pl.multiple_of(t * half, half), half)
            total[0, j, at] += jnp.dot(
                a0[k, at, lanes], b0[k, j, lanes], preferred_element_type=jnp.float32
            )
            return carry

        lax.fori_loop(0, 2, body, 0)

    def keep_cols(k, p, j):
        def body(t, carry):
            at = pl.ds(pl.multiple_of(t * half + p * piece, piece), piece)
            total[1, j, at] += jnp.dot(a1[k, j, at], b1[k], preferred_element_type=jnp.float32)
            return carry

        lax.fori_loop(0, 2, body, 0)

    def multiply(p, distances):
        def body(j, carry):
            for d in distances:
                keep_rows(y_at[d], p, j)
                keep_cols(z_at[d], p, j)
            return carry

        lax.fori_loop(0, 2, body, 0)

    b_along_x(0)
    b_local = pltpu.make_async_copy(b_ref.at[pl.ds(depth, depth)], b1.at[y], local_sem.at[2])
    b_local.start()
    for p in range(2):
        spread(B, 0, p, b_own(p, depth))
    landed(a1_own, local_sem.at[1])
    a_along_x(0)
    b_along_x(1)
    a_along_x(1)
    landed(a0.at[z], local_sem.at[0])
    for p in range(2):
        spread(A, 0, p)
    total[...] = jnp.zeros_like(total)

    panel_steps(0, 4)
    go_on(B, 0, 0)
    go_on(A, 0, 0)
    panel_steps(4, 9)
    go_on(B, 0, 1)
    go_on(A, 0, 1)
    panel_steps(9, 12)
    arrive(0)
    panel_steps(12, 16)
    for p in range(2):
        far(B, 0, p)
        far(A, 0, p)
    near_steps(0, 4)
    go_on(A, 1, 0)
    go_on(B, 1, 0)
    near_steps(4, 8)
    b_local.wait()
    go_on(A, 2, 0)
    go_on(B, 2, 0)
    arrive(1)
    for p in range(2):
        from_twin(0, p, (1, 2, 3))
    for s in (1, 2):
        from_twin(s, 0, (0, 1, 3))
    multiply(0, (0, 1))
    for s in (1, 2):
        far(A, s, 0)
        far(B, s, 0)
    multiply(0, (3,))
    go_on(A, 1, 1)
    go_on(B, 1, 1)
    for s in (1, 2):
        from_twin(s, 0, (2,))
        from_twin(s, 1, (0,))
    multiply(0, (2,))
    go_on(A, 2, 1)
    go_on(B, 2, 1)
    multiply(1, (0,))
    for s in (1, 2):
        from_twin(s, 1, (1, 3))
    multiply(1, (1, 3))
    for s in (1, 2):
        far(A, s, 1)
        far(B, s, 1)
    for s in (1, 2):
        from_twin(s, 1, (2,))

    keep_rows(y_at[2], 1, 1 - xl)
    give[0] = total[0, 1 - xl].astype(jnp.bfloat16)
    copies.send(give.at[0], take.at[0], last_sem.at[0], device(y, xh, z, 1 - xl, core))
    keep_cols(z_at[2], 1, 1 - xh)
    give[1] = total[1, 1 - xh].astype(jnp.bfloat16)
    copies.send(give.at[1], take.at[1], last_sem.at[1], device(y, 1 - xh, z, xl, core))
    keep_rows(y_at[2], 1, xl)
    keep_cols(z_at[2], 1, xh)
    landed(take.at[0], last_sem.at[0])
    landed(take.at[1], last_sem.at[1])
    out_ref[...] = (
        total[0, xl] + total[1, xh] + take[0].astype(jnp.float32) + take[1].astype(jnp.float32)
    ).astype(jnp.bfloat16)

    copies.finish()

    @pl.when(core == 0)
    def _():
        pltpu.make_async_copy(a_ref, a0.at[z], own_sem).wait()

    @pl.when(core == 1)
    def _():
        pltpu.make_async_copy(a_ref.at[own0], a1_own, own_sem).wait()


def screen(a, b, panel, near, panel_mask, near_mask, green):
    rows, depth = a.shape
    cols = b.shape[1]
    bf16 = jnp.bfloat16
    dma = pltpu.SemaphoreType.DMA
    hbm, vmem = pl.BlockSpec(memory_space=pl.ANY), pl.BlockSpec(memory_space=pltpu.VMEM)
    return pl.pallas_call(
        screen_kernel,
        out_shape=(
            jax.ShapeDtypeStruct((rows, cols), bf16),
            jax.ShapeDtypeStruct((8, TILE * 32, rows), bf16),
            jax.ShapeDtypeStruct((TILE * 32, cols), bf16),
        ),
        in_specs=[hbm] * 4 + [vmem] * 3,
        out_specs=(vmem, hbm, hbm),
        scratch_shapes=[
            pltpu.VMEM((4, rows, depth), bf16),
            pltpu.VMEM((4, 2, rows, depth), bf16),
            pltpu.VMEM((4, 2, depth, cols), bf16),
            pltpu.VMEM((4, depth, cols), bf16),
            pltpu.VMEM((rows // 2, depth), bf16),
            pltpu.VMEM((2, 2, rows, cols), jnp.float32),
            pltpu.VMEM((2, rows, cols), bf16),
            pltpu.VMEM((2, rows, cols), bf16),
            pltpu.VMEM((2, 128, 16, NL), bf16),
            pltpu.VMEM((2, 128 * 16, 128), jnp.float32),
            pltpu.VMEM((2, 8, 16 * 32, 128), bf16),
            pltpu.VMEM((2, 16 * 32, 128), bf16),
            dma((88,)),
            dma,
            dma((3,)),
            dma((2, 2, 2)),
            dma((6, 2, 2)),
            dma((6, 2, 2)),
            dma((3, 4, 2)),
            dma((2,)),
            dma((4,)),
        ],
        compiler_params=pltpu.CompilerParams(
            collective_id=0, has_side_effects=True, vmem_limit_bytes=56 * 2**20
        ),
        name="screen",
    )(a, b, panel, near, panel_mask, near_mask, green)


LATE = 1152


def contract_kernel(
    s_ref,
    panel_t,
    dressed,
    out_ref,
    energy_ref,
    block,
    part,
    far_y,
    near_y,
    cross_y,
    cross_x,
    far_x,
    near_x,
    total,
    other,
    dressed_b,
    tile,
    row_sum,
    tile_row,
    tile_col,
    send_sem,
    block_sem,
    far_sem,
    near_sem,
    cross_sem,
    row_sem,
    col_sem,
):
    y, xh, z, xl, core = place()
    col = (z * 2 + xl) * 2 + core
    f32, bf16 = jnp.float32, jnp.bfloat16

    def in_row(d, j):
        return device(lax.rem(y + d, 4), lax.rem(xh + j, 2), z, xl, core)

    def in_col(d):
        return (y * 2 + xh, lax.rem(col + d, 16))

    partners = [in_row(s // 2, s % 2) for s in range(1, 8)] + [in_col(d) for d in range(1, 16)]
    barrier = pltpu.get_barrier_semaphore()
    for partner in partners:
        pl.semaphore_signal(barrier, inc=1, device_id=partner, device_id_type=MESH)

    order = [(2, 1), (2, 0), (1, 1), (3, 1), (1, 0), (3, 0), (0, 1), (0, 0)]

    def fetch(i):
        d, j = order[i]
        share = lax.rem(y + d, 4) * 2 + lax.rem(xh + j, 2)
        return pltpu.make_async_copy(panel_t.at[share], block.at[i % 2], block_sem.at[i % 2])

    fetch(0).start()
    dressed_copy = pltpu.make_async_copy(dressed, dressed_b, block_sem.at[2])
    dressed_copy.start()
    pl.semaphore_wait(barrier, len(partners))

    copies = Copies(send_sem)
    rows = TILE * 32
    early = rows - LATE
    h_late, h_early = LATE // 2, early // 2
    up, down, across = in_row(1, 0), in_row(3, 0), in_row(0, 1)

    def late(d, j, start=0, count=LATE):
        return part.at[d * 2 + j, pl.ds(start, count)]

    def first(d, j, start=0, count=early):
        return part.at[d * 2 + j, pl.ds(LATE + start, count)]

    for i, (d, j) in enumerate(order):
        if i + 1 < 8:
            fetch(i + 1).start()
        fetch(i).wait()

        def multiply(t, carry):
            at = pl.ds(pl.multiple_of(t * 256, 256), 256)
            part[d * 2 + j, at] = jnp.dot(
                block[i % 2, at], s_ref[...], preferred_element_type=f32
            ).astype(bf16)
            return carry

        lax.fori_loop(0, rows // 256, multiply, 0)
        if j == 1:
            copies.send(first(d, 1), cross_x.at[d], cross_sem.at[d], across)
        if d == 2:
            copies.send(late(2, j, 0, h_late), far_y.at[j, 0], far_sem.at[j, 0], up)
            copies.send(late(2, j, h_late, h_late), far_y.at[j, 1], far_sem.at[j, 1], down)
        if d == 1:
            copies.send(late(1, j, h_late, h_late), near_y.at[j, 0, pl.ds(h_late, h_late)], near_sem.at[j, 0, 0], up)
        if d == 3:
            copies.send(late(3, j, 0, h_late), near_y.at[j, 1, pl.ds(0, h_late)], near_sem.at[j, 1, 0], down)

    def add(ref, *others):
        result = ref[...].astype(f32)
        for each in others:
            result = result + each[...].astype(f32)
        ref[...] = result.astype(bf16)

    for j in (1, 0):
        landed(far_y.at[j, 0], far_sem.at[j, 0])
        add(late(1, j, 0, h_late), far_y.at[j, 0])
        copies.send(late(1, j, 0, h_late), near_y.at[j, 0, pl.ds(0, h_late)], near_sem.at[j, 0, 1], up)
        landed(far_y.at[j, 1], far_sem.at[j, 1])
        add(late(3, j, h_late, h_late), far_y.at[j, 1])
        copies.send(late(3, j, h_late, h_late), near_y.at[j, 1, pl.ds(h_late, h_late)], near_sem.at[j, 1, 1], down)

    landed(cross_x.at[2], cross_sem.at[2])
    add(first(2, 0), cross_x.at[2])
    copies.send(first(2, 0, 0, h_early), far_x.at[0], far_sem.at[2, 0], up)
    copies.send(first(2, 0, h_early, h_early), far_x.at[1], far_sem.at[2, 1], down)
    landed(cross_x.at[1], cross_sem.at[1])
    add(first(1, 0), cross_x.at[1])
    copies.send(first(1, 0, h_early, h_early), near_x.at[0, pl.ds(h_early, h_early)], near_sem.at[2, 0, 0], up)
    landed(cross_x.at[3], cross_sem.at[3])
    add(first(3, 0), cross_x.at[3])
    copies.send(first(3, 0, 0, h_early), near_x.at[1, pl.ds(0, h_early)], near_sem.at[2, 1, 0], down)

    def both_near(j, ref):
        count = ref.shape[1] // 2
        for side in range(2):
            for turn in range(2):
                start = count if (side == 0) == (turn == 0) else 0
                landed(ref.at[side, pl.ds(start, count)], near_sem.at[j, side, turn])

    both_near(1, near_y.at[1])
    add(late(0, 1), near_y.at[1, 0], near_y.at[1, 1])
    copies.send(late(0, 1), cross_y, cross_sem.at[4], across)

    landed(far_x.at[0], far_sem.at[2, 0])
    add(first(1, 0, 0, h_early), far_x.at[0])
    copies.send(first(1, 0, 0, h_early), near_x.at[0, pl.ds(0, h_early)], near_sem.at[2, 0, 1], up)
    landed(far_x.at[1], far_sem.at[2, 1])
    add(first(3, 0, h_early, h_early), far_x.at[1])
    copies.send(first(3, 0, h_early, h_early), near_x.at[1, pl.ds(h_early, h_early)], near_sem.at[2, 1, 1], down)

    dressed_copy.wait()
    for h in range(2):
        other[h] = dressed_b[:, h * 128 : (h + 1) * 128].astype(f32)

    def settle(at, *terms):
        result = terms[0][...].astype(f32)
        for each in terms[1:]:
            result = result + each[...].astype(f32)
        result = result.astype(bf16)
        out_ref[at] = result
        for h in range(2):
            total[h, at] = result[:, h * 128 : (h + 1) * 128].astype(f32)

    both_near(0, near_y.at[0])
    landed(cross_x.at[0], cross_sem.at[0])
    landed(cross_y, cross_sem.at[4])
    settle(pl.ds(0, LATE), late(0, 0), near_y.at[0, 0], near_y.at[0, 1], cross_y)
    both_near(2, near_x)
    settle(pl.ds(LATE, early), first(0, 0), cross_x.at[0], near_x.at[0], near_x.at[1])

    def column(ref, l):
        halves = [ref[h, pl.ds(l, TILE, stride=32), :].astype(bf16) for h in range(2)]
        return jnp.concatenate(halves, 1)

    energy = jnp.zeros((TILE, TILE), f32)
    for l in range(32):
        energy = energy + lax.dot_general(
            column(total, l), column(other, l), (((1,), (1,)), ((), ())), preferred_element_type=f32
        )
    tile[...] = jnp.concatenate([-energy, jnp.zeros_like(energy)], 1)

    def share_of(row):
        return pl.ds(pl.multiple_of(row * 8, 8), 8)

    for s in range(1, 8):
        target = in_row(s // 2, s % 2)
        copies.send(tile.at[share_of(target[0])], tile_row.at[s], row_sem.at[s], target)
    mine = tile[share_of(y * 2 + xh)]
    for s in range(1, 8):
        landed(tile_row.at[s], row_sem.at[s])
        mine = mine + tile_row[s]
    row_sum[...] = mine
    for d in range(1, 16):
        copies.send(row_sum, tile_col.at[d], col_sem.at[d], in_col(d))
    for d in range(1, 16):
        landed(tile_col.at[d], col_sem.at[d])
        mine = mine + tile_col[d]
    energy_ref[...] = mine
    copies.finish()


def contract(screened, panel_t, dressed):
    rows = TILE * 32
    cols = screened.shape[1]
    early = rows - LATE
    bf16, f32 = jnp.bfloat16, jnp.float32
    dma = pltpu.SemaphoreType.DMA
    hbm, vmem = pl.BlockSpec(memory_space=pl.ANY), pl.BlockSpec(memory_space=pltpu.VMEM)
    return pl.pallas_call(
        contract_kernel,
        out_shape=(jax.ShapeDtypeStruct((rows, cols), bf16), jax.ShapeDtypeStruct((8, 128), f32)),
        in_specs=[vmem, hbm, hbm],
        out_specs=(vmem, vmem),
        scratch_shapes=[
            pltpu.VMEM((2, rows, screened.shape[0]), bf16),
            pltpu.VMEM((8, rows, cols), bf16),
            pltpu.VMEM((2, 2, LATE // 2, cols), bf16),
            pltpu.VMEM((2, 2, LATE, cols), bf16),
            pltpu.VMEM((LATE, cols), bf16),
            pltpu.VMEM((4, early, cols), bf16),
            pltpu.VMEM((2, early // 2, cols), bf16),
            pltpu.VMEM((2, early, cols), bf16),
            pltpu.VMEM((2, rows, 128), f32),
            pltpu.VMEM((2, rows, 128), f32),
            pltpu.VMEM((rows, cols), bf16),
            pltpu.VMEM((TILE, 128), f32),
            pltpu.VMEM((8, 128), f32),
            pltpu.VMEM((8, 8, 128), f32),
            pltpu.VMEM((16, 8, 128), f32),
            dma((48,)),
            dma((3,)),
            dma((3, 2)),
            dma((3, 2, 2)),
            dma((5,)),
            dma((8,)),
            dma((16,)),
        ],
        compiler_params=pltpu.CompilerParams(
            collective_id=1, has_side_effects=True, vmem_limit_bytes=56 * 2**20
        ),
        name="contract",
    )(screened, panel_t, dressed)


def per_device(
    polarization, metric, three_panel, three_near, green_function, mask_panel, mask_near
):
    row_index = lax.axis_index("row")
    col_index = lax.axis_index("col")
    row_count = lax.axis_size("row")
    panel_rows = polarization.shape[0]
    near_cols = metric.shape[1]
    panel_blocks = panel_rows // RB
    panel_mask = lax.dynamic_slice_in_dim(mask_panel, row_index * panel_blocks, panel_blocks, 0)
    near_blocks = near_cols // RB
    near_mask = lax.dynamic_slice_in_dim(mask_near, col_index * near_blocks, near_blocks, 0)
    near_share = NL // row_count
    green = lax.dynamic_slice_in_dim(green_function, row_index * near_share, near_share, 0)
    screened, panel_t, dressed = screen(
        polarization,
        metric,
        three_panel,
        three_near,
        expand_mask(panel_mask, RB, AB).astype(jnp.float32),
        expand_mask(near_mask, RB, AB).astype(jnp.float32),
        green,
    )
    contracted, energy = contract(screened, panel_t, dressed)
    contracted = contracted.T.reshape(near_cols, TILE, near_share)
    self_energy = lax.dynamic_slice_in_dim(energy, col_index * 4, 4, 1)
    return (screened, contracted, self_energy)


def solution(mesh):
    placed = (
        P("row", "col"),
        P("row", "col"),
        P("row", None, None),
        P("col", None, None),
        P(),
        P(),
        P(),
    )
    return jax.shard_map(
        per_device,
        mesh=mesh,
        in_specs=placed,
        out_specs=(P("row", "col"), P("col", None, "row"), P("row", "col")),
        check_vma=False,
    )
```

```python
import functools

import jax
import jax.numpy as jnp
from jax import lax
from jax.experimental import pallas as pl
from jax.experimental.pallas import tpu as pltpu
from jax.sharding import PartitionSpec as P

TILE = 64
NL = 256
RB = 64
AB = 32
MESH = pl.DeviceIdType.MESH


def place():
    row, col = lax.axis_index("row"), lax.axis_index("col")
    return row // 2, row % 2, col // 4, (col // 2) % 2, col % 2


def device(y, xh, z, xl, core):
    return (y * 2 + xh, (z * 2 + xl) * 2 + core)


class Copies:
    def __init__(self, send_sem):
        self.send_sem, self.started = send_sem, []

    def send(self, src, dst, recv_sem, target):
        index = len(self.started)
        copy = pltpu.make_async_remote_copy(
            src_ref=src,
            dst_ref=dst,
            send_sem=self.send_sem.at[index],
            recv_sem=recv_sem,
            device_id=target,
            device_id_type=MESH,
        )
        copy.start()
        self.started.append((copy, None))

    def send_if(self, wanted, src, dst, recv_sem, target):
        index = len(self.started)
        copy = pltpu.make_async_remote_copy(
            src_ref=src,
            dst_ref=dst,
            send_sem=self.send_sem.at[index],
            recv_sem=recv_sem,
            device_id=target,
            device_id_type=MESH,
        )
        pl.when(wanted)(copy.start)
        self.started.append((copy, wanted))

    def finish(self):
        for copy, wanted in self.started:
            if wanted is None:
                copy.wait_send()
            else:
                pl.when(wanted)(copy.wait_send)


def landed(ref, sem):
    pltpu.make_async_copy(ref, ref, sem).wait()


def prepare(panel, near, panel_mask, near_mask, green, panel_t, dressed, taken, flat, made, made_near, sem):
    start = lambda k, size: pl.ds(pl.multiple_of(k * size, size), size)

    def steps(source, mask, count, make, put, first, last):
        def fetch(i):
            block = source.at[start(i // 4, 128), start(i % 4, 16)]
            return pltpu.make_async_copy(block, taken.at[i % 2], sem.at[i % 2])

        fetch(first).start()

        def body(i, carry):
            @pl.when(i + 1 < last)
            def _():
                fetch(i + 1).start()

            fetch(i).wait()

            @pl.when(i >= first + 2)
            def _():
                put(i - 2).wait()

            for h in range(2):
                lanes = slice(h * 128, (h + 1) * 128)
                flat[h] = taken[i % 2, :, :, lanes].astype(jnp.float32).reshape(128 * 16, 128)
            rows = start(i // 4, 128)
            for m in range(16):
                make(
                    i,
                    m,
                    [
                        flat[h, pl.ds(m, 128, stride=16), :] * mask[rows, h * 128 : (h + 1) * 128]
                        for h in range(2)
                    ],
                )
            put(i).start()
            return carry

        lax.fori_loop(first, last, body, 0)
        put(last - 2).wait()
        put(last - 1).wait()

    def put_panel(i):
        place_at = panel_t.at[:, start(i % 4, 512), start(i // 4, 128)]
        return pltpu.make_async_copy(made.at[i % 2], place_at, sem.at[2 + i % 2])

    def put_near(i):
        place_at = dressed.at[start(i % 4, 512), start(i // 4, 128)]
        return pltpu.make_async_copy(made_near.at[i % 2], place_at, sem.at[2 + i % 2])

    def make_panel(i, m, halves):
        turned = jnp.concatenate([half.T.astype(jnp.bfloat16) for half in halves], 0)
        made[i % 2, :, m * 32 : (m + 1) * 32, :] = turned.reshape(8, 32, 128)

    def make_near(i, m, halves):
        block = jnp.concatenate([half.astype(jnp.bfloat16) for half in halves], 1)
        product = lax.dot_general(
            green[...], block, (((1,), (1,)), ((), ())), preferred_element_type=jnp.float32
        )
        made_near[i % 2, m * 32 : (m + 1) * 32, :] = product.astype(jnp.bfloat16)

    return (
        functools.partial(steps, panel, panel_mask, 16, make_panel, put_panel),
        functools.partial(steps, near, near_mask, 8, make_near, put_near),
    )


def screen_kernel(
    a_ref,
    b_ref,
    panel,
    near,
    panel_mask_ref,
    near_mask_ref,
    green_ref,
    out_ref,
    panel_t,
    dressed,
    a0,
    a1,
    b0,
    b1,
    a1_own,
    total,
    give,
    take,
    taken,
    flat,
    made,
    made_near,
    panel_blocks,
    near_blocks,
    panel_mask,
    near_mask,
    green,
    send_sem,
    own_sem,
    local_sem,
    x_sem,
    near_sem,
    far_sem,
    twin_sem,
    last_sem,
    step_sem,
    small_sem,
):
    row, col = lax.axis_index("row"), lax.axis_index("col")
    small = [
        pltpu.make_async_copy(panel_mask_ref, panel_blocks, small_sem.at[0]),
        pltpu.make_async_copy(near_mask_ref, near_blocks, small_sem.at[1]),
        pltpu.make_async_copy(
            green_ref.at[pl.ds(pl.multiple_of(row * 32, 32), 32)], green, small_sem.at[2]
        ),
    ]
    for copy in small:
        copy.start()

    def finish_masks():
        for copy in small:
            copy.wait()
        for blocks, mask, begin in (
            (panel_blocks, panel_mask, row * (panel_mask.shape[0] // RB)),
            (near_blocks, near_mask, col * (near_mask.shape[0] // RB)),
        ):
            count = mask.shape[0]
            shape = (count, blocks.shape[0])
            at = lax.broadcasted_iota(jnp.int32, shape, 0) // RB + begin
            pick = (at == lax.broadcasted_iota(jnp.int32, shape, 1)).astype(jnp.float32)
            shape = (blocks.shape[1], NL)
            wide = lax.broadcasted_iota(jnp.int32, shape, 1) // AB == lax.broadcasted_iota(jnp.int32, shape, 0)
            picked = jnp.dot(pick, blocks[...].astype(jnp.float32), preferred_element_type=jnp.float32)
            mask[...] = jnp.dot(picked, wide.astype(jnp.float32), preferred_element_type=jnp.float32)

    panel_steps, near_steps = prepare(
        panel, near, panel_mask, near_mask, green, panel_t, dressed, taken, flat, made, made_near, step_sem
    )
    y, xh, z, xl, core = place()
    twin = device(y, xh, z, xl, 1 - core)
    x = xh * 2 + xl
    rows, depth = a_ref.shape
    half, piece = rows // 2, rows // 4
    z_at = [lax.rem(z + d, 4) for d in range(4)]
    y_at = [lax.rem(y + d, 4) for d in range(4)]

    barrier = pltpu.get_barrier_semaphore()
    partners = [twin]
    partners += [device(y, xh, z_at[d], xl, core) for d in (1, 3)]
    partners += [device(y_at[d], xh, z, xl, core) for d in (1, 3)]
    for d in (1, 2, 3):
        other = lax.rem(x + d, 4)
        partners.append(device(y, other // 2, z, other % 2, core))
    for partner in partners:
        pl.semaphore_signal(barrier, inc=1, device_id=partner, device_id_type=MESH)
    pl.semaphore_wait(barrier, len(partners))

    copies = Copies(send_sem)

    own0, own1 = pl.ds(0, half), pl.ds(half, half)

    @pl.when(core == 0)
    def _():
        pltpu.make_async_copy(a_ref, a0.at[z], local_sem.at[0]).start()
        copy = pltpu.make_async_remote_copy(
            a_ref, a0.at[z], own_sem, local_sem.at[0], device_id=twin, device_id_type=MESH
        )
        copy.start()

    @pl.when(core == 1)
    def _():
        pltpu.make_async_copy(a_ref.at[own1], a1_own, local_sem.at[1]).start()
        copy = pltpu.make_async_remote_copy(
            a_ref.at[own0], a1_own, own_sem, local_sem.at[1], device_id=twin, device_id_type=MESH
        )
        copy.start()

    deep = (depth // 256 * 128 + 128, depth // 256 * 128)

    def b_slot(stream, k, p, part=None):
        buffer = b1.at[k] if stream == 0 else b0.at[k, stream - 1]
        start, count = p * deep[0], deep[p]
        if part is not None:
            start, count = start + part * (count // 2), count // 2
        return buffer.at[pl.ds(start, count)]

    def a_rows(stream, k, start, count):
        buffer = a0.at[k] if stream == 0 else a1.at[k, stream - 1]
        return buffer.at[pl.ds(start, count)]

    def a_slot(stream, k, p, part=None, of=core):
        start, count = of * half + p * piece, piece
        if part is not None:
            start, count = start + part * (count // 2), count // 2
        return a_rows(stream, k, pl.multiple_of(start, piece // 2), count)

    b_up = [device(y_at[1], xh, z, xl, core), device(y_at[3], xh, z, xl, core)]
    a_up = [device(y, xh, z_at[1], xl, core), device(y, xh, z_at[3], xl, core)]
    A, B = (a_slot, 0, z_at, a_up), (b_slot, 3, y_at, b_up)

    def b_own(p, base=0):
        return b_ref.at[pl.ds(base + p * deep[0], deep[p])]

    inner = xh != xl

    def b_along_x(p):
        def at(role):
            return b0.at[y, role, pl.ds(p * deep[0], deep[p])]

        for j in range(2):
            copies.send_if(inner, b_own(p), at(0), x_sem.at[1, 0, p], device(y, j, z, xh, core))

    def a_along_x(p):
        source = a1_own.at[pl.ds(p * piece, piece)]
        for j in range(2):
            copies.send_if(inner, source, a_slot(1, z, p), x_sem.at[0, 0, p], device(y, xl, z, j, core))

    outer = jnp.logical_not(inner)

    def a_outer_along_x(p):
        source = a1_own.at[pl.ds(p * piece, piece)]
        copies.send_if(outer, source, a_slot(2, z, p), x_sem.at[0, 1, p], device(y, xh, z, 1 - xl, core))

    def b_outer_along_x(p):
        copies.send_if(outer, b_own(p), b_slot(2, y, p), x_sem.at[1, 1, p], device(y, 1 - xh, z, xl, core))

    def outer_keep():
        for p in range(2):
            source = a1_own.at[pl.ds(p * piece, piece)]
            pltpu.make_async_copy(source, a_slot(2, z, p), x_sem.at[0, 1, p]).start()
            pltpu.make_async_copy(b_own(p), b_slot(2, y, p), x_sem.at[1, 1, p]).start()

    def spread(array, stream, p, source=None):
        slot, base, at, to = array
        for side in range(2):
            here = slot(stream, at[0], p)
            copies.send(here if source is None else source, here, near_sem.at[base + stream, side, p], to[side])

    def start_near(wanted, p, source):
        for side in range(2):
            copies.send_if(wanted, source, a_slot(0, z, p), near_sem.at[0, side, p], a_up[side])

    def to_twin(stream, k, p, index):
        here = a_slot(stream, k, p)
        copies.send(here, here, twin_sem.at[stream, index, p], twin)

    def go_on(array, stream, p):
        slot, base, at, to = array
        for side in range(2):
            k = at[3 - 2 * side]
            landed(slot(stream, k, p), near_sem.at[base + stream, side, p])
            half_of = slot(stream, k, p, side)
            copies.send(half_of, half_of, far_sem.at[base + stream, side, p], to[side])
        if base == 0:
            for side in range(2):
                to_twin(stream, at[3 - 2 * side], p, 3 - 2 * side)

    def far(array, stream, p):
        slot, base, at, to = array
        for side in range(2):
            landed(slot(stream, at[2], p, side), far_sem.at[base + stream, side, p])
        if base == 0:
            to_twin(stream, at[2], p, 2)

    def from_twin(stream, p, indices):
        for d in indices:
            landed(a_slot(stream, z_at[d], p, of=1 - core), twin_sem.at[stream, d, p])

    def arrive(s, p):
        landed(a_slot(s, z, p), x_sem.at[0, s - 1, p])
        spread(A, s, p)
        landed(b_slot(s, y, p), x_sem.at[1, s - 1, p])
        spread(B, s, p)
        to_twin(s, z, p, 0)

    def keep_rows(k, p, j):
        lanes = slice(p * deep[0], p * deep[0] + deep[p])

        def body(t, carry):
            at = pl.ds(pl.multiple_of(t * half, half), half)
            total[0, j, at] += jnp.dot(
                a0[k, at, lanes], b0[k, j, lanes], preferred_element_type=jnp.float32
            )
            return carry

        lax.fori_loop(0, 2, body, 0)

    def keep_cols(k, p, j):
        def body(t, carry):
            at = pl.ds(pl.multiple_of(t * half + p * piece, piece), piece)
            total[1, j, at] += jnp.dot(a1[k, j, at], b1[k], preferred_element_type=jnp.float32)
            return carry

        lax.fori_loop(0, 2, body, 0)

    for p in range(2):
        start_near(core == 0, p, a_ref.at[pl.ds(p * piece, piece)])
    b_along_x(0)
    for p in range(2):
        spread(B, 0, p, b_own(p, depth))
    landed(a1_own, local_sem.at[1])
    a_along_x(0)
    b_along_x(1)
    a_along_x(1)
    landed(a0.at[z], local_sem.at[0])
    for p in range(2):
        start_near(core == 1, p, a_slot(0, z, p))
    pl.when(outer)(outer_keep)
    b_local = pltpu.make_async_copy(b_ref.at[pl.ds(depth, depth)], b1.at[y], local_sem.at[2])
    b_local.start()
    total[...] = jnp.zeros_like(total)
    finish_masks()

    panel_steps(0, 4)
    go_on(B, 0, 0)
    go_on(A, 0, 0)
    panel_steps(4, 8)
    go_on(B, 0, 1)
    go_on(A, 0, 1)
    arrive(1, 0)
    for p in range(2):
        a_outer_along_x(p)
    panel_steps(8, 11)
    for p in range(2):
        far(B, 0, p)
        far(A, 0, p)
    arrive(1, 1)
    for p in range(2):
        b_outer_along_x(p)
    panel_steps(11, 14)
    go_on(A, 1, 0)
    go_on(B, 1, 0)
    panel_steps(14, 16)
    near_steps(0, 2)
    arrive(2, 0)
    go_on(A, 1, 1)
    go_on(B, 1, 1)
    near_steps(2, 4)
    for p in range(2):
        from_twin(0, p, (1, 2, 3))
    b_local.wait()

    def others(p):
        def step(d, carry):
            keep_rows(lax.rem(y + d, 4), p, 0)
            keep_cols(lax.rem(z + d, 4), p, 0)
            return carry

        lax.fori_loop(0, 4, step, 0)

    far(A, 1, 0)
    far(B, 1, 0)
    arrive(2, 1)
    near_steps(4, 8)
    from_twin(1, 0, (0, 1, 2, 3))
    others(0)
    far(A, 1, 1)
    far(B, 1, 1)
    go_on(A, 2, 0)
    go_on(B, 2, 0)
    from_twin(1, 1, (0, 1, 2, 3))
    others(1)
    for i in range(2):
        give[i] = total[i, 0].astype(jnp.bfloat16)
    copies.send(give.at[0], take.at[0], last_sem.at[0], device(y, xh, z, 1 - xl, core))
    copies.send(give.at[1], take.at[1], last_sem.at[1], device(y, 1 - xh, z, xl, core))
    from_twin(2, 0, (0, 1, 3))

    def own(p):
        def step(d):
            keep_rows(y_at[d], p, 1)
            keep_cols(z_at[d], p, 1)

        return step

    step = own(0)
    for d in (0, 1, 3):
        step(d)
    go_on(A, 2, 1)
    go_on(B, 2, 1)
    far(A, 2, 0)
    far(B, 2, 0)
    from_twin(2, 0, (2,))
    from_twin(2, 1, (0, 1, 3))
    step(2)
    step = own(1)
    for d in (0, 1, 3):
        step(d)
    far(B, 2, 1)
    keep_rows(y_at[2], 1, 1)
    far(A, 2, 1)
    landed(take.at[0], last_sem.at[0])
    landed(take.at[1], last_sem.at[1])
    total[0, 1] += total[1, 1] + take[0].astype(jnp.float32) + take[1].astype(jnp.float32)
    total[1, 1] = jnp.zeros_like(total[1, 1])
    from_twin(2, 1, (2,))
    keep_cols(z_at[2], 1, 1)
    out_ref[...] = (total[0, 1] + total[1, 1]).astype(jnp.bfloat16)

    copies.finish()

    @pl.when(core == 0)
    def _():
        pltpu.make_async_copy(a_ref, a0.at[z], own_sem).wait()

    @pl.when(core == 1)
    def _():
        pltpu.make_async_copy(a_ref.at[own0], a1_own, own_sem).wait()


def screen(a, b, panel, near, panel_mask, near_mask, green):
    rows, depth = a.shape
    cols = b.shape[1]
    bf16 = jnp.bfloat16
    dma = pltpu.SemaphoreType.DMA
    hbm, vmem = pl.BlockSpec(memory_space=pl.ANY), pl.BlockSpec(memory_space=pltpu.VMEM)
    return pl.pallas_call(
        screen_kernel,
        out_shape=(
            jax.ShapeDtypeStruct((rows, cols), bf16),
            jax.ShapeDtypeStruct((8, TILE * 32, rows), bf16),
            jax.ShapeDtypeStruct((TILE * 32, cols), bf16),
        ),
        in_specs=[hbm] * 7,
        out_specs=(vmem, hbm, hbm),
        scratch_shapes=[
            pltpu.VMEM((4, rows, depth), bf16),
            pltpu.VMEM((4, 2, rows, depth), bf16),
            pltpu.VMEM((4, 2, depth, cols), bf16),
            pltpu.VMEM((4, depth, cols), bf16),
            pltpu.VMEM((rows // 2, depth), bf16),
            pltpu.VMEM((2, 2, rows, cols), jnp.float32),
            pltpu.VMEM((2, rows, cols), bf16),
            pltpu.VMEM((2, rows, cols), bf16),
            pltpu.VMEM((2, 128, 16, NL), bf16),
            pltpu.VMEM((2, 128 * 16, 128), jnp.float32),
            pltpu.VMEM((2, 8, 16 * 32, 128), bf16),
            pltpu.VMEM((2, 16 * 32, 128), bf16),
            pltpu.VMEM(panel_mask.shape, jnp.int32),
            pltpu.VMEM(near_mask.shape, jnp.int32),
            pltpu.VMEM((rows, NL), jnp.float32),
            pltpu.VMEM((cols, NL), jnp.float32),
            pltpu.VMEM((32, NL), bf16),
            dma((96,)),
            dma,
            dma((3,)),
            dma((2, 2, 2)),
            dma((6, 2, 2)),
            dma((6, 2, 2)),
            dma((3, 4, 2)),
            dma((2,)),
            dma((4,)),
            dma((3,)),
        ],
        compiler_params=pltpu.CompilerParams(
            collective_id=0, has_side_effects=True, vmem_limit_bytes=56 * 2**20
        ),
        name="screen",
    )(a, b, panel, near, panel_mask, near_mask, green)


LATE = 1152


def contract_kernel(
    s_ref,
    panel_t,
    dressed,
    out_ref,
    energy_ref,
    block,
    part,
    far_y,
    near_y,
    cross_y,
    cross_x,
    far_x,
    near_x,
    total,
    other,
    dressed_b,
    tile,
    row_sum,
    tile_row,
    tile_col,
    send_sem,
    block_sem,
    far_sem,
    near_sem,
    cross_sem,
    row_sem,
    col_sem,
):
    y, xh, z, xl, core = place()
    col = (z * 2 + xl) * 2 + core
    f32, bf16 = jnp.float32, jnp.bfloat16

    def in_row(d, j):
        return device(lax.rem(y + d, 4), lax.rem(xh + j, 2), z, xl, core)

    def in_col(d):
        return (y * 2 + xh, lax.rem(col + d, 16))

    partners = [in_row(s // 2, s % 2) for s in range(1, 8)] + [in_col(d) for d in range(1, 16)]
    barrier = pltpu.get_barrier_semaphore()
    for partner in partners:
        pl.semaphore_signal(barrier, inc=1, device_id=partner, device_id_type=MESH)

    order = [(2, 1), (2, 0), (1, 1), (3, 1), (1, 0), (3, 0), (0, 1), (0, 0)]

    def fetch(i):
        d, j = order[i]
        share = lax.rem(y + d, 4) * 2 + lax.rem(xh + j, 2)
        return pltpu.make_async_copy(panel_t.at[share], block.at[i % 2], block_sem.at[i % 2])

    fetch(0).start()
    dressed_copy = pltpu.make_async_copy(dressed, dressed_b, block_sem.at[2])
    dressed_copy.start()
    pl.semaphore_wait(barrier, len(partners))

    copies = Copies(send_sem)
    rows = TILE * 32
    early = rows - LATE
    h_late, h_early = LATE // 2, early // 2
    up, down, across = in_row(1, 0), in_row(3, 0), in_row(0, 1)

    def late(d, j, start=0, count=LATE):
        return part.at[d * 2 + j, pl.ds(start, count)]

    def first(d, j, start=0, count=early):
        return part.at[d * 2 + j, pl.ds(LATE + start, count)]

    for i, (d, j) in enumerate(order):
        if i + 1 < 8:
            fetch(i + 1).start()
        fetch(i).wait()

        def multiply(t, carry):
            at = pl.ds(pl.multiple_of(t * 256, 256), 256)
            part[d * 2 + j, at] = jnp.dot(
                block[i % 2, at], s_ref[...], preferred_element_type=f32
            ).astype(bf16)
            return carry

        lax.fori_loop(0, rows // 256, multiply, 0)
        if j == 1:
            copies.send(first(d, 1), cross_x.at[d], cross_sem.at[d], across)
        if d == 2:
            copies.send(late(2, j, 0, h_late), far_y.at[j, 0], far_sem.at[j, 0], up)
            copies.send(late(2, j, h_late, h_late), far_y.at[j, 1], far_sem.at[j, 1], down)
        if d == 1:
            copies.send(late(1, j, h_late, h_late), near_y.at[j, 0, pl.ds(h_late, h_late)], near_sem.at[j, 0, 0], up)
        if d == 3:
            copies.send(late(3, j, 0, h_late), near_y.at[j, 1, pl.ds(0, h_late)], near_sem.at[j, 1, 0], down)

    def add(ref, *others):
        result = ref[...].astype(f32)
        for each in others:
            result = result + each[...].astype(f32)
        ref[...] = result.astype(bf16)

    for j in (1, 0):
        landed(far_y.at[j, 0], far_sem.at[j, 0])
        add(late(1, j, 0, h_late), far_y.at[j, 0])
        copies.send(late(1, j, 0, h_late), near_y.at[j, 0, pl.ds(0, h_late)], near_sem.at[j, 0, 1], up)
        landed(far_y.at[j, 1], far_sem.at[j, 1])
        add(late(3, j, h_late, h_late), far_y.at[j, 1])
        copies.send(late(3, j, h_late, h_late), near_y.at[j, 1, pl.ds(h_late, h_late)], near_sem.at[j, 1, 1], down)

    landed(cross_x.at[2], cross_sem.at[2])
    add(first(2, 0), cross_x.at[2])
    copies.send(first(2, 0, 0, h_early), far_x.at[0], far_sem.at[2, 0], up)
    copies.send(first(2, 0, h_early, h_early), far_x.at[1], far_sem.at[2, 1], down)
    landed(cross_x.at[1], cross_sem.at[1])
    add(first(1, 0), cross_x.at[1])
    copies.send(first(1, 0, h_early, h_early), near_x.at[0, pl.ds(h_early, h_early)], near_sem.at[2, 0, 0], up)
    landed(cross_x.at[3], cross_sem.at[3])
    add(first(3, 0), cross_x.at[3])
    copies.send(first(3, 0, 0, h_early), near_x.at[1, pl.ds(0, h_early)], near_sem.at[2, 1, 0], down)

    def both_near(j, ref):
        count = ref.shape[1] // 2
        for side in range(2):
            for turn in range(2):
                start = count if (side == 0) == (turn == 0) else 0
                landed(ref.at[side, pl.ds(start, count)], near_sem.at[j, side, turn])

    both_near(1, near_y.at[1])
    add(late(0, 1), near_y.at[1, 0], near_y.at[1, 1])
    copies.send(late(0, 1), cross_y, cross_sem.at[4], across)

    landed(far_x.at[0], far_sem.at[2, 0])
    add(first(1, 0, 0, h_early), far_x.at[0])
    copies.send(first(1, 0, 0, h_early), near_x.at[0, pl.ds(0, h_early)], near_sem.at[2, 0, 1], up)
    landed(far_x.at[1], far_sem.at[2, 1])
    add(first(3, 0, h_early, h_early), far_x.at[1])
    copies.send(first(3, 0, h_early, h_early), near_x.at[1, pl.ds(h_early, h_early)], near_sem.at[2, 1, 1], down)

    dressed_copy.wait()
    for h in range(2):
        other[h] = dressed_b[:, h * 128 : (h + 1) * 128].astype(f32)

    def settle(at, *terms):
        result = terms[0][...].astype(f32)
        for each in terms[1:]:
            result = result + each[...].astype(f32)
        result = result.astype(bf16)
        out_ref[at] = result
        for h in range(2):
            total[h, at] = result[:, h * 128 : (h + 1) * 128].astype(f32)

    def column(ref, l, start, count):
        halves = [ref[h, pl.ds(start * 32 + l, count, stride=32), :].astype(bf16) for h in range(2)]
        return jnp.concatenate(halves, 1)

    def energy(start):
        result = jnp.zeros((TILE // 2, TILE), f32)
        for l in range(32):
            result = result + lax.dot_general(
                column(total, l, start, TILE // 2),
                column(other, l, 0, TILE),
                (((1,), (1,)), ((), ())),
                preferred_element_type=f32,
            )
        tile[start : start + TILE // 2] = jnp.concatenate([-result, jnp.zeros_like(result)], 1)

    both_near(0, near_y.at[0])
    landed(cross_x.at[0], cross_sem.at[0])
    landed(cross_y, cross_sem.at[4])
    settle(pl.ds(0, LATE), late(0, 0), near_y.at[0, 0], near_y.at[0, 1], cross_y)
    energy(0)
    both_near(2, near_x)
    settle(pl.ds(LATE, early), first(0, 0), cross_x.at[0], near_x.at[0], near_x.at[1])
    energy(TILE // 2)

    def share_of(row):
        return pl.ds(pl.multiple_of(row * 8, 8), 8)

    for s in range(1, 8):
        target = in_row(s // 2, s % 2)
        copies.send(tile.at[share_of(target[0])], tile_row.at[s], row_sem.at[s], target)
    mine = tile[share_of(y * 2 + xh)]
    for s in range(1, 8):
        landed(tile_row.at[s], row_sem.at[s])
        mine = mine + tile_row[s]
    row_sum[...] = mine
    for d in range(1, 16):
        copies.send(row_sum, tile_col.at[d], col_sem.at[d], in_col(d))
    for d in range(1, 16):
        landed(tile_col.at[d], col_sem.at[d])
        mine = mine + tile_col[d]
    energy_ref[...] = mine
    copies.finish()


def contract(screened, panel_t, dressed):
    rows = TILE * 32
    cols = screened.shape[1]
    early = rows - LATE
    bf16, f32 = jnp.bfloat16, jnp.float32
    dma = pltpu.SemaphoreType.DMA
    hbm, vmem = pl.BlockSpec(memory_space=pl.ANY), pl.BlockSpec(memory_space=pltpu.VMEM)
    return pl.pallas_call(
        contract_kernel,
        out_shape=(jax.ShapeDtypeStruct((rows, cols), bf16), jax.ShapeDtypeStruct((8, 128), f32)),
        in_specs=[vmem, hbm, hbm],
        out_specs=(vmem, vmem),
        scratch_shapes=[
            pltpu.VMEM((2, rows, screened.shape[0]), bf16),
            pltpu.VMEM((8, rows, cols), bf16),
            pltpu.VMEM((2, 2, LATE // 2, cols), bf16),
            pltpu.VMEM((2, 2, LATE, cols), bf16),
            pltpu.VMEM((LATE, cols), bf16),
            pltpu.VMEM((4, early, cols), bf16),
            pltpu.VMEM((2, early // 2, cols), bf16),
            pltpu.VMEM((2, early, cols), bf16),
            pltpu.VMEM((2, rows, 128), f32),
            pltpu.VMEM((2, rows, 128), f32),
            pltpu.VMEM((rows, cols), bf16),
            pltpu.VMEM((TILE, 128), f32),
            pltpu.VMEM((8, 128), f32),
            pltpu.VMEM((8, 8, 128), f32),
            pltpu.VMEM((16, 8, 128), f32),
            dma((48,)),
            dma((3,)),
            dma((3, 2)),
            dma((3, 2, 2)),
            dma((5,)),
            dma((8,)),
            dma((16,)),
        ],
        compiler_params=pltpu.CompilerParams(
            collective_id=1, has_side_effects=True, vmem_limit_bytes=56 * 2**20
        ),
        name="contract",
    )(screened, panel_t, dressed)


def per_device(
    polarization, metric, three_panel, three_near, green_function, mask_panel, mask_near
):
    row_count = lax.axis_size("row")
    col_index = lax.axis_index("col")
    near_cols = metric.shape[1]
    near_share = NL // row_count
    screened, panel_t, dressed = screen(
        polarization, metric, three_panel, three_near, mask_panel, mask_near, green_function
    )
    contracted, energy = contract(screened, panel_t, dressed)
    contracted = contracted.T.reshape(near_cols, TILE, near_share)
    self_energy = lax.dynamic_slice_in_dim(energy, col_index * 4, 4, 1)
    return (screened, contracted, self_energy)


def solution(mesh):
    placed = (
        P("row", "col"),
        P("row", "col"),
        P("row", None, None),
        P("col", None, None),
        P(),
        P(),
        P(),
    )
    return jax.shard_map(
        per_device,
        mesh=mesh,
        in_specs=placed,
        out_specs=(P("row", "col"), P("col", None, "row"), P("row", "col")),
        check_vma=False,
    )
```

```python
import functools

import jax
import jax.numpy as jnp
from jax import lax
from jax.experimental import pallas as pl
from jax.experimental.pallas import tpu as pltpu
from jax.sharding import PartitionSpec as P

TILE = 64
NL = 256
RB = 64
AB = 32
MESH = pl.DeviceIdType.MESH


def place():
    row, col = lax.axis_index("row"), lax.axis_index("col")
    return row // 2, row % 2, col // 4, (col // 2) % 2, col % 2


def device(y, xh, z, xl, core):
    return (y * 2 + xh, (z * 2 + xl) * 2 + core)


class Copies:
    def __init__(self, send_sem):
        self.send_sem, self.started = send_sem, []

    def send(self, src, dst, recv_sem, target):
        index = len(self.started)
        copy = pltpu.make_async_remote_copy(
            src_ref=src,
            dst_ref=dst,
            send_sem=self.send_sem.at[index],
            recv_sem=recv_sem,
            device_id=target,
            device_id_type=MESH,
        )
        copy.start()
        self.started.append((copy, None))

    def send_if(self, wanted, src, dst, recv_sem, target):
        index = len(self.started)
        copy = pltpu.make_async_remote_copy(
            src_ref=src,
            dst_ref=dst,
            send_sem=self.send_sem.at[index],
            recv_sem=recv_sem,
            device_id=target,
            device_id_type=MESH,
        )
        pl.when(wanted)(copy.start)
        self.started.append((copy, wanted))

    def finish(self):
        for copy, wanted in self.started:
            if wanted is None:
                copy.wait_send()
            else:
                pl.when(wanted)(copy.wait_send)


def landed(ref, sem):
    pltpu.make_async_copy(ref, ref, sem).wait()


def prepare(panel, near, panel_mask, near_mask, green, panel_t, dressed, taken, flat, made, made_near, sem):
    start = lambda k, size: pl.ds(pl.multiple_of(k * size, size), size)

    def steps(source, mask, count, make, put, first, last):
        def fetch(i):
            block = source.at[start(i // 4, 128), start(i % 4, 16)]
            return pltpu.make_async_copy(block, taken.at[i % 2], sem.at[i % 2])

        fetch(first).start()

        def body(i, carry):
            @pl.when(i + 1 < last)
            def _():
                fetch(i + 1).start()

            fetch(i).wait()

            @pl.when(i >= first + 2)
            def _():
                put(i - 2).wait()

            for h in range(2):
                lanes = slice(h * 128, (h + 1) * 128)
                flat[h] = taken[i % 2, :, :, lanes].astype(jnp.float32).reshape(128 * 16, 128)
            rows = start(i // 4, 128)
            for m in range(16):
                make(
                    i,
                    m,
                    [
                        flat[h, pl.ds(m, 128, stride=16), :] * mask[rows, h * 128 : (h + 1) * 128]
                        for h in range(2)
                    ],
                )
            put(i).start()
            return carry

        lax.fori_loop(first, last, body, 0)
        put(last - 2).wait()
        put(last - 1).wait()

    def put_panel(i):
        place_at = panel_t.at[:, start(i % 4, 512), start(i // 4, 128)]
        return pltpu.make_async_copy(made.at[i % 2], place_at, sem.at[2 + i % 2])

    def put_near(i):
        place_at = dressed.at[start(i % 4, 512), start(i // 4, 128)]
        return pltpu.make_async_copy(made_near.at[i % 2], place_at, sem.at[2 + i % 2])

    def make_panel(i, m, halves):
        turned = jnp.concatenate([half.T.astype(jnp.bfloat16) for half in halves], 0)
        made[i % 2, :, m * 32 : (m + 1) * 32, :] = turned.reshape(8, 32, 128)

    def make_near(i, m, halves):
        block = jnp.concatenate([half.astype(jnp.bfloat16) for half in halves], 1)
        product = lax.dot_general(
            green[...], block, (((1,), (1,)), ((), ())), preferred_element_type=jnp.float32
        )
        made_near[i % 2, m * 32 : (m + 1) * 32, :] = product.astype(jnp.bfloat16)

    return (
        functools.partial(steps, panel, panel_mask, 16, make_panel, put_panel),
        functools.partial(steps, near, near_mask, 8, make_near, put_near),
    )


def screen_part(
    a_ref,
    b_ref,
    panel,
    near,
    panel_mask_ref,
    near_mask_ref,
    green_ref,
    out_ref,
    panel_t,
    dressed,
    ahead,
    a0,
    a1,
    b0,
    b1,
    a1_own,
    total,
    give,
    take,
    taken,
    flat,
    made,
    made_near,
    panel_blocks,
    near_blocks,
    panel_mask,
    near_mask,
    green,
    send_sem,
    own_sem,
    local_sem,
    x_sem,
    near_sem,
    far_sem,
    twin_sem,
    last_sem,
    step_sem,
    small_sem,
):
    row, col = lax.axis_index("row"), lax.axis_index("col")
    small = [
        pltpu.make_async_copy(panel_mask_ref, panel_blocks, small_sem.at[0]),
        pltpu.make_async_copy(near_mask_ref, near_blocks, small_sem.at[1]),
        pltpu.make_async_copy(
            green_ref.at[pl.ds(pl.multiple_of(row * 32, 32), 32)], green, small_sem.at[2]
        ),
    ]
    for copy in small:
        copy.start()

    def finish_masks():
        for copy in small:
            copy.wait()
        for blocks, mask, begin in (
            (panel_blocks, panel_mask, row * (panel_mask.shape[0] // RB)),
            (near_blocks, near_mask, col * (near_mask.shape[0] // RB)),
        ):
            count = mask.shape[0]
            shape = (count, blocks.shape[1])
            at = lax.broadcasted_iota(jnp.int32, shape, 0) // RB + begin
            pick = (at == lax.broadcasted_iota(jnp.int32, shape, 1)).astype(jnp.float32)
            shape = (blocks.shape[0], NL)
            wide = lax.broadcasted_iota(jnp.int32, shape, 1) // AB == lax.broadcasted_iota(jnp.int32, shape, 0)
            picked = lax.dot_general(
                pick, blocks[...].astype(jnp.float32), (((1,), (1,)), ((), ())), preferred_element_type=jnp.float32
            )
            mask[...] = jnp.dot(picked, wide.astype(jnp.float32), preferred_element_type=jnp.float32)

    panel_steps, near_steps = prepare(
        panel, near, panel_mask, near_mask, green, panel_t, dressed, taken, flat, made, made_near, step_sem
    )
    y, xh, z, xl, core = place()
    twin = device(y, xh, z, xl, 1 - core)
    rows, depth = a_ref.shape
    half, piece = rows // 2, rows // 4
    z_at = [lax.rem(z + d, 4) for d in range(4)]
    y_at = [lax.rem(y + d, 4) for d in range(4)]

    barrier = pltpu.get_barrier_semaphore()
    partners = [device(lax.rem(y + k // 2, 4), lax.rem(xh + k, 2), z, xl, core) for k in range(1, 8)]
    partners += [(row, lax.rem(col + k, 16)) for k in range(1, 16)]
    partners.append(device(y, 1 - xh, z, 1 - xl, core))
    for partner in partners:
        pl.semaphore_signal(barrier, inc=1, device_id=partner, device_id_type=MESH)
    pl.semaphore_wait(barrier, len(partners))

    copies = Copies(send_sem)

    own0, own1 = pl.ds(0, half), pl.ds(half, half)

    @pl.when(core == 0)
    def _():
        pltpu.make_async_copy(a_ref, a0.at[z], local_sem.at[0]).start()
        copy = pltpu.make_async_remote_copy(
            a_ref, a0.at[z], own_sem, local_sem.at[0], device_id=twin, device_id_type=MESH
        )
        copy.start()

    @pl.when(core == 1)
    def _():
        pltpu.make_async_copy(a_ref.at[own1], a1_own, local_sem.at[1]).start()
        copy = pltpu.make_async_remote_copy(
            a_ref.at[own0], a1_own, own_sem, local_sem.at[1], device_id=twin, device_id_type=MESH
        )
        copy.start()

    deep = (depth // 256 * 128 + 128, depth // 256 * 128)

    def b_slot(stream, k, p, part=None):
        buffer = b1.at[k] if stream == 0 else b0.at[k, stream - 1]
        start, count = p * deep[0], deep[p]
        if part is not None:
            start, count = start + part * (count // 2), count // 2
        return buffer.at[pl.ds(start, count)]

    def a_rows(stream, k, start, count):
        buffer = a0.at[k] if stream == 0 else a1.at[k, stream - 1]
        return buffer.at[pl.ds(start, count)]

    def a_slot(stream, k, p, part=None, of=core):
        start, count = of * half + p * piece, piece
        if part is not None:
            start, count = start + part * (count // 2), count // 2
        return a_rows(stream, k, pl.multiple_of(start, piece // 2), count)

    b_up = [device(y_at[1], xh, z, xl, core), device(y_at[3], xh, z, xl, core)]
    a_up = [device(y, xh, z_at[1], xl, core), device(y, xh, z_at[3], xl, core)]
    A, B = (a_slot, 0, z_at, a_up), (b_slot, 3, y_at, b_up)

    def b_own(p, base=0):
        return b_ref.at[pl.ds(base + p * deep[0], deep[p])]

    inner = xh != xl

    def b_along_x(p):
        def at(role):
            return b0.at[y, role, pl.ds(p * deep[0], deep[p])]

        for j in range(2):
            copies.send_if(inner, b_own(p), at(0), x_sem.at[1, 0, p], device(y, j, z, xh, core))

    def a_along_x(p):
        source = a1_own.at[pl.ds(p * piece, piece)]
        for j in range(2):
            copies.send_if(inner, source, a_slot(1, z, p), x_sem.at[0, 0, p], device(y, xl, z, j, core))

    outer = jnp.logical_not(inner)

    def a_outer_along_x(p):
        source = a1_own.at[pl.ds(p * piece, piece)]
        copies.send_if(outer, source, a_slot(2, z, p), x_sem.at[0, 1, p], device(y, xh, z, 1 - xl, core))

    def b_outer_along_x(p):
        copies.send_if(outer, b_own(p), b_slot(2, y, p), x_sem.at[1, 1, p], device(y, 1 - xh, z, xl, core))

    def outer_keep():
        for p in range(2):
            source = a1_own.at[pl.ds(p * piece, piece)]
            pltpu.make_async_copy(source, a_slot(2, z, p), x_sem.at[0, 1, p]).start()
            pltpu.make_async_copy(b_own(p), b_slot(2, y, p), x_sem.at[1, 1, p]).start()

    def spread(array, stream, p, source=None):
        slot, base, at, to = array
        for side in range(2):
            here = slot(stream, at[0], p)
            copies.send(here if source is None else source, here, near_sem.at[base + stream, side, p], to[side])

    def start_near(wanted, p, source):
        for side in range(2):
            copies.send_if(wanted, source, a_slot(0, z, p), near_sem.at[0, side, p], a_up[side])

    def to_twin(stream, k, p, index):
        here = a_slot(stream, k, p)
        copies.send(here, here, twin_sem.at[stream, index, p], twin)

    def go_on(array, stream, p):
        slot, base, at, to = array
        for side in range(2):
            k = at[3 - 2 * side]
            landed(slot(stream, k, p), near_sem.at[base + stream, side, p])
            half_of = slot(stream, k, p, side)
            copies.send(half_of, half_of, far_sem.at[base + stream, side, p], to[side])
        if base == 0:
            for side in range(2):
                to_twin(stream, at[3 - 2 * side], p, 3 - 2 * side)

    def far(array, stream, p):
        slot, base, at, to = array
        for side in range(2):
            landed(slot(stream, at[2], p, side), far_sem.at[base + stream, side, p])
        if base == 0:
            to_twin(stream, at[2], p, 2)

    def from_twin(stream, p, indices):
        for d in indices:
            landed(a_slot(stream, z_at[d], p, of=1 - core), twin_sem.at[stream, d, p])

    def arrive(s, p):
        landed(a_slot(s, z, p), x_sem.at[0, s - 1, p])
        spread(A, s, p)
        landed(b_slot(s, y, p), x_sem.at[1, s - 1, p])
        spread(B, s, p)
        to_twin(s, z, p, 0)

    def keep_rows(k, p, j):
        lanes = slice(p * deep[0], p * deep[0] + deep[p])

        def body(t, carry):
            at = pl.ds(pl.multiple_of(t * half, half), half)
            total[0, j, at] += jnp.dot(
                a0[k, at, lanes], b0[k, j, lanes], preferred_element_type=jnp.float32
            )
            return carry

        lax.fori_loop(0, 2, body, 0)

    def keep_cols(k, p, j):
        def body(t, carry):
            at = pl.ds(pl.multiple_of(t * half + p * piece, piece), piece)
            total[1, j, at] += jnp.dot(a1[k, j, at], b1[k], preferred_element_type=jnp.float32)
            return carry

        lax.fori_loop(0, 2, body, 0)

    for p in range(2):
        start_near(core == 0, p, a_ref.at[pl.ds(p * piece, piece)])
    b_along_x(0)
    for p in range(2):
        spread(B, 0, p, b_own(p, depth))
    landed(a1_own, local_sem.at[1])
    a_along_x(0)
    b_along_x(1)
    a_along_x(1)
    landed(a0.at[z], local_sem.at[0])
    for p in range(2):
        start_near(core == 1, p, a_slot(0, z, p))
    pl.when(outer)(outer_keep)
    b_local = pltpu.make_async_copy(b_ref.at[pl.ds(depth, depth)], b1.at[y], local_sem.at[2])
    b_local.start()
    total[...] = jnp.zeros_like(total)
    finish_masks()

    panel_steps(0, 4)
    go_on(B, 0, 0)
    go_on(A, 0, 0)
    panel_steps(4, 8)
    go_on(B, 0, 1)
    go_on(A, 0, 1)
    arrive(1, 0)
    for p in range(2):
        a_outer_along_x(p)
    panel_steps(8, 11)
    for p in range(2):
        far(B, 0, p)
        far(A, 0, p)
    arrive(1, 1)
    for p in range(2):
        b_outer_along_x(p)
    panel_steps(11, 14)
    go_on(A, 1, 0)
    go_on(B, 1, 0)
    panel_steps(14, 16)
    near_steps(0, 2)
    arrive(2, 0)
    go_on(A, 1, 1)
    go_on(B, 1, 1)
    near_steps(2, 4)
    for p in range(2):
        from_twin(0, p, (1, 2, 3))
    b_local.wait()

    def others(p):
        def step(d, carry):
            keep_rows(lax.rem(y + d, 4), p, 0)
            keep_cols(lax.rem(z + d, 4), p, 0)
            return carry

        lax.fori_loop(0, 4, step, 0)

    far(A, 1, 0)
    far(B, 1, 0)
    arrive(2, 1)
    near_steps(4, 8)
    from_twin(1, 0, (0, 1, 2, 3))
    others(0)
    far(A, 1, 1)
    far(B, 1, 1)
    go_on(A, 2, 0)
    go_on(B, 2, 0)
    from_twin(1, 1, (0, 1, 2, 3))
    others(1)
    for i in range(2):
        give[i] = total[i, 0].astype(jnp.bfloat16)
    copies.send(give.at[0], take.at[0], last_sem.at[0], device(y, xh, z, 1 - xl, core))
    copies.send(give.at[1], take.at[1], last_sem.at[1], device(y, 1 - xh, z, xl, core))
    from_twin(2, 0, (0, 1, 3))

    def own(p):
        def step(d):
            keep_rows(y_at[d], p, 1)
            keep_cols(z_at[d], p, 1)

        return step

    step = own(0)
    for d in (0, 1, 3):
        step(d)
    go_on(A, 2, 1)
    go_on(B, 2, 1)
    far(A, 2, 0)
    far(B, 2, 0)
    from_twin(2, 0, (2,))
    from_twin(2, 1, (0, 1, 3))
    step(2)
    step = own(1)
    for d in (0, 1, 3):
        step(d)
    ahead()
    far(B, 2, 1)
    keep_rows(y_at[2], 1, 1)
    far(A, 2, 1)
    landed(take.at[0], last_sem.at[0])
    landed(take.at[1], last_sem.at[1])
    total[0, 1] += total[1, 1] + take[0].astype(jnp.float32) + take[1].astype(jnp.float32)
    total[1, 1] = jnp.zeros_like(total[1, 1])
    from_twin(2, 1, (2,))
    keep_cols(z_at[2], 1, 1)
    out_ref[...] = (total[0, 1] + total[1, 1]).astype(jnp.bfloat16)

    def finish():
        copies.finish()

        @pl.when(core == 0)
        def _():
            pltpu.make_async_copy(a_ref, a0.at[z], own_sem).wait()

        @pl.when(core == 1)
        def _():
            pltpu.make_async_copy(a_ref.at[own0], a1_own, own_sem).wait()

    return finish


LATE = 1152


def contract_part(
    s_ref,
    panel_t,
    dressed,
    out_ref,
    energy_ref,
    block,
    part,
    far_y,
    near_y,
    cross_y,
    cross_x,
    far_x,
    near_x,
    total,
    other,
    tile,
    row_sum,
    tile_row,
    tile_col,
    send_sem,
    block_sem,
    far_sem,
    near_sem,
    cross_sem,
    row_sem,
    col_sem,
):
    y, xh, z, xl, core = place()
    col = (z * 2 + xl) * 2 + core
    f32, bf16 = jnp.float32, jnp.bfloat16

    def in_row(d, j):
        return device(lax.rem(y + d, 4), lax.rem(xh + j, 2), z, xl, core)

    def in_col(d):
        return (y * 2 + xh, lax.rem(col + d, 16))

    order = [(2, 1), (2, 0), (1, 1), (3, 1), (1, 0), (3, 0), (0, 1), (0, 0)]
    chunk = block.shape[1]

    def fetch(i):
        d, j = order[i // 2]
        share = lax.rem(y + d, 4) * 2 + lax.rem(xh + j, 2)
        return pltpu.make_async_copy(
            panel_t.at[share, pl.ds(i % 2 * chunk, chunk)], block.at[i % 2], block_sem.at[i % 2]
        )

    fetch(0).start()
    fetch(1).start()
    for h in range(2):
        other[h] = dressed[:, h * 128 : (h + 1) * 128].astype(f32)
    yield

    copies = Copies(send_sem)
    rows = TILE * 32
    early = rows - LATE
    h_late, h_early = LATE // 2, early // 2
    up, down, across = in_row(1, 0), in_row(3, 0), in_row(0, 1)

    def late(d, j, start=0, count=LATE):
        return part.at[d * 2 + j, pl.ds(start, count)]

    def first(d, j, start=0, count=early):
        return part.at[d * 2 + j, pl.ds(LATE + start, count)]

    for i, (d, j) in enumerate(order):
        for h in range(2):
            fetch(i * 2 + h).wait()

            def multiply(t, carry):
                at = pl.ds(pl.multiple_of(t * 256, 256), 256)
                to = pl.ds(pl.multiple_of(h * chunk + t * 256, 256), 256)
                part[d * 2 + j, to] = jnp.dot(
                    block[h, at], s_ref[...], preferred_element_type=f32
                ).astype(bf16)
                return carry

            lax.fori_loop(0, chunk // 256, multiply, 0)
            if i < 7:
                fetch(i * 2 + 2 + h).start()
        if j == 1:
            copies.send(first(d, 1), cross_x.at[d], cross_sem.at[d], across)
        if d == 2:
            copies.send(late(2, j, 0, h_late), far_y.at[j, 0], far_sem.at[j, 0], up)
            copies.send(late(2, j, h_late, h_late), far_y.at[j, 1], far_sem.at[j, 1], down)
        if d == 1:
            copies.send(late(1, j, h_late, h_late), near_y.at[j, 0, pl.ds(h_late, h_late)], near_sem.at[j, 0, 0], up)
        if d == 3:
            copies.send(late(3, j, 0, h_late), near_y.at[j, 1, pl.ds(0, h_late)], near_sem.at[j, 1, 0], down)

    def add(ref, *others):
        result = ref[...].astype(f32)
        for each in others:
            result = result + each[...].astype(f32)
        ref[...] = result.astype(bf16)

    for j in (1, 0):
        landed(far_y.at[j, 0], far_sem.at[j, 0])
        add(late(1, j, 0, h_late), far_y.at[j, 0])
        copies.send(late(1, j, 0, h_late), near_y.at[j, 0, pl.ds(0, h_late)], near_sem.at[j, 0, 1], up)
        landed(far_y.at[j, 1], far_sem.at[j, 1])
        add(late(3, j, h_late, h_late), far_y.at[j, 1])
        copies.send(late(3, j, h_late, h_late), near_y.at[j, 1, pl.ds(h_late, h_late)], near_sem.at[j, 1, 1], down)

    landed(cross_x.at[2], cross_sem.at[2])
    add(first(2, 0), cross_x.at[2])
    copies.send(first(2, 0, 0, h_early), far_x.at[0], far_sem.at[2, 0], up)
    copies.send(first(2, 0, h_early, h_early), far_x.at[1], far_sem.at[2, 1], down)
    landed(cross_x.at[1], cross_sem.at[1])
    add(first(1, 0), cross_x.at[1])
    copies.send(first(1, 0, h_early, h_early), near_x.at[0, pl.ds(h_early, h_early)], near_sem.at[2, 0, 0], up)
    landed(cross_x.at[3], cross_sem.at[3])
    add(first(3, 0), cross_x.at[3])
    copies.send(first(3, 0, 0, h_early), near_x.at[1, pl.ds(0, h_early)], near_sem.at[2, 1, 0], down)

    def both_near(j, ref):
        count = ref.shape[1] // 2
        for side in range(2):
            for turn in range(2):
                start = count if (side == 0) == (turn == 0) else 0
                landed(ref.at[side, pl.ds(start, count)], near_sem.at[j, side, turn])

    both_near(1, near_y.at[1])
    add(late(0, 1), near_y.at[1, 0], near_y.at[1, 1])
    copies.send(late(0, 1), cross_y, cross_sem.at[4], across)

    landed(far_x.at[0], far_sem.at[2, 0])
    add(first(1, 0, 0, h_early), far_x.at[0])
    copies.send(first(1, 0, 0, h_early), near_x.at[0, pl.ds(0, h_early)], near_sem.at[2, 0, 1], up)
    landed(far_x.at[1], far_sem.at[2, 1])
    add(first(3, 0, h_early, h_early), far_x.at[1])
    copies.send(first(3, 0, h_early, h_early), near_x.at[1, pl.ds(h_early, h_early)], near_sem.at[2, 1, 1], down)

    def settle(at, *terms):
        result = terms[0][...].astype(f32)
        for each in terms[1:]:
            result = result + each[...].astype(f32)
        result = result.astype(bf16)
        out_ref[at] = result
        for h in range(2):
            total[h, at] = result[:, h * 128 : (h + 1) * 128].astype(f32)

    def column(ref, l, start, count):
        halves = [ref[h, pl.ds(start * 32 + l, count, stride=32), :].astype(bf16) for h in range(2)]
        return jnp.concatenate(halves, 1)

    def energy(start):
        result = jnp.zeros((TILE // 2, TILE), f32)
        for l in range(32):
            result = result + lax.dot_general(
                column(total, l, start, TILE // 2),
                column(other, l, 0, TILE),
                (((1,), (1,)), ((), ())),
                preferred_element_type=f32,
            )
        tile[start : start + TILE // 2] = jnp.concatenate([-result, jnp.zeros_like(result)], 1)

    both_near(0, near_y.at[0])
    landed(cross_x.at[0], cross_sem.at[0])
    landed(cross_y, cross_sem.at[4])
    settle(pl.ds(0, LATE), late(0, 0), near_y.at[0, 0], near_y.at[0, 1], cross_y)
    energy(0)
    both_near(2, near_x)
    settle(pl.ds(LATE, early), first(0, 0), cross_x.at[0], near_x.at[0], near_x.at[1])
    energy(TILE // 2)

    def share_of(row):
        return pl.ds(pl.multiple_of(row * 8, 8), 8)

    for s in range(1, 8):
        target = in_row(s // 2, s % 2)
        copies.send(tile.at[share_of(target[0])], tile_row.at[s], row_sem.at[s], target)
    mine = tile[share_of(y * 2 + xh)]
    for s in range(1, 8):
        landed(tile_row.at[s], row_sem.at[s])
        mine = mine + tile_row[s]
    row_sum[...] = mine
    for d in range(1, 16):
        copies.send(row_sum, tile_col.at[d], col_sem.at[d], in_col(d))
    for d in range(1, 16):
        landed(tile_col.at[d], col_sem.at[d])
        mine = mine + tile_col[d]
    turned = pltpu.roll(mine, lax.rem(128 - 4 * col, 128), 1).T
    energy_ref[...] = turned[:4]
    copies.finish()


SCREEN_SCRATCH = 27


def kernel(*refs):
    inputs, (screened, contracted, energy, panel_t), scratch = refs[:7], refs[7:11], refs[11:]
    dressed, (first, second) = scratch[0], (scratch[1 : 1 + SCREEN_SCRATCH], scratch[1 + SCREEN_SCRATCH :])
    flat = first[9]
    steps = contract_part(screened, panel_t, dressed, contracted, energy, *second[:8], flat, *second[8:])
    finish = screen_part(*inputs, screened, panel_t, dressed, lambda: next(steps), *first)
    next(steps, None)
    finish()


def tile_terms(a, b, panel, near, panel_mask, near_mask, green):
    rows, depth = a.shape
    cols = b.shape[1]
    long = TILE * 32
    early = long - LATE
    bf16, f32 = jnp.bfloat16, jnp.float32
    dma = pltpu.SemaphoreType.DMA
    hbm, vmem = pl.BlockSpec(memory_space=pl.ANY), pl.BlockSpec(memory_space=pltpu.VMEM)
    first = [
        pltpu.VMEM((4, rows, depth), bf16),
        pltpu.VMEM((4, 2, rows, depth), bf16),
        pltpu.VMEM((4, 2, depth, cols), bf16),
        pltpu.VMEM((4, depth, cols), bf16),
        pltpu.VMEM((rows // 2, depth), bf16),
        pltpu.VMEM((2, 2, rows, cols), f32),
        pltpu.VMEM((2, rows, cols), bf16),
        pltpu.VMEM((2, rows, cols), bf16),
        pltpu.VMEM((2, 128, 16, NL), bf16),
        pltpu.VMEM((2, 128 * 16, 128), f32),
        pltpu.VMEM((2, 8, 16 * 32, 128), bf16),
        pltpu.VMEM((2, 16 * 32, 128), bf16),
        pltpu.VMEM(panel_mask.shape, jnp.int32),
        pltpu.VMEM(near_mask.shape, jnp.int32),
        pltpu.VMEM((rows, NL), f32),
        pltpu.VMEM((cols, NL), f32),
        pltpu.VMEM((32, NL), bf16),
        dma((96,)),
        dma,
        dma((3,)),
        dma((2, 2, 2)),
        dma((6, 2, 2)),
        dma((6, 2, 2)),
        dma((3, 4, 2)),
        dma((2,)),
        dma((4,)),
        dma((3,)),
    ]
    second = [
        pltpu.VMEM((2, long // 2, rows), bf16),
        pltpu.VMEM((8, long, cols), bf16),
        pltpu.VMEM((2, 2, LATE // 2, cols), bf16),
        pltpu.VMEM((2, 2, LATE, cols), bf16),
        pltpu.VMEM((LATE, cols), bf16),
        pltpu.VMEM((4, early, cols), bf16),
        pltpu.VMEM((2, early // 2, cols), bf16),
        pltpu.VMEM((2, early, cols), bf16),
        pltpu.VMEM((2, long, 128), f32),
        pltpu.VMEM((TILE, 128), f32),
        pltpu.VMEM((8, 128), f32),
        pltpu.VMEM((8, 8, 128), f32),
        pltpu.VMEM((16, 8, 128), f32),
        dma((48,)),
        dma((2,)),
        dma((3, 2)),
        dma((3, 2, 2)),
        dma((5,)),
        dma((8,)),
        dma((16,)),
    ]
    assert len(first) == SCREEN_SCRATCH
    return pl.pallas_call(
        kernel,
        out_shape=(
            jax.ShapeDtypeStruct((rows, cols), bf16),
            jax.ShapeDtypeStruct((long, cols), bf16),
            jax.ShapeDtypeStruct((4, 8), f32),
            jax.ShapeDtypeStruct((8, long, rows), bf16),
        ),
        in_specs=[hbm] * 7,
        out_specs=(vmem, vmem, vmem, hbm),
        scratch_shapes=[pltpu.VMEM((long, cols), bf16)] + first + second,
        compiler_params=pltpu.CompilerParams(
            collective_id=0, has_side_effects=True, vmem_limit_bytes=64 * 2**20 - 2**16
        ),
        name="tile_terms",
    )(a, b, panel, near, panel_mask, near_mask, green)


def hand_over_kernel(*refs):
    sources, results, sem = refs[:3], refs[3:6], refs[6]
    copies = [pltpu.make_async_copy(sources[i], results[i], sem.at[i]) for i in range(3)]
    for copy in copies:
        copy.start()
    for copy in copies:
        copy.wait()


def hand_over(*arrays):
    hbm = pl.BlockSpec(memory_space=pl.ANY)
    return pl.pallas_call(
        hand_over_kernel,
        out_shape=tuple(jax.ShapeDtypeStruct(array.shape, array.dtype) for array in arrays),
        in_specs=[hbm] * 3,
        out_specs=(hbm,) * 3,
        scratch_shapes=[pltpu.SemaphoreType.DMA((3,))],
        name="hand_over",
    )(*arrays)


def per_device(
    polarization, metric, three_panel, three_near, green_function, mask_panel, mask_near
):
    near_cols = metric.shape[1]
    screened, contracted, energy, _ = tile_terms(
        polarization, metric, three_panel, three_near, mask_panel.T, mask_near.T, green_function
    )
    screened, contracted, energy = hand_over(screened, contracted, energy)
    return screened, contracted.T.reshape(near_cols, TILE, contracted.shape[0] // TILE), energy.T


def solution(mesh):
    placed = (
        P("row", "col"),
        P("row", "col"),
        P("row", None, None),
        P("col", None, None),
        P(),
        P(),
        P(),
    )
    return jax.shard_map(
        per_device,
        mesh=mesh,
        in_specs=placed,
        out_specs=(P("row", "col"), P("col", None, "row"), P("row", "col")),
        check_vma=False,
    )
```

```python
import functools

import jax
import jax.numpy as jnp
from jax import lax
from jax.experimental import pallas as pl
from jax.experimental.pallas import tpu as pltpu
from jax.sharding import PartitionSpec as P

TILE = 64
NL = 256
RB = 64
AB = 32
MESH = pl.DeviceIdType.MESH


def place():
    row, col = lax.axis_index("row"), lax.axis_index("col")
    return row // 2, row % 2, col // 4, (col // 2) % 2, col % 2


def device(y, xh, z, xl, core):
    return (y * 2 + xh, (z * 2 + xl) * 2 + core)


class Copies:
    def __init__(self, send_sem):
        self.send_sem, self.started = send_sem, []

    def send(self, src, dst, recv_sem, target):
        index = len(self.started)
        copy = pltpu.make_async_remote_copy(
            src_ref=src,
            dst_ref=dst,
            send_sem=self.send_sem.at[index],
            recv_sem=recv_sem,
            device_id=target,
            device_id_type=MESH,
        )
        copy.start()
        self.started.append((copy, None))

    def send_if(self, wanted, src, dst, recv_sem, target):
        index = len(self.started)
        copy = pltpu.make_async_remote_copy(
            src_ref=src,
            dst_ref=dst,
            send_sem=self.send_sem.at[index],
            recv_sem=recv_sem,
            device_id=target,
            device_id_type=MESH,
        )
        pl.when(wanted)(copy.start)
        self.started.append((copy, wanted))

    def finish(self):
        for copy, wanted in self.started:
            if wanted is None:
                copy.wait_send()
            else:
                pl.when(wanted)(copy.wait_send)


def landed(ref, sem):
    pltpu.make_async_copy(ref, ref, sem).wait()


def prepare(panel, near, panel_mask, near_mask, green, panel_t, dressed, taken, flat, made, sem):
    start = lambda k, size: pl.ds(pl.multiple_of(k * size, size), size)

    def steps(source, mask, count, make, put, first, last):
        def fetch(i):
            block = source.at[start(i // 4, 128), start(i % 4, 16)]
            return pltpu.make_async_copy(block, taken.at[i % 2], sem.at[i % 2])

        fetch(first).start()

        def body(i, carry):
            @pl.when(i + 1 < last)
            def _():
                fetch(i + 1).start()

            fetch(i).wait()

            @pl.when(i >= first + 2)
            def _():
                put(i - 2).wait()

            for h in range(2):
                lanes = slice(h * 128, (h + 1) * 128)
                flat[h] = taken[i % 2, :, :, lanes].astype(jnp.float32).reshape(128 * 16, 128)
            rows = start(i // 4, 128)
            for m in range(16):
                make(
                    i,
                    m,
                    [
                        flat[h, pl.ds(m, 128, stride=16), :] * mask[rows, h * 128 : (h + 1) * 128]
                        for h in range(2)
                    ],
                )
            put(i).start()
            return carry

        lax.fori_loop(first, last, body, 0)
        put(last - 2).wait()
        put(last - 1).wait()

    def put_to(result):
        def put(i):
            place_at = result.at[:, start(i % 4, 512), start(i // 4, 128)]
            return pltpu.make_async_copy(made.at[i % 2], place_at, sem.at[2 + i % 2])

        return put

    def make_panel(i, m, halves):
        turned = jnp.concatenate([half.T.astype(jnp.bfloat16) for half in halves], 0)
        made[i % 2, :, m * 32 : (m + 1) * 32, :] = turned.reshape(8, 32, 128)

    def make_near(i, m, halves):
        block = jnp.concatenate([half.astype(jnp.bfloat16) for half in halves], 1)
        product = lax.dot_general(
            green[...], block, (((1,), (1,)), ((), ())), preferred_element_type=jnp.float32
        )
        made[i % 2, :, m * 32 : (m + 1) * 32, :] = product.astype(jnp.bfloat16).reshape(8, 32, 128)

    return (
        functools.partial(steps, panel, panel_mask, 16, make_panel, put_to(panel_t)),
        functools.partial(steps, near, near_mask, 8, make_near, put_to(dressed)),
    )


def screen_part(
    a_ref,
    b_ref,
    panel,
    near,
    panel_mask_ref,
    near_mask_ref,
    green_ref,
    out_ref,
    panel_t,
    dressed,
    ahead,
    a0,
    a1,
    b0,
    b1,
    a1_own,
    total,
    give,
    take,
    taken,
    flat,
    made,
    panel_blocks,
    near_blocks,
    panel_mask,
    near_mask,
    green,
    send_sem,
    own_sem,
    local_sem,
    x_sem,
    near_sem,
    far_sem,
    twin_sem,
    last_sem,
    step_sem,
    small_sem,
):
    row, col = lax.axis_index("row"), lax.axis_index("col")
    small = [
        pltpu.make_async_copy(panel_mask_ref, panel_blocks, small_sem.at[0]),
        pltpu.make_async_copy(near_mask_ref, near_blocks, small_sem.at[1]),
        pltpu.make_async_copy(green_ref, green, small_sem.at[2]),
    ]
    for copy in small:
        copy.start()

    def finish_masks():
        for copy in small:
            copy.wait()
        for blocks, mask, begin in (
            (panel_blocks, panel_mask, row * (panel_mask.shape[0] // RB)),
            (near_blocks, near_mask, col * (near_mask.shape[0] // RB)),
        ):
            count = mask.shape[0]
            shape = (count, blocks.shape[1])
            at = lax.broadcasted_iota(jnp.int32, shape, 0) // RB + begin
            pick = (at == lax.broadcasted_iota(jnp.int32, shape, 1)).astype(jnp.float32)
            shape = (blocks.shape[0], NL)
            wide = lax.broadcasted_iota(jnp.int32, shape, 1) // AB == lax.broadcasted_iota(jnp.int32, shape, 0)
            picked = lax.dot_general(
                pick, blocks[...].astype(jnp.float32), (((1,), (1,)), ((), ())), preferred_element_type=jnp.float32
            )
            mask[...] = jnp.dot(picked, wide.astype(jnp.float32), preferred_element_type=jnp.float32)

    panel_steps, near_steps = prepare(
        panel, near, panel_mask, near_mask, green, panel_t, dressed, taken, flat, made, step_sem
    )
    y, xh, z, xl, core = place()
    twin = device(y, xh, z, xl, 1 - core)
    rows, depth = a_ref.shape
    half, piece = rows // 2, rows // 4
    z_at = [lax.rem(z + d, 4) for d in range(4)]
    y_at = [lax.rem(y + d, 4) for d in range(4)]

    barrier = pltpu.get_barrier_semaphore()
    partners = [device(lax.rem(y + k // 2, 4), lax.rem(xh + k, 2), z, xl, core) for k in range(1, 8)]
    partners += [(row, lax.rem(col + k, 16)) for k in range(1, 16)]
    partners.append(device(y, 1 - xh, z, 1 - xl, core))
    for partner in partners:
        pl.semaphore_signal(barrier, inc=1, device_id=partner, device_id_type=MESH)
    pl.semaphore_wait(barrier, len(partners))

    copies = Copies(send_sem)

    own0, own1 = pl.ds(0, half), pl.ds(half, half)

    @pl.when(core == 0)
    def _():
        pltpu.make_async_copy(a_ref, a0.at[z], local_sem.at[0]).start()
        copy = pltpu.make_async_remote_copy(
            a_ref, a0.at[z], own_sem, local_sem.at[0], device_id=twin, device_id_type=MESH
        )
        copy.start()

    @pl.when(core == 1)
    def _():
        pltpu.make_async_copy(a_ref.at[own1], a1_own, local_sem.at[1]).start()
        copy = pltpu.make_async_remote_copy(
            a_ref.at[own0], a1_own, own_sem, local_sem.at[1], device_id=twin, device_id_type=MESH
        )
        copy.start()

    deep = (depth // 256 * 128 + 128, depth // 256 * 128)

    def b_slot(stream, k, p, part=None):
        buffer = b1.at[k] if stream == 0 else b0.at[k, stream - 1]
        start, count = p * deep[0], deep[p]
        if part is not None:
            start, count = start + part * (count // 2), count // 2
        return buffer.at[pl.ds(start, count)]

    def a_rows(stream, k, start, count):
        buffer = a0.at[k] if stream == 0 else a1.at[k, stream - 1]
        return buffer.at[pl.ds(start, count)]

    def a_slot(stream, k, p, part=None, of=core):
        start, count = of * half + p * piece, piece
        if part is not None:
            start, count = start + part * (count // 2), count // 2
        return a_rows(stream, k, pl.multiple_of(start, piece // 2), count)

    b_up = [device(y_at[1], xh, z, xl, core), device(y_at[3], xh, z, xl, core)]
    a_up = [device(y, xh, z_at[1], xl, core), device(y, xh, z_at[3], xl, core)]
    A, B = (a_slot, 0, z_at, a_up), (b_slot, 3, y_at, b_up)

    def b_own(p, base=0):
        return b_ref.at[pl.ds(base + p * deep[0], deep[p])]

    inner = xh != xl

    def b_along_x(p):
        def at(role):
            return b0.at[y, role, pl.ds(p * deep[0], deep[p])]

        for j in range(2):
            copies.send_if(inner, b_own(p), at(0), x_sem.at[1, 0, p], device(y, j, z, xh, core))

    def a_along_x(p):
        source = a1_own.at[pl.ds(p * piece, piece)]
        for j in range(2):
            copies.send_if(inner, source, a_slot(1, z, p), x_sem.at[0, 0, p], device(y, xl, z, j, core))

    outer = jnp.logical_not(inner)

    def a_outer_along_x(p):
        source = a1_own.at[pl.ds(p * piece, piece)]
        copies.send_if(outer, source, a_slot(2, z, p), x_sem.at[0, 1, p], device(y, xh, z, 1 - xl, core))

    def b_outer_along_x(p):
        copies.send_if(outer, b_own(p), b_slot(2, y, p), x_sem.at[1, 1, p], device(y, 1 - xh, z, xl, core))

    def outer_keep():
        for p in range(2):
            source = a1_own.at[pl.ds(p * piece, piece)]
            pltpu.make_async_copy(source, a_slot(2, z, p), x_sem.at[0, 1, p]).start()
            pltpu.make_async_copy(b_own(p), b_slot(2, y, p), x_sem.at[1, 1, p]).start()

    def spread(array, stream, p, source=None):
        slot, base, at, to = array
        for side in range(2):
            here = slot(stream, at[0], p)
            copies.send(here if source is None else source, here, near_sem.at[base + stream, side, p], to[side])

    def start_near(wanted, p, source):
        for side in range(2):
            copies.send_if(wanted, source, a_slot(0, z, p), near_sem.at[0, side, p], a_up[side])

    def to_twin(stream, k, p, index):
        here = a_slot(stream, k, p)
        copies.send(here, here, twin_sem.at[stream, index, p], twin)

    def go_on(array, stream, p):
        slot, base, at, to = array
        for side in range(2):
            k = at[3 - 2 * side]
            landed(slot(stream, k, p), near_sem.at[base + stream, side, p])
            half_of = slot(stream, k, p, side)
            copies.send(half_of, half_of, far_sem.at[base + stream, side, p], to[side])
        if base == 0:
            for side in range(2):
                to_twin(stream, at[3 - 2 * side], p, 3 - 2 * side)

    def far(array, stream, p):
        slot, base, at, to = array
        for side in range(2):
            landed(slot(stream, at[2], p, side), far_sem.at[base + stream, side, p])
        if base == 0:
            to_twin(stream, at[2], p, 2)

    def from_twin(stream, p, indices):
        for d in indices:
            landed(a_slot(stream, z_at[d], p, of=1 - core), twin_sem.at[stream, d, p])

    def arrive(s, p):
        landed(a_slot(s, z, p), x_sem.at[0, s - 1, p])
        spread(A, s, p)
        landed(b_slot(s, y, p), x_sem.at[1, s - 1, p])
        spread(B, s, p)
        to_twin(s, z, p, 0)

    def keep_rows(k, p, j):
        lanes = slice(p * deep[0], p * deep[0] + deep[p])

        def body(t, carry):
            at = pl.ds(pl.multiple_of(t * half, half), half)
            total[0, j, at] += jnp.dot(
                a0[k, at, lanes], b0[k, j, lanes], preferred_element_type=jnp.float32
            )
            return carry

        lax.fori_loop(0, 2, body, 0)

    def keep_cols(k, p, j):
        def body(t, carry):
            at = pl.ds(pl.multiple_of(t * half + p * piece, piece), piece)
            total[1, j, at] += jnp.dot(a1[k, j, at], b1[k], preferred_element_type=jnp.float32)
            return carry

        lax.fori_loop(0, 2, body, 0)

    for p in range(2):
        start_near(core == 0, p, a_ref.at[pl.ds(p * piece, piece)])
    b_along_x(0)
    for p in range(2):
        spread(B, 0, p, b_own(p, depth))
    landed(a1_own, local_sem.at[1])
    a_along_x(0)
    b_along_x(1)
    a_along_x(1)
    landed(a0.at[z], local_sem.at[0])
    for p in range(2):
        start_near(core == 1, p, a_slot(0, z, p))
    pl.when(outer)(outer_keep)
    b_local = pltpu.make_async_copy(b_ref.at[pl.ds(depth, depth)], b1.at[y], local_sem.at[2])
    b_local.start()
    total[...] = jnp.zeros_like(total)
    finish_masks()

    panel_steps(0, 4)
    go_on(B, 0, 0)
    go_on(A, 0, 0)
    panel_steps(4, 8)
    go_on(B, 0, 1)
    go_on(A, 0, 1)
    arrive(1, 0)
    for p in range(2):
        a_outer_along_x(p)
    panel_steps(8, 11)
    for p in range(2):
        far(B, 0, p)
        far(A, 0, p)
    arrive(1, 1)
    for p in range(2):
        b_outer_along_x(p)
    panel_steps(11, 14)
    go_on(A, 1, 0)
    go_on(B, 1, 0)
    panel_steps(14, 16)
    near_steps(0, 2)
    arrive(2, 0)
    go_on(A, 1, 1)
    go_on(B, 1, 1)
    near_steps(2, 4)
    for p in range(2):
        from_twin(0, p, (1, 2, 3))
    b_local.wait()

    def others(p):
        def step(d, carry):
            keep_rows(lax.rem(y + d, 4), p, 0)
            keep_cols(lax.rem(z + d, 4), p, 0)
            return carry

        lax.fori_loop(0, 4, step, 0)

    far(A, 1, 0)
    far(B, 1, 0)
    arrive(2, 1)
    near_steps(4, 8)
    from_twin(1, 0, (0, 1, 2, 3))
    others(0)
    far(A, 1, 1)
    far(B, 1, 1)
    go_on(A, 2, 0)
    go_on(B, 2, 0)
    from_twin(1, 1, (0, 1, 2, 3))
    others(1)
    for i in range(2):
        give[i] = total[i, 0].astype(jnp.bfloat16)
    copies.send(give.at[0], take.at[0], last_sem.at[0], device(y, xh, z, 1 - xl, core))
    copies.send(give.at[1], take.at[1], last_sem.at[1], device(y, 1 - xh, z, xl, core))
    from_twin(2, 0, (0, 1, 3))

    def own(p):
        def step(d):
            keep_rows(y_at[d], p, 1)
            keep_cols(z_at[d], p, 1)

        return step

    step = own(0)
    for d in (0, 1, 3):
        step(d)
    go_on(A, 2, 1)
    go_on(B, 2, 1)
    far(A, 2, 0)
    far(B, 2, 0)
    from_twin(2, 0, (2,))
    from_twin(2, 1, (0, 1, 3))
    step(2)
    step = own(1)
    for d in (0, 1, 3):
        step(d)
    ahead()
    far(B, 2, 1)
    keep_rows(y_at[2], 1, 1)
    far(A, 2, 1)
    landed(take.at[0], last_sem.at[0])
    landed(take.at[1], last_sem.at[1])
    total[0, 1] += total[1, 1] + take[0].astype(jnp.float32) + take[1].astype(jnp.float32)
    total[1, 1] = jnp.zeros_like(total[1, 1])
    from_twin(2, 1, (2,))
    keep_cols(z_at[2], 1, 1)
    out_ref[...] = (total[0, 1] + total[1, 1]).astype(jnp.bfloat16)

    def finish():
        copies.finish()

        @pl.when(core == 0)
        def _():
            pltpu.make_async_copy(a_ref, a0.at[z], own_sem).wait()

        @pl.when(core == 1)
        def _():
            pltpu.make_async_copy(a_ref.at[own0], a1_own, own_sem).wait()

    return finish


LATE = 1152


def contract_part(
    s_ref,
    panel_t,
    dressed,
    out_ref,
    energy_ref,
    block,
    part,
    far_y,
    near_y,
    cross_y,
    cross_x,
    far_x,
    near_x,
    total,
    other,
    dressed_b,
    tile,
    row_sum,
    tile_row,
    tile_col,
    send_sem,
    block_sem,
    far_sem,
    near_sem,
    cross_sem,
    row_sem,
    col_sem,
):
    y, xh, z, xl, core = place()
    col = (z * 2 + xl) * 2 + core
    f32, bf16 = jnp.float32, jnp.bfloat16

    def in_row(d, j):
        return device(lax.rem(y + d, 4), lax.rem(xh + j, 2), z, xl, core)

    def in_col(d):
        return (y * 2 + xh, lax.rem(col + d, 16))

    order = [(2, 1), (2, 0), (1, 1), (3, 1), (1, 0), (3, 0), (0, 1), (0, 0)]
    chunk = block.shape[1]

    def fetch(i):
        d, j = order[i // 2]
        share = lax.rem(y + d, 4) * 2 + lax.rem(xh + j, 2)
        return pltpu.make_async_copy(
            panel_t.at[share, pl.ds(i % 2 * chunk, chunk)], block.at[i % 2], block_sem.at[i % 2]
        )

    fetch(0).start()
    fetch(1).start()
    yield

    copies = Copies(send_sem)
    rows = TILE * 32
    early = rows - LATE
    h_late, h_early = LATE // 2, early // 2
    up, down, across = in_row(1, 0), in_row(3, 0), in_row(0, 1)

    def late(d, j, start=0, count=LATE):
        return part.at[d * 2 + j, pl.ds(start, count)]

    def first(d, j, start=0, count=early):
        return part.at[d * 2 + j, pl.ds(LATE + start, count)]

    for i, (d, j) in enumerate(order):
        for h in range(2):
            fetch(i * 2 + h).wait()

            def multiply(t, carry):
                at = pl.ds(pl.multiple_of(t * 256, 256), 256)
                to = pl.ds(pl.multiple_of(h * chunk + t * 256, 256), 256)
                part[d * 2 + j, to] = jnp.dot(
                    block[h, at], s_ref[...], preferred_element_type=f32
                ).astype(bf16)
                return carry

            lax.fori_loop(0, chunk // 256, multiply, 0)
            if i < 7:
                fetch(i * 2 + 2 + h).start()
        if j == 1:
            copies.send(first(d, 1), cross_x.at[d], cross_sem.at[d], across)
        if d == 2:
            copies.send(late(2, j, 0, h_late), far_y.at[j, 0], far_sem.at[j, 0], up)
            copies.send(late(2, j, h_late, h_late), far_y.at[j, 1], far_sem.at[j, 1], down)
        if d == 1:
            copies.send(late(1, j, h_late, h_late), near_y.at[j, 0, pl.ds(h_late, h_late)], near_sem.at[j, 0, 0], up)
        if d == 3:
            copies.send(late(3, j, 0, h_late), near_y.at[j, 1, pl.ds(0, h_late)], near_sem.at[j, 1, 0], down)

    def add(ref, *others):
        result = ref[...].astype(f32)
        for each in others:
            result = result + each[...].astype(f32)
        ref[...] = result.astype(bf16)

    def share(d, j):
        return lax.rem(y + d, 4) * 2 + lax.rem(xh + j, 2)

    turns = [(1, 1), (3, 1), (1, 0), (3, 0), (2, 0), (2, 1), (0, 1), (0, 0)]

    def fetch_dressed(i):
        return pltpu.make_async_copy(dressed.at[share(*turns[i])], dressed_b, block_sem.at[2])

    fetch_dressed(0).start()
    tile[...] = jnp.zeros_like(tile)

    def energy(i):
        d, j = turns[i]
        fetch_dressed(i).wait()
        for h in range(2):
            lanes = slice(h * 128, (h + 1) * 128)
            other[h] = dressed_b[:, lanes].astype(f32)
            total[h] = part[d * 2 + j, :, lanes].astype(f32)
        if i < 7:
            fetch_dressed(i + 1).start()

        def column(ref, l):
            halves = [ref[h, pl.ds(l, TILE, stride=32), :].astype(bf16) for h in range(2)]
            return jnp.concatenate(halves, 1)

        def body(k, carry):
            for l in range(4):
                carry = carry + lax.dot_general(
                    column(total, k * 4 + l),
                    column(other, k * 4 + l),
                    (((1,), (1,)), ((), ())),
                    preferred_element_type=f32,
                )
            return carry

        tile[:, :TILE] += lax.fori_loop(0, 8, body, jnp.zeros((TILE, TILE), f32))

    def forward_y(j):
        landed(far_y.at[j, 0], far_sem.at[j, 0])
        add(late(1, j, 0, h_late), far_y.at[j, 0])
        copies.send(late(1, j, 0, h_late), near_y.at[j, 0, pl.ds(0, h_late)], near_sem.at[j, 0, 1], up)
        landed(far_y.at[j, 1], far_sem.at[j, 1])
        add(late(3, j, h_late, h_late), far_y.at[j, 1])
        copies.send(late(3, j, h_late, h_late), near_y.at[j, 1, pl.ds(h_late, h_late)], near_sem.at[j, 1, 1], down)

    def both_near(j, ref):
        count = ref.shape[1] // 2
        for side in range(2):
            for turn in range(2):
                start = count if (side == 0) == (turn == 0) else 0
                landed(ref.at[side, pl.ds(start, count)], near_sem.at[j, side, turn])

    def share_of(row):
        return pl.ds(pl.multiple_of(row * 8, 8), 8)

    def settle(at, *terms):
        result = terms[0][...].astype(f32)
        for each in terms[1:]:
            result = result + each[...].astype(f32)
        out_ref[at] = result.astype(bf16)

    energy(0)
    energy(1)
    forward_y(1)
    energy(2)
    energy(3)
    forward_y(0)
    energy(4)
    landed(cross_x.at[2], cross_sem.at[2])
    add(first(2, 0), cross_x.at[2])
    copies.send(first(2, 0, 0, h_early), far_x.at[0], far_sem.at[2, 0], up)
    copies.send(first(2, 0, h_early, h_early), far_x.at[1], far_sem.at[2, 1], down)
    landed(cross_x.at[1], cross_sem.at[1])
    add(first(1, 0), cross_x.at[1])
    copies.send(first(1, 0, h_early, h_early), near_x.at[0, pl.ds(h_early, h_early)], near_sem.at[2, 0, 0], up)
    landed(cross_x.at[3], cross_sem.at[3])
    add(first(3, 0), cross_x.at[3])
    copies.send(first(3, 0, 0, h_early), near_x.at[1, pl.ds(0, h_early)], near_sem.at[2, 1, 0], down)
    energy(5)
    energy(6)

    both_near(1, near_y.at[1])
    add(late(0, 1), near_y.at[1, 0], near_y.at[1, 1])
    copies.send(late(0, 1), cross_y, cross_sem.at[4], across)

    landed(far_x.at[0], far_sem.at[2, 0])
    add(first(1, 0, 0, h_early), far_x.at[0])
    copies.send(first(1, 0, 0, h_early), near_x.at[0, pl.ds(0, h_early)], near_sem.at[2, 0, 1], up)
    landed(far_x.at[1], far_sem.at[2, 1])
    add(first(3, 0, h_early, h_early), far_x.at[1])
    copies.send(first(3, 0, h_early, h_early), near_x.at[1, pl.ds(h_early, h_early)], near_sem.at[2, 1, 1], down)

    energy(7)
    for s in range(1, 8):
        target = in_row(s // 2, s % 2)
        copies.send(tile.at[share_of(target[0])], tile_row.at[s], row_sem.at[s], target)
    mine = tile[share_of(y * 2 + xh)]
    for s in range(1, 8):
        landed(tile_row.at[s], row_sem.at[s])
        mine = mine + tile_row[s]
    row_sum[...] = mine
    for d in range(1, 16):
        copies.send(row_sum, tile_col.at[d], col_sem.at[d], in_col(d))

    both_near(0, near_y.at[0])
    landed(cross_x.at[0], cross_sem.at[0])
    landed(cross_y, cross_sem.at[4])
    settle(pl.ds(0, LATE), late(0, 0), near_y.at[0, 0], near_y.at[0, 1], cross_y)
    for d in range(1, 16):
        landed(tile_col.at[d], col_sem.at[d])
        mine = mine + tile_col[d]
    turned = pltpu.roll(-mine, lax.rem(128 - 4 * col, 128), 1).T
    energy_ref[...] = turned[:4]
    both_near(2, near_x)
    settle(pl.ds(LATE, early), first(0, 0), cross_x.at[0], near_x.at[0], near_x.at[1])
    copies.finish()


SCREEN_SCRATCH = 26


def kernel(*refs):
    inputs, (screened, contracted, energy, panel_t, dressed), scratch = refs[:7], refs[7:12], refs[12:]
    first, second = scratch[:SCREEN_SCRATCH], scratch[SCREEN_SCRATCH:]
    flat = first[9]
    steps = contract_part(screened, panel_t, dressed, contracted, energy, *second[:8], flat, *second[8:])
    finish = screen_part(*inputs, screened, panel_t, dressed, lambda: next(steps), *first)
    next(steps, None)
    finish()


def tile_terms(a, b, panel, near, panel_mask, near_mask, green):
    rows, depth = a.shape
    cols = b.shape[1]
    long = TILE * 32
    early = long - LATE
    bf16, f32 = jnp.bfloat16, jnp.float32
    dma = pltpu.SemaphoreType.DMA
    hbm, vmem = pl.BlockSpec(memory_space=pl.ANY), pl.BlockSpec(memory_space=pltpu.VMEM)
    first = [
        pltpu.VMEM((4, rows, depth), bf16),
        pltpu.VMEM((4, 2, rows, depth), bf16),
        pltpu.VMEM((4, 2, depth, cols), bf16),
        pltpu.VMEM((4, depth, cols), bf16),
        pltpu.VMEM((rows // 2, depth), bf16),
        pltpu.VMEM((2, 2, rows, cols), f32),
        pltpu.VMEM((2, rows, cols), bf16),
        pltpu.VMEM((2, rows, cols), bf16),
        pltpu.VMEM((2, 128, 16, NL), bf16),
        pltpu.VMEM((2, 128 * 16, 128), f32),
        pltpu.VMEM((2, 8, 16 * 32, 128), bf16),
        pltpu.VMEM(panel_mask.shape, jnp.int32),
        pltpu.VMEM(near_mask.shape, jnp.int32),
        pltpu.VMEM((rows, NL), f32),
        pltpu.VMEM((cols, NL), f32),
        pltpu.VMEM((NL, NL), bf16),
        dma((96,)),
        dma,
        dma((3,)),
        dma((2, 2, 2)),
        dma((6, 2, 2)),
        dma((6, 2, 2)),
        dma((3, 4, 2)),
        dma((2,)),
        dma((4,)),
        dma((3,)),
    ]
    second = [
        pltpu.VMEM((2, long // 2, rows), bf16),
        pltpu.VMEM((8, long, cols), bf16),
        pltpu.VMEM((2, 2, LATE // 2, cols), bf16),
        pltpu.VMEM((2, 2, LATE, cols), bf16),
        pltpu.VMEM((LATE, cols), bf16),
        pltpu.VMEM((4, early, cols), bf16),
        pltpu.VMEM((2, early // 2, cols), bf16),
        pltpu.VMEM((2, early, cols), bf16),
        pltpu.VMEM((2, long, 128), f32),
        pltpu.VMEM((long, cols), bf16),
        pltpu.VMEM((TILE, 128), f32),
        pltpu.VMEM((8, 128), f32),
        pltpu.VMEM((8, 8, 128), f32),
        pltpu.VMEM((16, 8, 128), f32),
        dma((48,)),
        dma((3,)),
        dma((3, 2)),
        dma((3, 2, 2)),
        dma((5,)),
        dma((8,)),
        dma((16,)),
    ]
    assert len(first) == SCREEN_SCRATCH
    return pl.pallas_call(
        kernel,
        out_shape=(
            jax.ShapeDtypeStruct((rows, cols), bf16),
            jax.ShapeDtypeStruct((long, cols), bf16),
            jax.ShapeDtypeStruct((4, 8), f32),
            jax.ShapeDtypeStruct((8, long, rows), bf16),
            jax.ShapeDtypeStruct((8, long, cols), bf16),
        ),
        in_specs=[hbm] * 7,
        out_specs=(vmem, vmem, vmem, hbm, hbm),
        scratch_shapes=first + second,
        compiler_params=pltpu.CompilerParams(
            collective_id=0, has_side_effects=True, vmem_limit_bytes=64 * 2**20 - 2**16
        ),
        name="tile_terms",
    )(a, b, panel, near, panel_mask, near_mask, green)


def hand_over_kernel(*refs):
    sources, results, held, sem = refs[:3], refs[3:6], refs[6:9], refs[9]
    pieces = []
    for k, source in enumerate(sources):
        count = 4 if k == 1 else 1
        size = source.shape[0] // count
        pieces += [(k, pl.ds(i * size, size)) for i in range(count)]
    taken = [pltpu.make_async_copy(sources[k].at[at], held[k].at[at], sem.at[0, i]) for i, (k, at) in enumerate(pieces)]
    given = [pltpu.make_async_copy(held[k].at[at], results[k].at[at], sem.at[1, i]) for i, (k, at) in enumerate(pieces)]
    for copy in taken:
        copy.start()
    for i, copy in enumerate(given):
        taken[i].wait()
        copy.start()
    for copy in given:
        copy.wait()


def hand_over(*arrays):
    hbm = pl.BlockSpec(memory_space=pl.ANY)
    return pl.pallas_call(
        hand_over_kernel,
        out_shape=tuple(jax.ShapeDtypeStruct(array.shape, array.dtype) for array in arrays),
        in_specs=[hbm] * 3,
        out_specs=(hbm,) * 3,
        scratch_shapes=[pltpu.VMEM(array.shape, array.dtype) for array in arrays]
        + [pltpu.SemaphoreType.DMA((2, 6))],
        name="hand_over",
    )(*arrays)


def per_device(
    polarization, metric, three_panel, three_near, green_function, mask_panel, mask_near
):
    near_cols = metric.shape[1]
    screened, contracted, energy, *_ = tile_terms(
        polarization, metric, three_panel, three_near, mask_panel.T, mask_near.T, green_function
    )
    screened, contracted, energy = hand_over(screened, contracted, energy)
    return screened, contracted.T.reshape(near_cols, TILE, contracted.shape[0] // TILE), energy.T


def solution(mesh):
    placed = (
        P("row", "col"),
        P("row", "col"),
        P("row", None, None),
        P("col", None, None),
        P(),
        P(),
        P(),
    )
    return jax.shard_map(
        per_device,
        mesh=mesh,
        in_specs=placed,
        out_specs=(P("row", "col"), P("col", None, "row"), P("row", "col")),
        check_vma=False,
    )
```

```python
import functools

import jax
import jax.numpy as jnp
from jax import lax
from jax.experimental import pallas as pl
from jax.experimental.pallas import tpu as pltpu
from jax.sharding import PartitionSpec as P

TILE = 64
NL = 256
RB = 64
AB = 32
MESH = pl.DeviceIdType.MESH


def place():
    row, col = lax.axis_index("row"), lax.axis_index("col")
    return row // 2, row % 2, col // 4, (col // 2) % 2, col % 2


def device(y, xh, z, xl, core):
    return (y * 2 + xh, (z * 2 + xl) * 2 + core)


class Copies:
    def __init__(self, send_sem):
        self.send_sem, self.started = send_sem, []

    def send(self, src, dst, recv_sem, target):
        index = len(self.started)
        copy = pltpu.make_async_remote_copy(
            src_ref=src,
            dst_ref=dst,
            send_sem=self.send_sem.at[index],
            recv_sem=recv_sem,
            device_id=target,
            device_id_type=MESH,
        )
        copy.start()
        self.started.append((copy, None))

    def send_if(self, wanted, src, dst, recv_sem, target):
        index = len(self.started)
        copy = pltpu.make_async_remote_copy(
            src_ref=src,
            dst_ref=dst,
            send_sem=self.send_sem.at[index],
            recv_sem=recv_sem,
            device_id=target,
            device_id_type=MESH,
        )
        pl.when(wanted)(copy.start)
        self.started.append((copy, wanted))

    def finish(self):
        for copy, wanted in self.started:
            if wanted is None:
                copy.wait_send()
            else:
                pl.when(wanted)(copy.wait_send)


def landed(ref, sem):
    pltpu.make_async_copy(ref, ref, sem).wait()


def prepare(panel, near, panel_mask, near_mask, green, panel_t, dressed, taken, flat, made, sem):
    start = lambda k, size: pl.ds(pl.multiple_of(k * size, size), size)

    def steps(source, mask, count, make, put, first, last):
        def fetch(i):
            block = source.at[start(i // 4, 128), start(i % 4, 16)]
            return pltpu.make_async_copy(block, taken.at[i % 2], sem.at[i % 2])

        fetch(first).start()

        def body(i, carry):
            @pl.when(i + 1 < last)
            def _():
                fetch(i + 1).start()

            fetch(i).wait()

            @pl.when(i >= first + 2)
            def _():
                put(i - 2).wait()

            for h in range(2):
                lanes = slice(h * 128, (h + 1) * 128)
                flat[h] = taken[i % 2, :, :, lanes].astype(jnp.float32).reshape(128 * 16, 128)
            rows = start(i // 4, 128)
            for m in range(16):
                make(
                    i,
                    m,
                    [
                        flat[h, pl.ds(m, 128, stride=16), :] * mask[rows, h * 128 : (h + 1) * 128]
                        for h in range(2)
                    ],
                )
            put(i).start()
            return carry

        lax.fori_loop(first, last, body, 0)
        put(last - 2).wait()
        put(last - 1).wait()

    def put_to(result):
        def put(i):
            place_at = result.at[:, start(i % 4, 512), start(i // 4, 128)]
            return pltpu.make_async_copy(made.at[i % 2], place_at, sem.at[2 + i % 2])

        return put

    def make_panel(i, m, halves):
        turned = jnp.concatenate([half.T.astype(jnp.bfloat16) for half in halves], 0)
        made[i % 2, :, m * 32 : (m + 1) * 32, :] = turned.reshape(8, 32, 128)

    def make_near(i, m, halves):
        block = jnp.concatenate([half.astype(jnp.bfloat16) for half in halves], 1)
        product = lax.dot_general(
            green[...], block, (((1,), (1,)), ((), ())), preferred_element_type=jnp.float32
        )
        made[i % 2, :, m * 32 : (m + 1) * 32, :] = product.astype(jnp.bfloat16).reshape(8, 32, 128)

    return (
        functools.partial(steps, panel, panel_mask, 16, make_panel, put_to(panel_t)),
        functools.partial(steps, near, near_mask, 8, make_near, put_to(dressed)),
    )


def screen_part(
    a_ref,
    b_ref,
    panel,
    near,
    panel_mask_ref,
    near_mask_ref,
    green_ref,
    out_ref,
    panel_t,
    dressed,
    ahead,
    a0,
    a1,
    b0,
    b1,
    a1_own,
    total,
    give,
    take,
    taken,
    flat,
    made,
    panel_blocks,
    near_blocks,
    panel_mask,
    near_mask,
    green,
    send_sem,
    own_sem,
    local_sem,
    x_sem,
    near_sem,
    far_sem,
    twin_sem,
    last_sem,
    step_sem,
    small_sem,
):
    row, col = lax.axis_index("row"), lax.axis_index("col")
    small = [
        pltpu.make_async_copy(panel_mask_ref, panel_blocks, small_sem.at[0]),
        pltpu.make_async_copy(near_mask_ref, near_blocks, small_sem.at[1]),
        pltpu.make_async_copy(green_ref, green, small_sem.at[2]),
    ]
    for copy in small:
        copy.start()

    def finish_masks():
        for copy in small:
            copy.wait()
        for blocks, mask, begin in (
            (panel_blocks, panel_mask, row * (panel_mask.shape[0] // RB)),
            (near_blocks, near_mask, col * (near_mask.shape[0] // RB)),
        ):
            count = mask.shape[0]
            shape = (count, blocks.shape[1])
            at = lax.broadcasted_iota(jnp.int32, shape, 0) // RB + begin
            pick = (at == lax.broadcasted_iota(jnp.int32, shape, 1)).astype(jnp.float32)
            shape = (blocks.shape[0], NL)
            wide = lax.broadcasted_iota(jnp.int32, shape, 1) // AB == lax.broadcasted_iota(jnp.int32, shape, 0)
            picked = lax.dot_general(
                pick, blocks[...].astype(jnp.float32), (((1,), (1,)), ((), ())), preferred_element_type=jnp.float32
            )
            mask[...] = jnp.dot(picked, wide.astype(jnp.float32), preferred_element_type=jnp.float32)

    panel_steps, near_steps = prepare(
        panel, near, panel_mask, near_mask, green, panel_t, dressed, taken, flat, made, step_sem
    )
    y, xh, z, xl, core = place()
    twin = device(y, xh, z, xl, 1 - core)
    rows, depth = a_ref.shape
    half, piece = rows // 2, rows // 4
    z_at = [lax.rem(z + d, 4) for d in range(4)]
    y_at = [lax.rem(y + d, 4) for d in range(4)]

    barrier = pltpu.get_barrier_semaphore()
    partners = [device(lax.rem(y + k // 2, 4), lax.rem(xh + k, 2), z, xl, core) for k in range(1, 8)]
    partners += [(row, lax.rem(col + k, 16)) for k in range(1, 16)]
    partners.append(device(y, 1 - xh, z, 1 - xl, core))
    for partner in partners:
        pl.semaphore_signal(barrier, inc=1, device_id=partner, device_id_type=MESH)
    pl.semaphore_wait(barrier, len(partners))

    copies = Copies(send_sem)

    own0, own1 = pl.ds(0, half), pl.ds(half, half)

    @pl.when(core == 0)
    def _():
        pltpu.make_async_copy(a_ref, a0.at[z], local_sem.at[0]).start()
        copy = pltpu.make_async_remote_copy(
            a_ref, a0.at[z], own_sem, local_sem.at[0], device_id=twin, device_id_type=MESH
        )
        copy.start()

    @pl.when(core == 1)
    def _():
        pltpu.make_async_copy(a_ref.at[own1], a1_own, local_sem.at[1]).start()
        copy = pltpu.make_async_remote_copy(
            a_ref.at[own0], a1_own, own_sem, local_sem.at[1], device_id=twin, device_id_type=MESH
        )
        copy.start()

    deep = (depth // 256 * 128 + 128, depth // 256 * 128)

    def b_slot(stream, k, p, part=None):
        buffer = b1.at[k] if stream == 0 else b0.at[k, stream - 1]
        start, count = p * deep[0], deep[p]
        if part is not None:
            start, count = start + part * (count // 2), count // 2
        return buffer.at[pl.ds(start, count)]

    def a_rows(stream, k, start, count):
        buffer = a0.at[k] if stream == 0 else a1.at[k, stream - 1]
        return buffer.at[pl.ds(start, count)]

    def a_slot(stream, k, p, part=None, of=core):
        start, count = of * half + p * piece, piece
        if part is not None:
            start, count = start + part * (count // 2), count // 2
        return a_rows(stream, k, pl.multiple_of(start, piece // 2), count)

    b_up = [device(y_at[1], xh, z, xl, core), device(y_at[3], xh, z, xl, core)]
    a_up = [device(y, xh, z_at[1], xl, core), device(y, xh, z_at[3], xl, core)]
    A, B = (a_slot, 0, z_at, a_up), (b_slot, 3, y_at, b_up)

    def b_own(p, base=0):
        return b_ref.at[pl.ds(base + p * deep[0], deep[p])]

    inner = xh != xl

    def b_along_x(p):
        def at(role):
            return b0.at[y, role, pl.ds(p * deep[0], deep[p])]

        for j in range(2):
            copies.send_if(inner, b_own(p), at(0), x_sem.at[1, 0, p], device(y, j, z, xh, core))

    def a_along_x(p):
        source = a1_own.at[pl.ds(p * piece, piece)]
        for j in range(2):
            copies.send_if(inner, source, a_slot(1, z, p), x_sem.at[0, 0, p], device(y, xl, z, j, core))

    outer = jnp.logical_not(inner)

    def a_outer_along_x(p):
        source = a1_own.at[pl.ds(p * piece, piece)]
        copies.send_if(outer, source, a_slot(2, z, p), x_sem.at[0, 1, p], device(y, xh, z, 1 - xl, core))

    def b_outer_along_x(p):
        copies.send_if(outer, b_own(p), b_slot(2, y, p), x_sem.at[1, 1, p], device(y, 1 - xh, z, xl, core))

    def outer_keep():
        for p in range(2):
            source = a1_own.at[pl.ds(p * piece, piece)]
            pltpu.make_async_copy(source, a_slot(2, z, p), x_sem.at[0, 1, p]).start()
            pltpu.make_async_copy(b_own(p), b_slot(2, y, p), x_sem.at[1, 1, p]).start()

    def spread(array, stream, p, source=None):
        slot, base, at, to = array
        for side in range(2):
            here = slot(stream, at[0], p)
            copies.send(here if source is None else source, here, near_sem.at[base + stream, side, p], to[side])

    def start_near(wanted, p, source):
        for side in range(2):
            copies.send_if(wanted, source, a_slot(0, z, p), near_sem.at[0, side, p], a_up[side])

    def to_twin(stream, k, p, index):
        here = a_slot(stream, k, p)
        copies.send(here, here, twin_sem.at[stream, index, p], twin)

    def go_on(array, stream, p):
        slot, base, at, to = array
        for side in range(2):
            k = at[3 - 2 * side]
            landed(slot(stream, k, p), near_sem.at[base + stream, side, p])
            half_of = slot(stream, k, p, side)
            copies.send(half_of, half_of, far_sem.at[base + stream, side, p], to[side])
        if base == 0:
            for side in range(2):
                to_twin(stream, at[3 - 2 * side], p, 3 - 2 * side)

    def far(array, stream, p):
        slot, base, at, to = array
        for side in range(2):
            landed(slot(stream, at[2], p, side), far_sem.at[base + stream, side, p])
        if base == 0:
            to_twin(stream, at[2], p, 2)

    def from_twin(stream, p, indices):
        for d in indices:
            landed(a_slot(stream, z_at[d], p, of=1 - core), twin_sem.at[stream, d, p])

    def arrive(s, p):
        landed(a_slot(s, z, p), x_sem.at[0, s - 1, p])
        spread(A, s, p)
        landed(b_slot(s, y, p), x_sem.at[1, s - 1, p])
        spread(B, s, p)
        to_twin(s, z, p, 0)

    def keep_rows(k, p, j):
        lanes = slice(p * deep[0], p * deep[0] + deep[p])

        def body(t, carry):
            at = pl.ds(pl.multiple_of(t * half, half), half)
            total[0, j, at] += jnp.dot(
                a0[k, at, lanes], b0[k, j, lanes], preferred_element_type=jnp.float32
            )
            return carry

        lax.fori_loop(0, 2, body, 0)

    def keep_cols(k, p, j):
        def body(t, carry):
            at = pl.ds(pl.multiple_of(t * half + p * piece, piece), piece)
            total[1, j, at] += jnp.dot(a1[k, j, at], b1[k], preferred_element_type=jnp.float32)
            return carry

        lax.fori_loop(0, 2, body, 0)

    for p in range(2):
        start_near(core == 0, p, a_ref.at[pl.ds(p * piece, piece)])
    b_along_x(0)
    for p in range(2):
        spread(B, 0, p, b_own(p, depth))
    landed(a1_own, local_sem.at[1])
    a_along_x(0)
    b_along_x(1)
    a_along_x(1)
    landed(a0.at[z], local_sem.at[0])
    for p in range(2):
        start_near(core == 1, p, a_slot(0, z, p))
    pl.when(outer)(outer_keep)
    b_local = pltpu.make_async_copy(b_ref.at[pl.ds(depth, depth)], b1.at[y], local_sem.at[2])
    b_local.start()
    total[...] = jnp.zeros_like(total)
    finish_masks()

    panel_steps(0, 6)
    for p in range(2):
        a_outer_along_x(p)
    go_on(B, 0, 0)
    go_on(A, 0, 0)
    panel_steps(6, 12)
    go_on(B, 0, 1)
    go_on(A, 0, 1)
    arrive(1, 0)
    panel_steps(12, 16)
    near_steps(0, 4)
    for p in range(2):
        far(B, 0, p)
        far(A, 0, p)
    arrive(1, 1)
    for p in range(2):
        b_outer_along_x(p)
    go_on(A, 1, 0)
    go_on(B, 1, 0)
    near_steps(4, 8)
    go_on(A, 1, 1)
    go_on(B, 1, 1)
    arrive(2, 0)
    for p in range(2):
        from_twin(0, p, (1, 2, 3))
    b_local.wait()

    def others(p):
        def step(d, carry):
            keep_rows(lax.rem(y + d, 4), p, 0)
            keep_cols(lax.rem(z + d, 4), p, 0)
            return carry

        lax.fori_loop(0, 4, step, 0)

    far(A, 1, 0)
    far(B, 1, 0)
    from_twin(1, 0, (0, 1, 2, 3))
    others(0)
    arrive(2, 1)
    far(A, 1, 1)
    far(B, 1, 1)
    go_on(A, 2, 0)
    go_on(B, 2, 0)
    from_twin(1, 1, (0, 1, 2, 3))
    others(1)
    for i in range(2):
        give[i] = total[i, 0].astype(jnp.bfloat16)
    copies.send(give.at[0], take.at[0], last_sem.at[0], device(y, xh, z, 1 - xl, core))
    copies.send(give.at[1], take.at[1], last_sem.at[1], device(y, 1 - xh, z, xl, core))
    from_twin(2, 0, (0, 1, 3))

    def own(p):
        def step(d):
            keep_rows(y_at[d], p, 1)
            keep_cols(z_at[d], p, 1)

        return step

    step = own(0)
    for d in (0, 1, 3):
        step(d)
    go_on(A, 2, 1)
    go_on(B, 2, 1)
    far(A, 2, 0)
    far(B, 2, 0)
    from_twin(2, 0, (2,))
    from_twin(2, 1, (0, 1, 3))
    step(2)
    step = own(1)
    for d in (0, 1, 3):
        step(d)
    ahead()
    far(B, 2, 1)
    keep_rows(y_at[2], 1, 1)
    far(A, 2, 1)
    landed(take.at[0], last_sem.at[0])
    landed(take.at[1], last_sem.at[1])
    total[0, 1] += total[1, 1] + take[0].astype(jnp.float32) + take[1].astype(jnp.float32)
    total[1, 1] = jnp.zeros_like(total[1, 1])
    from_twin(2, 1, (2,))
    keep_cols(z_at[2], 1, 1)
    out_ref[...] = (total[0, 1] + total[1, 1]).astype(jnp.bfloat16)

    def finish():
        copies.finish()

        @pl.when(core == 0)
        def _():
            pltpu.make_async_copy(a_ref, a0.at[z], own_sem).wait()

        @pl.when(core == 1)
        def _():
            pltpu.make_async_copy(a_ref.at[own0], a1_own, own_sem).wait()

    return finish


LATE = 1152


def contract_part(
    s_ref,
    panel_t,
    dressed,
    out_ref,
    energy_ref,
    block,
    part,
    far_y,
    near_y,
    cross_y,
    cross_x,
    far_x,
    near_x,
    total,
    other,
    dressed_b,
    tile,
    row_sum,
    tile_row,
    tile_col,
    send_sem,
    block_sem,
    far_sem,
    near_sem,
    cross_sem,
    row_sem,
    col_sem,
):
    y, xh, z, xl, core = place()
    col = (z * 2 + xl) * 2 + core
    f32, bf16 = jnp.float32, jnp.bfloat16

    def in_row(d, j):
        return device(lax.rem(y + d, 4), lax.rem(xh + j, 2), z, xl, core)

    def in_col(d):
        return (y * 2 + xh, lax.rem(col + d, 16))

    order = [(2, 1), (2, 0), (1, 1), (3, 1), (1, 0), (3, 0), (0, 1), (0, 0)]
    chunk = block.shape[1]

    def fetch(i):
        d, j = order[i // 2]
        share = lax.rem(y + d, 4) * 2 + lax.rem(xh + j, 2)
        return pltpu.make_async_copy(
            panel_t.at[share, pl.ds(i % 2 * chunk, chunk)], block.at[i % 2], block_sem.at[i % 2]
        )

    fetch(0).start()
    fetch(1).start()
    yield

    copies = Copies(send_sem)
    rows = TILE * 32
    early = rows - LATE
    h_late, h_early = LATE // 2, early // 2
    up, down, across = in_row(1, 0), in_row(3, 0), in_row(0, 1)

    def late(d, j, start=0, count=LATE):
        return part.at[d * 2 + j, pl.ds(start, count)]

    def first(d, j, start=0, count=early):
        return part.at[d * 2 + j, pl.ds(LATE + start, count)]

    for i, (d, j) in enumerate(order):
        for h in range(2):
            fetch(i * 2 + h).wait()

            def multiply(t, carry):
                at = pl.ds(pl.multiple_of(t * 256, 256), 256)
                to = pl.ds(pl.multiple_of(h * chunk + t * 256, 256), 256)
                part[d * 2 + j, to] = jnp.dot(
                    block[h, at], s_ref[...], preferred_element_type=f32
                ).astype(bf16)
                return carry

            lax.fori_loop(0, chunk // 256, multiply, 0)
            if i < 7:
                fetch(i * 2 + 2 + h).start()
        if j == 1:
            copies.send(first(d, 1), cross_x.at[d], cross_sem.at[d], across)
        if d == 2:
            copies.send(late(2, j, 0, h_late), far_y.at[j, 0], far_sem.at[j, 0], up)
            copies.send(late(2, j, h_late, h_late), far_y.at[j, 1], far_sem.at[j, 1], down)
        if d == 1:
            copies.send(late(1, j, h_late, h_late), near_y.at[j, 0, pl.ds(h_late, h_late)], near_sem.at[j, 0, 0], up)
        if d == 3:
            copies.send(late(3, j, 0, h_late), near_y.at[j, 1, pl.ds(0, h_late)], near_sem.at[j, 1, 0], down)

    def add(ref, *others):
        result = ref[...].astype(f32)
        for each in others:
            result = result + each[...].astype(f32)
        ref[...] = result.astype(bf16)

    def share(d, j):
        return lax.rem(y + d, 4) * 2 + lax.rem(xh + j, 2)

    turns = [(1, 1), (3, 1), (1, 0), (3, 0), (2, 0), (2, 1), (0, 1), (0, 0)]

    def fetch_dressed(i):
        return pltpu.make_async_copy(dressed.at[share(*turns[i])], dressed_b, block_sem.at[2])

    fetch_dressed(0).start()
    tile[...] = jnp.zeros_like(tile)

    def energy(i):
        d, j = turns[i]
        fetch_dressed(i).wait()
        for h in range(2):
            lanes = slice(h * 128, (h + 1) * 128)
            other[h] = dressed_b[:, lanes].astype(f32)
            total[h] = part[d * 2 + j, :, lanes].astype(f32)
        if i < 7:
            fetch_dressed(i + 1).start()

        def column(ref, l):
            halves = [ref[h, pl.ds(l, TILE, stride=32), :].astype(bf16) for h in range(2)]
            return jnp.concatenate(halves, 1)

        def body(k, carry):
            for l in range(4):
                carry = carry + lax.dot_general(
                    column(total, k * 4 + l),
                    column(other, k * 4 + l),
                    (((1,), (1,)), ((), ())),
                    preferred_element_type=f32,
                )
            return carry

        tile[:, :TILE] += lax.fori_loop(0, 8, body, jnp.zeros((TILE, TILE), f32))

    def forward_y(j):
        landed(far_y.at[j, 0], far_sem.at[j, 0])
        add(late(1, j, 0, h_late), far_y.at[j, 0])
        copies.send(late(1, j, 0, h_late), near_y.at[j, 0, pl.ds(0, h_late)], near_sem.at[j, 0, 1], up)
        landed(far_y.at[j, 1], far_sem.at[j, 1])
        add(late(3, j, h_late, h_late), far_y.at[j, 1])
        copies.send(late(3, j, h_late, h_late), near_y.at[j, 1, pl.ds(h_late, h_late)], near_sem.at[j, 1, 1], down)

    def both_near(j, ref):
        count = ref.shape[1] // 2
        for side in range(2):
            for turn in range(2):
                start = count if (side == 0) == (turn == 0) else 0
                landed(ref.at[side, pl.ds(start, count)], near_sem.at[j, side, turn])

    def share_of(row):
        return pl.ds(pl.multiple_of(row * 8, 8), 8)

    def settle(at, *terms):
        result = terms[0][...].astype(f32)
        for each in terms[1:]:
            result = result + each[...].astype(f32)
        out_ref[at] = result.astype(bf16)

    energy(0)
    energy(1)
    forward_y(1)
    energy(2)
    energy(3)
    forward_y(0)
    energy(4)
    landed(cross_x.at[2], cross_sem.at[2])
    add(first(2, 0), cross_x.at[2])
    copies.send(first(2, 0, 0, h_early), far_x.at[0], far_sem.at[2, 0], up)
    copies.send(first(2, 0, h_early, h_early), far_x.at[1], far_sem.at[2, 1], down)
    landed(cross_x.at[1], cross_sem.at[1])
    add(first(1, 0), cross_x.at[1])
    copies.send(first(1, 0, h_early, h_early), near_x.at[0, pl.ds(h_early, h_early)], near_sem.at[2, 0, 0], up)
    landed(cross_x.at[3], cross_sem.at[3])
    add(first(3, 0), cross_x.at[3])
    copies.send(first(3, 0, 0, h_early), near_x.at[1, pl.ds(0, h_early)], near_sem.at[2, 1, 0], down)
    energy(5)
    energy(6)

    both_near(1, near_y.at[1])
    add(late(0, 1), near_y.at[1, 0], near_y.at[1, 1])
    copies.send(late(0, 1), cross_y, cross_sem.at[4], across)

    landed(far_x.at[0], far_sem.at[2, 0])
    add(first(1, 0, 0, h_early), far_x.at[0])
    copies.send(first(1, 0, 0, h_early), near_x.at[0, pl.ds(0, h_early)], near_sem.at[2, 0, 1], up)
    landed(far_x.at[1], far_sem.at[2, 1])
    add(first(3, 0, h_early, h_early), far_x.at[1])
    copies.send(first(3, 0, h_early, h_early), near_x.at[1, pl.ds(h_early, h_early)], near_sem.at[2, 1, 1], down)

    energy(7)
    for s in range(1, 8):
        target = in_row(s // 2, s % 2)
        copies.send(tile.at[share_of(target[0])], tile_row.at[s], row_sem.at[s], target)
    mine = tile[share_of(y * 2 + xh)]
    for s in range(1, 8):
        landed(tile_row.at[s], row_sem.at[s])
        mine = mine + tile_row[s]
    row_sum[...] = mine
    for d in range(1, 16):
        copies.send(row_sum, tile_col.at[d], col_sem.at[d], in_col(d))

    both_near(0, near_y.at[0])
    for h in range(2):
        lanes = slice(h * 128, (h + 1) * 128)
        total[h, :LATE] = (
            part[0, :LATE, lanes].astype(f32) + near_y[0, 0, :, lanes].astype(f32) + near_y[0, 1, :, lanes].astype(f32)
        )
    for d in range(1, 16):
        landed(tile_col.at[d], col_sem.at[d])
        mine = mine + tile_col[d]
    turned = pltpu.roll(-mine, lax.rem(128 - 4 * col, 128), 1).T
    energy_ref[...] = turned[:4]
    landed(cross_x.at[0], cross_sem.at[0])
    both_near(2, near_x)
    settle(pl.ds(LATE, early), first(0, 0), cross_x.at[0], near_x.at[0], near_x.at[1])
    landed(cross_y, cross_sem.at[4])
    for h in range(2):
        lanes = slice(h * 128, (h + 1) * 128)
        out_ref[:LATE, lanes] = (total[h, :LATE] + cross_y[:, lanes].astype(f32)).astype(bf16)
    copies.finish()


SCREEN_SCRATCH = 26


def kernel(*refs):
    inputs, (screened, contracted, energy, panel_t, dressed), scratch = refs[:7], refs[7:12], refs[12:]
    first, second = scratch[:SCREEN_SCRATCH], scratch[SCREEN_SCRATCH:]
    flat = first[9]
    steps = contract_part(screened, panel_t, dressed, contracted, energy, *second[:8], flat, *second[8:])
    finish = screen_part(*inputs, screened, panel_t, dressed, lambda: next(steps), *first)
    next(steps, None)
    finish()


def tile_terms(a, b, panel, near, panel_mask, near_mask, green):
    rows, depth = a.shape
    cols = b.shape[1]
    long = TILE * 32
    early = long - LATE
    bf16, f32 = jnp.bfloat16, jnp.float32
    dma = pltpu.SemaphoreType.DMA
    hbm, vmem = pl.BlockSpec(memory_space=pl.ANY), pl.BlockSpec(memory_space=pltpu.VMEM)
    first = [
        pltpu.VMEM((4, rows, depth), bf16),
        pltpu.VMEM((4, 2, rows, depth), bf16),
        pltpu.VMEM((4, 2, depth, cols), bf16),
        pltpu.VMEM((4, depth, cols), bf16),
        pltpu.VMEM((rows // 2, depth), bf16),
        pltpu.VMEM((2, 2, rows, cols), f32),
        pltpu.VMEM((2, rows, cols), bf16),
        pltpu.VMEM((2, rows, cols), bf16),
        pltpu.VMEM((2, 128, 16, NL), bf16),
        pltpu.VMEM((2, 128 * 16, 128), f32),
        pltpu.VMEM((2, 8, 16 * 32, 128), bf16),
        pltpu.VMEM(panel_mask.shape, jnp.int32),
        pltpu.VMEM(near_mask.shape, jnp.int32),
        pltpu.VMEM((rows, NL), f32),
        pltpu.VMEM((cols, NL), f32),
        pltpu.VMEM((NL, NL), bf16),
        dma((96,)),
        dma,
        dma((3,)),
        dma((2, 2, 2)),
        dma((6, 2, 2)),
        dma((6, 2, 2)),
        dma((3, 4, 2)),
        dma((2,)),
        dma((4,)),
        dma((3,)),
    ]
    second = [
        pltpu.VMEM((2, long // 2, rows), bf16),
        pltpu.VMEM((8, long, cols), bf16),
        pltpu.VMEM((2, 2, LATE // 2, cols), bf16),
        pltpu.VMEM((2, 2, LATE, cols), bf16),
        pltpu.VMEM((LATE, cols), bf16),
        pltpu.VMEM((4, early, cols), bf16),
        pltpu.VMEM((2, early // 2, cols), bf16),
        pltpu.VMEM((2, early, cols), bf16),
        pltpu.VMEM((2, long, 128), f32),
        pltpu.VMEM((long, cols), bf16),
        pltpu.VMEM((TILE, 128), f32),
        pltpu.VMEM((8, 128), f32),
        pltpu.VMEM((8, 8, 128), f32),
        pltpu.VMEM((16, 8, 128), f32),
        dma((48,)),
        dma((3,)),
        dma((3, 2)),
        dma((3, 2, 2)),
        dma((5,)),
        dma((8,)),
        dma((16,)),
    ]
    assert len(first) == SCREEN_SCRATCH
    return pl.pallas_call(
        kernel,
        out_shape=(
            jax.ShapeDtypeStruct((rows, cols), bf16),
            jax.ShapeDtypeStruct((long, cols), bf16),
            jax.ShapeDtypeStruct((4, 8), f32),
            jax.ShapeDtypeStruct((8, long, rows), bf16),
            jax.ShapeDtypeStruct((8, long, cols), bf16),
        ),
        in_specs=[hbm] * 7,
        out_specs=(vmem, vmem, vmem, hbm, hbm),
        scratch_shapes=first + second,
        compiler_params=pltpu.CompilerParams(
            collective_id=0, has_side_effects=True, vmem_limit_bytes=64 * 2**20 - 2**16
        ),
        name="tile_terms",
    )(a, b, panel, near, panel_mask, near_mask, green)


def hand_over_kernel(*refs):
    sources, results, held, sem = refs[:3], refs[3:6], refs[6:9], refs[9]
    pieces = []
    for k, source in enumerate(sources):
        count = 4 if k == 1 else 1
        size = source.shape[0] // count
        pieces += [(k, pl.ds(i * size, size)) for i in range(count)]
    taken = [pltpu.make_async_copy(sources[k].at[at], held[k].at[at], sem.at[0, i]) for i, (k, at) in enumerate(pieces)]
    given = [pltpu.make_async_copy(held[k].at[at], results[k].at[at], sem.at[1, i]) for i, (k, at) in enumerate(pieces)]
    for copy in taken:
        copy.start()
    for i, copy in enumerate(given):
        taken[i].wait()
        copy.start()
    for copy in given:
        copy.wait()


def hand_over(*arrays):
    hbm = pl.BlockSpec(memory_space=pl.ANY)
    return pl.pallas_call(
        hand_over_kernel,
        out_shape=tuple(jax.ShapeDtypeStruct(array.shape, array.dtype) for array in arrays),
        in_specs=[hbm] * 3,
        out_specs=(hbm,) * 3,
        scratch_shapes=[pltpu.VMEM(array.shape, array.dtype) for array in arrays]
        + [pltpu.SemaphoreType.DMA((2, 6))],
        name="hand_over",
    )(*arrays)


def per_device(
    polarization, metric, three_panel, three_near, green_function, mask_panel, mask_near
):
    near_cols = metric.shape[1]
    screened, contracted, energy, *_ = tile_terms(
        polarization, metric, three_panel, three_near, mask_panel.T, mask_near.T, green_function
    )
    screened, contracted, energy = hand_over(screened, contracted, energy)
    return screened, contracted.T.reshape(near_cols, TILE, contracted.shape[0] // TILE), energy.T


def solution(mesh):
    placed = (
        P("row", "col"),
        P("row", "col"),
        P("row", None, None),
        P("col", None, None),
        P(),
        P(),
        P(),
    )
    return jax.shard_map(
        per_device,
        mesh=mesh,
        in_specs=placed,
        out_specs=(P("row", "col"), P("col", None, "row"), P("row", "col")),
        check_vma=False,
    )
```

```python
import functools

import jax
import jax.numpy as jnp
from jax import lax
from jax.experimental import pallas as pl
from jax.experimental.pallas import tpu as pltpu
from jax.sharding import PartitionSpec as P

TILE = 64
NL = 256
RB = 64
AB = 32
MESH = pl.DeviceIdType.MESH


def place():
    row, col = lax.axis_index("row"), lax.axis_index("col")
    return row // 2, row % 2, col // 4, (col // 2) % 2, col % 2


def device(y, xh, z, xl, core):
    return (y * 2 + xh, (z * 2 + xl) * 2 + core)


class Copies:
    def __init__(self, send_sem):
        self.send_sem, self.started = send_sem, []

    def send(self, src, dst, recv_sem, target):
        index = len(self.started)
        copy = pltpu.make_async_remote_copy(
            src_ref=src,
            dst_ref=dst,
            send_sem=self.send_sem.at[index],
            recv_sem=recv_sem,
            device_id=target,
            device_id_type=MESH,
        )
        copy.start()
        self.started.append((copy, None))

    def send_if(self, wanted, src, dst, recv_sem, target):
        index = len(self.started)
        copy = pltpu.make_async_remote_copy(
            src_ref=src,
            dst_ref=dst,
            send_sem=self.send_sem.at[index],
            recv_sem=recv_sem,
            device_id=target,
            device_id_type=MESH,
        )
        pl.when(wanted)(copy.start)
        self.started.append((copy, wanted))

    def finish(self):
        for copy, wanted in self.started:
            if wanted is None:
                copy.wait_send()
            else:
                pl.when(wanted)(copy.wait_send)


def landed(ref, sem):
    pltpu.make_async_copy(ref, ref, sem).wait()


def prepare(panel, near, panel_mask, near_mask, green, panel_t, dressed, taken, flat, made, sem):
    start = lambda k, size: pl.ds(pl.multiple_of(k * size, size), size)

    def steps(source, mask, count, make, put, first, last):
        def fetch(i):
            block = source.at[start(i // 4, 128), start(i % 4, 16)]
            return pltpu.make_async_copy(block, taken.at[i % 2], sem.at[i % 2])

        fetch(first).start()

        def body(i, carry):
            @pl.when(i + 1 < last)
            def _():
                fetch(i + 1).start()

            fetch(i).wait()

            @pl.when(i >= first + 2)
            def _():
                put(i - 2).wait()

            for h in range(2):
                lanes = slice(h * 128, (h + 1) * 128)
                flat[h] = taken[i % 2, :, :, lanes].astype(jnp.float32).reshape(128 * 16, 128)
            rows = start(i // 4, 128)
            for m in range(16):
                make(
                    i,
                    m,
                    [
                        flat[h, pl.ds(m, 128, stride=16), :] * mask[rows, h * 128 : (h + 1) * 128]
                        for h in range(2)
                    ],
                )
            put(i).start()
            return carry

        lax.fori_loop(first, last, body, 0)
        put(last - 2).wait()
        put(last - 1).wait()

    def put_to(result):
        def put(i):
            place_at = result.at[:, start(i % 4, 512), start(i // 4, 128)]
            return pltpu.make_async_copy(made.at[i % 2], place_at, sem.at[2 + i % 2])

        return put

    def make_panel(i, m, halves):
        turned = jnp.concatenate([half.T.astype(jnp.bfloat16) for half in halves], 0)
        made[i % 2, :, m * 32 : (m + 1) * 32, :] = turned.reshape(8, 32, 128)

    def make_near(i, m, halves):
        block = jnp.concatenate([half.astype(jnp.bfloat16) for half in halves], 1)
        product = lax.dot_general(
            green[...], block, (((1,), (1,)), ((), ())), preferred_element_type=jnp.float32
        )
        made[i % 2, :, m * 32 : (m + 1) * 32, :] = product.astype(jnp.bfloat16).reshape(8, 32, 128)

    return (
        functools.partial(steps, panel, panel_mask, 16, make_panel, put_to(panel_t)),
        functools.partial(steps, near, near_mask, 8, make_near, put_to(dressed)),
    )


def screen_part(
    a_ref,
    b_ref,
    panel,
    near,
    panel_mask_ref,
    near_mask_ref,
    green_ref,
    out_ref,
    panel_t,
    dressed,
    ahead,
    a0,
    a1,
    b0,
    b1,
    a1_own,
    total,
    give,
    take,
    taken,
    flat,
    made,
    panel_blocks,
    near_blocks,
    panel_mask,
    near_mask,
    green,
    send_sem,
    own_sem,
    local_sem,
    x_sem,
    near_sem,
    far_sem,
    twin_sem,
    last_sem,
    step_sem,
    small_sem,
):
    row, col = lax.axis_index("row"), lax.axis_index("col")
    small = [
        pltpu.make_async_copy(panel_mask_ref, panel_blocks, small_sem.at[0]),
        pltpu.make_async_copy(near_mask_ref, near_blocks, small_sem.at[1]),
        pltpu.make_async_copy(green_ref, green, small_sem.at[2]),
    ]
    for copy in small:
        copy.start()

    def finish_masks():
        for copy in small:
            copy.wait()
        for blocks, mask, begin in (
            (panel_blocks, panel_mask, row * (panel_mask.shape[0] // RB)),
            (near_blocks, near_mask, col * (near_mask.shape[0] // RB)),
        ):
            count = mask.shape[0]
            shape = (count, blocks.shape[1])
            at = lax.broadcasted_iota(jnp.int32, shape, 0) // RB + begin
            pick = (at == lax.broadcasted_iota(jnp.int32, shape, 1)).astype(jnp.float32)
            shape = (blocks.shape[0], NL)
            wide = lax.broadcasted_iota(jnp.int32, shape, 1) // AB == lax.broadcasted_iota(jnp.int32, shape, 0)
            picked = lax.dot_general(
                pick, blocks[...].astype(jnp.float32), (((1,), (1,)), ((), ())), preferred_element_type=jnp.float32
            )
            mask[...] = jnp.dot(picked, wide.astype(jnp.float32), preferred_element_type=jnp.float32)

    panel_steps, near_steps = prepare(
        panel, near, panel_mask, near_mask, green, panel_t, dressed, taken, flat, made, step_sem
    )
    y, xh, z, xl, core = place()
    twin = device(y, xh, z, xl, 1 - core)
    rows, depth = a_ref.shape
    half, piece = rows // 2, rows // 4
    z_at = [lax.rem(z + d, 4) for d in range(4)]
    y_at = [lax.rem(y + d, 4) for d in range(4)]

    barrier = pltpu.get_barrier_semaphore()
    partners = [device(lax.rem(y + k // 2, 4), lax.rem(xh + k, 2), z, xl, core) for k in range(1, 8)]
    partners += [device(y, xh, lax.rem(z + k, 4), xl, core) for k in range(1, 4)]
    partners += [twin, device(y, xh, z, 1 - xl, core), device(y, xh, z, 1 - xl, 1 - core)]
    partners.append(device(y, 1 - xh, z, 1 - xl, core))
    for partner in partners:
        pl.semaphore_signal(barrier, inc=1, device_id=partner, device_id_type=MESH)
    pl.semaphore_wait(barrier, len(partners))

    copies = Copies(send_sem)

    own0, own1 = pl.ds(0, half), pl.ds(half, half)

    @pl.when(core == 0)
    def _():
        pltpu.make_async_copy(a_ref, a0.at[z], local_sem.at[0]).start()
        copy = pltpu.make_async_remote_copy(
            a_ref, a0.at[z], own_sem, local_sem.at[0], device_id=twin, device_id_type=MESH
        )
        copy.start()

    @pl.when(core == 1)
    def _():
        pltpu.make_async_copy(a_ref.at[own1], a1_own, local_sem.at[1]).start()
        copy = pltpu.make_async_remote_copy(
            a_ref.at[own0], a1_own, own_sem, local_sem.at[1], device_id=twin, device_id_type=MESH
        )
        copy.start()

    deep = (depth // 256 * 128 + 128, depth // 256 * 128)

    def b_slot(stream, k, p, part=None):
        buffer = b1.at[k] if stream == 0 else b0.at[k, stream - 1]
        start, count = p * deep[0], deep[p]
        if part is not None:
            start, count = start + part * (count // 2), count // 2
        return buffer.at[pl.ds(start, count)]

    def a_rows(stream, k, start, count):
        buffer = a0.at[k] if stream == 0 else a1.at[k, stream - 1]
        return buffer.at[pl.ds(start, count)]

    def a_slot(stream, k, p, part=None, of=core):
        start, count = of * half + p * piece, piece
        if part is not None:
            start, count = start + part * (count // 2), count // 2
        return a_rows(stream, k, pl.multiple_of(start, piece // 2), count)

    b_up = [device(y_at[1], xh, z, xl, core), device(y_at[3], xh, z, xl, core)]
    a_up = [device(y, xh, z_at[1], xl, core), device(y, xh, z_at[3], xl, core)]
    A, B = (a_slot, 0, z_at, a_up), (b_slot, 3, y_at, b_up)

    def b_own(p, base=0):
        return b_ref.at[pl.ds(base + p * deep[0], deep[p])]

    inner = xh != xl

    def b_along_x(p):
        def at(role):
            return b0.at[y, role, pl.ds(p * deep[0], deep[p])]

        for j in range(2):
            copies.send_if(inner, b_own(p), at(0), x_sem.at[1, 0, p], device(y, j, z, xh, core))

    def a_along_x(p):
        source = a1_own.at[pl.ds(p * piece, piece)]
        for j in range(2):
            copies.send_if(inner, source, a_slot(1, z, p), x_sem.at[0, 0, p], device(y, xl, z, j, core))

    outer = jnp.logical_not(inner)

    def a_outer_along_x(p):
        source = a1_own.at[pl.ds(p * piece, piece)]
        copies.send_if(outer, source, a_slot(2, z, p), x_sem.at[0, 1, p], device(y, xh, z, 1 - xl, core))

    def b_outer_along_x(p):
        copies.send_if(outer, b_own(p), b_slot(2, y, p), x_sem.at[1, 1, p], device(y, 1 - xh, z, xl, core))

    def outer_keep():
        for p in range(2):
            source = a1_own.at[pl.ds(p * piece, piece)]
            pltpu.make_async_copy(source, a_slot(2, z, p), x_sem.at[0, 1, p]).start()
            pltpu.make_async_copy(b_own(p), b_slot(2, y, p), x_sem.at[1, 1, p]).start()

    def spread(array, stream, p, source=None):
        slot, base, at, to = array
        for side in range(2):
            here = slot(stream, at[0], p)
            copies.send(here if source is None else source, here, near_sem.at[base + stream, side, p], to[side])

    def start_near(wanted, p, source):
        for side in range(2):
            copies.send_if(wanted, source, a_slot(0, z, p), near_sem.at[0, side, p], a_up[side])

    def to_twin(stream, k, p, index):
        here = a_slot(stream, k, p)
        copies.send(here, here, twin_sem.at[stream, index, p], twin)

    def go_on(array, stream, p):
        slot, base, at, to = array
        for side in range(2):
            k = at[3 - 2 * side]
            landed(slot(stream, k, p), near_sem.at[base + stream, side, p])
            half_of = slot(stream, k, p, side)
            copies.send(half_of, half_of, far_sem.at[base + stream, side, p], to[side])
        if base == 0:
            for side in range(2):
                to_twin(stream, at[3 - 2 * side], p, 3 - 2 * side)

    def far(array, stream, p):
        slot, base, at, to = array
        for side in range(2):
            landed(slot(stream, at[2], p, side), far_sem.at[base + stream, side, p])
        if base == 0:
            to_twin(stream, at[2], p, 2)

    def from_twin(stream, p, indices):
        for d in indices:
            landed(a_slot(stream, z_at[d], p, of=1 - core), twin_sem.at[stream, d, p])

    def arrive(s, p):
        landed(a_slot(s, z, p), x_sem.at[0, s - 1, p])
        spread(A, s, p)
        landed(b_slot(s, y, p), x_sem.at[1, s - 1, p])
        spread(B, s, p)
        to_twin(s, z, p, 0)

    def keep_rows(k, p, j):
        lanes = slice(p * deep[0], p * deep[0] + deep[p])

        def body(t, carry):
            at = pl.ds(pl.multiple_of(t * half, half), half)
            total[0, j, at] += jnp.dot(
                a0[k, at, lanes], b0[k, j, lanes], preferred_element_type=jnp.float32
            )
            return carry

        lax.fori_loop(0, 2, body, 0)

    def keep_cols(k, p, j):
        def body(t, carry):
            at = pl.ds(pl.multiple_of(t * half + p * piece, piece), piece)
            total[1, j, at] += jnp.dot(a1[k, j, at], b1[k], preferred_element_type=jnp.float32)
            return carry

        lax.fori_loop(0, 2, body, 0)

    for p in range(2):
        start_near(core == 0, p, a_ref.at[pl.ds(p * piece, piece)])
    b_along_x(0)
    for p in range(2):
        spread(B, 0, p, b_own(p, depth))
    landed(a1_own, local_sem.at[1])
    a_along_x(0)
    b_along_x(1)
    a_along_x(1)
    landed(a0.at[z], local_sem.at[0])
    for p in range(2):
        start_near(core == 1, p, a_slot(0, z, p))
    pl.when(outer)(outer_keep)
    b_local = pltpu.make_async_copy(b_ref.at[pl.ds(depth, depth)], b1.at[y], local_sem.at[2])
    b_local.start()
    total[...] = jnp.zeros_like(total)
    finish_masks()

    panel_steps(0, 6)
    for p in range(2):
        a_outer_along_x(p)
    go_on(B, 0, 0)
    go_on(A, 0, 0)
    panel_steps(6, 12)
    go_on(B, 0, 1)
    go_on(A, 0, 1)
    arrive(1, 0)
    panel_steps(12, 16)
    near_steps(0, 4)
    for p in range(2):
        far(B, 0, p)
        far(A, 0, p)
    arrive(1, 1)
    for p in range(2):
        b_outer_along_x(p)
    go_on(A, 1, 0)
    go_on(B, 1, 0)
    near_steps(4, 8)
    go_on(A, 1, 1)
    go_on(B, 1, 1)
    arrive(2, 0)
    for p in range(2):
        from_twin(0, p, (1, 2, 3))
    b_local.wait()

    def others(p):
        def step(d, carry):
            keep_rows(lax.rem(y + d, 4), p, 0)
            keep_cols(lax.rem(z + d, 4), p, 0)
            return carry

        lax.fori_loop(0, 4, step, 0)

    far(A, 1, 0)
    far(B, 1, 0)
    from_twin(1, 0, (0, 1, 2, 3))
    others(0)
    arrive(2, 1)
    far(A, 1, 1)
    far(B, 1, 1)
    go_on(A, 2, 0)
    go_on(B, 2, 0)
    from_twin(1, 1, (0, 1, 2, 3))
    others(1)
    for i in range(2):
        give[i] = total[i, 0].astype(jnp.bfloat16)
    copies.send(give.at[0], take.at[0], last_sem.at[0], device(y, xh, z, 1 - xl, core))
    copies.send(give.at[1], take.at[1], last_sem.at[1], device(y, 1 - xh, z, xl, core))
    from_twin(2, 0, (0, 1, 3))

    def own(p):
        def step(d):
            keep_rows(y_at[d], p, 1)
            keep_cols(z_at[d], p, 1)

        return step

    for d in (0, 1, 3):
        own(0)(d)
    go_on(A, 2, 1)
    go_on(B, 2, 1)
    from_twin(2, 1, (0, 1, 3))
    for d in (0, 1, 3):
        own(1)(d)
    ahead()
    landed(take.at[0], last_sem.at[0])
    landed(take.at[1], last_sem.at[1])
    total[0, 1] += take[0].astype(jnp.float32) + take[1].astype(jnp.float32)
    far(B, 2, 0)
    far(A, 2, 0)
    keep_rows(y_at[2], 0, 1)
    from_twin(2, 0, (2,))
    keep_cols(z_at[2], 0, 1)
    far(B, 2, 1)
    far(A, 2, 1)
    keep_rows(y_at[2], 1, 1)
    from_twin(2, 1, (2,))
    keep_cols(z_at[2], 1, 1)
    out_ref[...] = (total[0, 1] + total[1, 1]).astype(jnp.bfloat16)

    def finish():
        copies.finish()

        @pl.when(core == 0)
        def _():
            pltpu.make_async_copy(a_ref, a0.at[z], own_sem).wait()

        @pl.when(core == 1)
        def _():
            pltpu.make_async_copy(a_ref.at[own0], a1_own, own_sem).wait()

    return finish


LATE = 1152


def contract_part(
    s_ref,
    panel_t,
    dressed,
    out_ref,
    energy_ref,
    block,
    part,
    far_y,
    near_y,
    cross_y,
    cross_x,
    far_x,
    near_x,
    total,
    other,
    dressed_b,
    tile,
    row_sum,
    tile_row,
    tile_col,
    send_sem,
    block_sem,
    far_sem,
    near_sem,
    cross_sem,
    row_sem,
    col_sem,
):
    y, xh, z, xl, core = place()
    col = (z * 2 + xl) * 2 + core
    f32, bf16 = jnp.float32, jnp.bfloat16

    def in_row(d, j):
        return device(lax.rem(y + d, 4), lax.rem(xh + j, 2), z, xl, core)

    order = [(2, 1), (2, 0), (1, 1), (3, 1), (1, 0), (3, 0), (0, 1), (0, 0)]
    chunk = block.shape[1]

    def fetch(i):
        d, j = order[i // 2]
        share = lax.rem(y + d, 4) * 2 + lax.rem(xh + j, 2)
        return pltpu.make_async_copy(
            panel_t.at[share, pl.ds(i % 2 * chunk, chunk)], block.at[i % 2], block_sem.at[i % 2]
        )

    fetch(0).start()
    fetch(1).start()
    yield

    copies = Copies(send_sem)
    rows = TILE * 32
    early = rows - LATE
    h_late, h_early = LATE // 2, early // 2
    up, down, across = in_row(1, 0), in_row(3, 0), in_row(0, 1)

    def late(d, j, start=0, count=LATE):
        return part.at[d * 2 + j, pl.ds(start, count)]

    def first(d, j, start=0, count=early):
        return part.at[d * 2 + j, pl.ds(LATE + start, count)]

    for i, (d, j) in enumerate(order):
        for h in range(2):
            fetch(i * 2 + h).wait()

            def multiply(t, carry):
                at = pl.ds(pl.multiple_of(t * 256, 256), 256)
                to = pl.ds(pl.multiple_of(h * chunk + t * 256, 256), 256)
                part[d * 2 + j, to] = jnp.dot(
                    block[h, at], s_ref[...], preferred_element_type=f32
                ).astype(bf16)
                return carry

            lax.fori_loop(0, chunk // 256, multiply, 0)
            if i < 7:
                fetch(i * 2 + 2 + h).start()
        if j == 1:
            copies.send(first(d, 1), cross_x.at[d], cross_sem.at[d], across)
        if d == 2:
            copies.send(late(2, j, 0, h_late), far_y.at[j, 0], far_sem.at[j, 0], up)
            copies.send(late(2, j, h_late, h_late), far_y.at[j, 1], far_sem.at[j, 1], down)
        if d == 1:
            copies.send(late(1, j, h_late, h_late), near_y.at[j, 0, pl.ds(h_late, h_late)], near_sem.at[j, 0, 0], up)
        if d == 3:
            copies.send(late(3, j, 0, h_late), near_y.at[j, 1, pl.ds(0, h_late)], near_sem.at[j, 1, 0], down)

    def add(ref, *others):
        result = ref[...].astype(f32)
        for each in others:
            result = result + each[...].astype(f32)
        ref[...] = result.astype(bf16)

    def share(d, j):
        return lax.rem(y + d, 4) * 2 + lax.rem(xh + j, 2)

    turns = [(1, 1), (3, 1), (1, 0), (3, 0), (2, 0), (2, 1), (0, 1), (0, 0)]

    def fetch_dressed(i):
        return pltpu.make_async_copy(dressed.at[share(*turns[i])], dressed_b, block_sem.at[2])

    fetch_dressed(0).start()
    tile[...] = jnp.zeros_like(tile)

    def energy(i):
        d, j = turns[i]
        fetch_dressed(i).wait()
        for h in range(2):
            lanes = slice(h * 128, (h + 1) * 128)
            other[h] = dressed_b[:, lanes].astype(f32)
            total[h] = part[d * 2 + j, :, lanes].astype(f32)
        if i < 7:
            fetch_dressed(i + 1).start()

        def column(ref, l):
            halves = [ref[h, pl.ds(l, TILE, stride=32), :].astype(bf16) for h in range(2)]
            return jnp.concatenate(halves, 1)

        def body(k, carry):
            for l in range(4):
                carry = carry + lax.dot_general(
                    column(total, k * 4 + l),
                    column(other, k * 4 + l),
                    (((1,), (1,)), ((), ())),
                    preferred_element_type=f32,
                )
            return carry

        tile[:, :TILE] += lax.fori_loop(0, 8, body, jnp.zeros((TILE, TILE), f32))

    def forward_y(j):
        landed(far_y.at[j, 0], far_sem.at[j, 0])
        add(late(1, j, 0, h_late), far_y.at[j, 0])
        copies.send(late(1, j, 0, h_late), near_y.at[j, 0, pl.ds(0, h_late)], near_sem.at[j, 0, 1], up)
        landed(far_y.at[j, 1], far_sem.at[j, 1])
        add(late(3, j, h_late, h_late), far_y.at[j, 1])
        copies.send(late(3, j, h_late, h_late), near_y.at[j, 1, pl.ds(h_late, h_late)], near_sem.at[j, 1, 1], down)

    def both_near(j, ref):
        count = ref.shape[1] // 2
        for side in range(2):
            for turn in range(2):
                start = count if (side == 0) == (turn == 0) else 0
                landed(ref.at[side, pl.ds(start, count)], near_sem.at[j, side, turn])

    def share_of(row):
        return pl.ds(pl.multiple_of(row * 8, 8), 8)

    def settle(at, *terms):
        result = terms[0][...].astype(f32)
        for each in terms[1:]:
            result = result + each[...].astype(f32)
        out_ref[at] = result.astype(bf16)

    energy(0)
    energy(1)
    forward_y(1)
    energy(2)
    energy(3)
    forward_y(0)
    energy(4)
    landed(cross_x.at[2], cross_sem.at[2])
    add(first(2, 0), cross_x.at[2])
    copies.send(first(2, 0, 0, h_early), far_x.at[0], far_sem.at[2, 0], up)
    copies.send(first(2, 0, h_early, h_early), far_x.at[1], far_sem.at[2, 1], down)
    landed(cross_x.at[1], cross_sem.at[1])
    add(first(1, 0), cross_x.at[1])
    copies.send(first(1, 0, h_early, h_early), near_x.at[0, pl.ds(h_early, h_early)], near_sem.at[2, 0, 0], up)
    landed(cross_x.at[3], cross_sem.at[3])
    add(first(3, 0), cross_x.at[3])
    copies.send(first(3, 0, 0, h_early), near_x.at[1, pl.ds(0, h_early)], near_sem.at[2, 1, 0], down)
    energy(5)
    energy(6)
    energy(7)
    for s in range(1, 8):
        target = in_row(s // 2, s % 2)
        copies.send(tile.at[share_of(target[0])], tile_row.at[s], row_sem.at[s], target)

    both_near(1, near_y.at[1])
    add(late(0, 1), near_y.at[1, 0], near_y.at[1, 1])
    copies.send(late(0, 1), cross_y, cross_sem.at[4], across)

    landed(far_x.at[0], far_sem.at[2, 0])
    add(first(1, 0, 0, h_early), far_x.at[0])
    copies.send(first(1, 0, 0, h_early), near_x.at[0, pl.ds(0, h_early)], near_sem.at[2, 0, 1], up)
    landed(far_x.at[1], far_sem.at[2, 1])
    add(first(3, 0, h_early, h_early), far_x.at[1])
    copies.send(first(3, 0, h_early, h_early), near_x.at[1, pl.ds(h_early, h_early)], near_sem.at[2, 1, 1], down)

    mine = tile[share_of(y * 2 + xh)]
    for s in range(1, 8):
        landed(tile_row.at[s], row_sem.at[s])
        mine = mine + tile_row[s]
    along_z = [device(y, xh, lax.rem(z + d, 4), xl, core) for d in range(1, 4)]
    close = [device(y, xh, z, xl, 1 - core), device(y, xh, z, 1 - xl, core), device(y, xh, z, 1 - xl, 1 - core)]
    for turn, targets in enumerate((along_z, close)):
        row_sum[turn] = mine
        for d, target in enumerate(targets):
            copies.send(row_sum.at[turn], tile_col.at[turn * 3 + d], col_sem.at[turn * 3 + d], target)
        for d in range(turn * 3, turn * 3 + 3):
            landed(tile_col.at[d], col_sem.at[d])
            mine = mine + tile_col[d]

    both_near(0, near_y.at[0])
    for h in range(2):
        lanes = slice(h * 128, (h + 1) * 128)
        total[h, :LATE] = (
            part[0, :LATE, lanes].astype(f32) + near_y[0, 0, :, lanes].astype(f32) + near_y[0, 1, :, lanes].astype(f32)
        )
    turned = pltpu.roll(-mine, lax.rem(128 - 4 * col, 128), 1).T
    energy_ref[...] = turned[:4]
    landed(cross_x.at[0], cross_sem.at[0])
    both_near(2, near_x)
    settle(pl.ds(LATE, early), first(0, 0), cross_x.at[0], near_x.at[0], near_x.at[1])
    landed(cross_y, cross_sem.at[4])
    for h in range(2):
        lanes = slice(h * 128, (h + 1) * 128)
        out_ref[:LATE, lanes] = (total[h, :LATE] + cross_y[:, lanes].astype(f32)).astype(bf16)
    copies.finish()


SCREEN_SCRATCH = 26


def kernel(*refs):
    inputs, (screened, contracted, energy, panel_t, dressed), scratch = refs[:7], refs[7:12], refs[12:]
    first, second = scratch[:SCREEN_SCRATCH], scratch[SCREEN_SCRATCH:]
    flat = first[9]
    steps = contract_part(screened, panel_t, dressed, contracted, energy, *second[:8], flat, *second[8:])
    finish = screen_part(*inputs, screened, panel_t, dressed, lambda: next(steps), *first)
    next(steps, None)
    finish()


def tile_terms(a, b, panel, near, panel_mask, near_mask, green):
    rows, depth = a.shape
    cols = b.shape[1]
    long = TILE * 32
    early = long - LATE
    bf16, f32 = jnp.bfloat16, jnp.float32
    dma = pltpu.SemaphoreType.DMA
    hbm, vmem = pl.BlockSpec(memory_space=pl.ANY), pl.BlockSpec(memory_space=pltpu.VMEM)
    first = [
        pltpu.VMEM((4, rows, depth), bf16),
        pltpu.VMEM((4, 2, rows, depth), bf16),
        pltpu.VMEM((4, 2, depth, cols), bf16),
        pltpu.VMEM((4, depth, cols), bf16),
        pltpu.VMEM((rows // 2, depth), bf16),
        pltpu.VMEM((2, 2, rows, cols), f32),
        pltpu.VMEM((2, rows, cols), bf16),
        pltpu.VMEM((2, rows, cols), bf16),
        pltpu.VMEM((2, 128, 16, NL), bf16),
        pltpu.VMEM((2, 128 * 16, 128), f32),
        pltpu.VMEM((2, 8, 16 * 32, 128), bf16),
        pltpu.VMEM(panel_mask.shape, jnp.int32),
        pltpu.VMEM(near_mask.shape, jnp.int32),
        pltpu.VMEM((rows, NL), f32),
        pltpu.VMEM((cols, NL), f32),
        pltpu.VMEM((NL, NL), bf16),
        dma((96,)),
        dma,
        dma((3,)),
        dma((2, 2, 2)),
        dma((6, 2, 2)),
        dma((6, 2, 2)),
        dma((3, 4, 2)),
        dma((2,)),
        dma((4,)),
        dma((3,)),
    ]
    second = [
        pltpu.VMEM((2, long // 2, rows), bf16),
        pltpu.VMEM((8, long, cols), bf16),
        pltpu.VMEM((2, 2, LATE // 2, cols), bf16),
        pltpu.VMEM((2, 2, LATE, cols), bf16),
        pltpu.VMEM((LATE, cols), bf16),
        pltpu.VMEM((4, early, cols), bf16),
        pltpu.VMEM((2, early // 2, cols), bf16),
        pltpu.VMEM((2, early, cols), bf16),
        pltpu.VMEM((2, long, 128), f32),
        pltpu.VMEM((long, cols), bf16),
        pltpu.VMEM((TILE, 128), f32),
        pltpu.VMEM((2, 8, 128), f32),
        pltpu.VMEM((8, 8, 128), f32),
        pltpu.VMEM((6, 8, 128), f32),
        dma((48,)),
        dma((3,)),
        dma((3, 2)),
        dma((3, 2, 2)),
        dma((5,)),
        dma((8,)),
        dma((6,)),
    ]
    assert len(first) == SCREEN_SCRATCH
    return pl.pallas_call(
        kernel,
        out_shape=(
            jax.ShapeDtypeStruct((rows, cols), bf16),
            jax.ShapeDtypeStruct((long, cols), bf16),
            jax.ShapeDtypeStruct((4, 8), f32),
            jax.ShapeDtypeStruct((8, long, rows), bf16),
            jax.ShapeDtypeStruct((8, long, cols), bf16),
        ),
        in_specs=[hbm] * 7,
        out_specs=(vmem, vmem, vmem, hbm, hbm),
        scratch_shapes=first + second,
        compiler_params=pltpu.CompilerParams(
            collective_id=0, has_side_effects=True, vmem_limit_bytes=64 * 2**20 - 2**16
        ),
        name="tile_terms",
    )(a, b, panel, near, panel_mask, near_mask, green)


def hand_over_kernel(*refs):
    sources, results, held, sem = refs[:3], refs[3:6], refs[6:9], refs[9]
    pieces = []
    for k, source in enumerate(sources):
        count = 4 if k == 1 else 1
        size = source.shape[0] // count
        pieces += [(k, pl.ds(i * size, size)) for i in range(count)]
    taken = [pltpu.make_async_copy(sources[k].at[at], held[k].at[at], sem.at[0, i]) for i, (k, at) in enumerate(pieces)]
    given = [pltpu.make_async_copy(held[k].at[at], results[k].at[at], sem.at[1, i]) for i, (k, at) in enumerate(pieces)]
    for copy in taken:
        copy.start()
    for i, copy in enumerate(given):
        taken[i].wait()
        copy.start()
    for copy in given:
        copy.wait()


def hand_over(*arrays):
    hbm = pl.BlockSpec(memory_space=pl.ANY)
    return pl.pallas_call(
        hand_over_kernel,
        out_shape=tuple(jax.ShapeDtypeStruct(array.shape, array.dtype) for array in arrays),
        in_specs=[hbm] * 3,
        out_specs=(hbm,) * 3,
        scratch_shapes=[pltpu.VMEM(array.shape, array.dtype) for array in arrays]
        + [pltpu.SemaphoreType.DMA((2, 6))],
        name="hand_over",
    )(*arrays)


def per_device(
    polarization, metric, three_panel, three_near, green_function, mask_panel, mask_near
):
    near_cols = metric.shape[1]
    screened, contracted, energy, *_ = tile_terms(
        polarization, metric, three_panel, three_near, mask_panel.T, mask_near.T, green_function
    )
    screened, contracted, energy = hand_over(screened, contracted, energy)
    return screened, contracted.T.reshape(near_cols, TILE, contracted.shape[0] // TILE), energy.T


def solution(mesh):
    placed = (
        P("row", "col"),
        P("row", "col"),
        P("row", None, None),
        P("col", None, None),
        P(),
        P(),
        P(),
    )
    return jax.shard_map(
        per_device,
        mesh=mesh,
        in_specs=placed,
        out_specs=(P("row", "col"), P("col", None, "row"), P("row", "col")),
        check_vma=False,
    )
```

```python
import functools

import jax
import jax.numpy as jnp
from jax import lax
from jax.experimental import pallas as pl
from jax.experimental.pallas import tpu as pltpu
from jax.sharding import PartitionSpec as P

TILE = 64
NL = 256
RB = 64
AB = 32
MESH = pl.DeviceIdType.MESH


def place():
    row, col = lax.axis_index("row"), lax.axis_index("col")
    return row // 2, row % 2, col // 4, (col // 2) % 2, col % 2


def device(y, xh, z, xl, core):
    return (y * 2 + xh, (z * 2 + xl) * 2 + core)


class Copies:
    def __init__(self, send_sem):
        self.send_sem, self.started, self.count = send_sem, [], 0

    def send(self, src, dst, recv_sem, target):
        index, self.count = self.count, self.count + 1
        copy = pltpu.make_async_remote_copy(
            src_ref=src,
            dst_ref=dst,
            send_sem=self.send_sem.at[index],
            recv_sem=recv_sem,
            device_id=target,
            device_id_type=MESH,
        )
        copy.start()
        self.started.append((copy, None))

    def send_if(self, wanted, src, dst, recv_sem, target):
        index, self.count = self.count, self.count + 1
        copy = pltpu.make_async_remote_copy(
            src_ref=src,
            dst_ref=dst,
            send_sem=self.send_sem.at[index],
            recv_sem=recv_sem,
            device_id=target,
            device_id_type=MESH,
        )
        pl.when(wanted)(copy.start)
        self.started.append((copy, wanted))

    def finish(self, but=0):
        done = len(self.started) - but
        for copy, wanted in self.started[:done]:
            if wanted is None:
                copy.wait_send()
            else:
                pl.when(wanted)(copy.wait_send)
        self.started = self.started[done:]


def landed(ref, sem):
    pltpu.make_async_copy(ref, ref, sem).wait()


def prepare(panel, near, panel_mask, near_mask, green, panel_t, dressed, taken, flat, made, sem):
    start = lambda k, size: pl.ds(pl.multiple_of(k * size, size), size)

    def steps(source, mask, count, make, put, first, last):
        def fetch(i):
            block = source.at[start(i // 4, 128), start(i % 4, 16)]
            return pltpu.make_async_copy(block, taken.at[i % 2], sem.at[i % 2])

        fetch(first).start()

        def body(i, carry):
            @pl.when(i + 1 < last)
            def _():
                fetch(i + 1).start()

            fetch(i).wait()

            @pl.when(i >= first + 2)
            def _():
                put(i - 2).wait()

            for h in range(2):
                lanes = slice(h * 128, (h + 1) * 128)
                flat[h] = taken[i % 2, :, :, lanes].astype(jnp.float32).reshape(128 * 16, 128)
            rows = start(i // 4, 128)
            for m in range(16):
                make(
                    i,
                    m,
                    [
                        flat[h, pl.ds(m, 128, stride=16), :] * mask[rows, h * 128 : (h + 1) * 128]
                        for h in range(2)
                    ],
                )
            put(i).start()
            return carry

        lax.fori_loop(first, last, body, 0)
        put(last - 2).wait()
        put(last - 1).wait()

    def put_to(result):
        def put(i):
            place_at = result.at[:, start(i % 4, 512), start(i // 4, 128)]
            return pltpu.make_async_copy(made.at[i % 2], place_at, sem.at[2 + i % 2])

        return put

    def make_panel(i, m, halves):
        turned = jnp.concatenate([half.T.astype(jnp.bfloat16) for half in halves], 0)
        made[i % 2, :, m * 32 : (m + 1) * 32, :] = turned.reshape(8, 32, 128)

    def make_near(i, m, halves):
        block = jnp.concatenate([half.astype(jnp.bfloat16) for half in halves], 1)
        product = lax.dot_general(
            green[...], block, (((1,), (1,)), ((), ())), preferred_element_type=jnp.float32
        )
        made[i % 2, :, m * 32 : (m + 1) * 32, :] = product.astype(jnp.bfloat16).reshape(8, 32, 128)

    return (
        functools.partial(steps, panel, panel_mask, 16, make_panel, put_to(panel_t)),
        functools.partial(steps, near, near_mask, 8, make_near, put_to(dressed)),
    )


def screen_part(
    a_ref,
    b_ref,
    panel,
    near,
    panel_mask_ref,
    near_mask_ref,
    green_ref,
    out_ref,
    panel_t,
    dressed,
    ahead,
    a0,
    a1,
    b0,
    b1,
    a1_own,
    total,
    give,
    take,
    taken,
    flat,
    made,
    panel_blocks,
    near_blocks,
    panel_mask,
    near_mask,
    green,
    send_sem,
    own_sem,
    local_sem,
    x_sem,
    near_sem,
    far_sem,
    twin_sem,
    last_sem,
    step_sem,
    small_sem,
):
    row, col = lax.axis_index("row"), lax.axis_index("col")
    small = [
        pltpu.make_async_copy(panel_mask_ref, panel_blocks, small_sem.at[0]),
        pltpu.make_async_copy(near_mask_ref, near_blocks, small_sem.at[1]),
        pltpu.make_async_copy(green_ref, green, small_sem.at[2]),
    ]
    for copy in small:
        copy.start()

    def finish_masks():
        for copy in small:
            copy.wait()
        for blocks, mask, begin in (
            (panel_blocks, panel_mask, row * (panel_mask.shape[0] // RB)),
            (near_blocks, near_mask, col * (near_mask.shape[0] // RB)),
        ):
            count = mask.shape[0]
            shape = (count, blocks.shape[1])
            at = lax.broadcasted_iota(jnp.int32, shape, 0) // RB + begin
            pick = (at == lax.broadcasted_iota(jnp.int32, shape, 1)).astype(jnp.float32)
            shape = (blocks.shape[0], NL)
            wide = lax.broadcasted_iota(jnp.int32, shape, 1) // AB == lax.broadcasted_iota(jnp.int32, shape, 0)
            picked = lax.dot_general(
                pick, blocks[...].astype(jnp.float32), (((1,), (1,)), ((), ())), preferred_element_type=jnp.float32
            )
            mask[...] = jnp.dot(picked, wide.astype(jnp.float32), preferred_element_type=jnp.float32)

    panel_steps, near_steps = prepare(
        panel, near, panel_mask, near_mask, green, panel_t, dressed, taken, flat, made, step_sem
    )
    y, xh, z, xl, core = place()
    twin = device(y, xh, z, xl, 1 - core)
    rows, depth = a_ref.shape
    half, piece = rows // 2, rows // 4
    z_at = [lax.rem(z + d, 4) for d in range(4)]
    y_at = [lax.rem(y + d, 4) for d in range(4)]

    barrier = pltpu.get_barrier_semaphore()
    partners = [device(lax.rem(y + k // 2, 4), lax.rem(xh + k, 2), z, xl, core) for k in range(1, 8)]
    partners += [device(y, xh, lax.rem(z + k, 4), xl, core) for k in range(1, 4)]
    partners += [twin, device(y, xh, z, 1 - xl, core), device(y, xh, z, 1 - xl, 1 - core)]
    partners.append(device(y, 1 - xh, z, 1 - xl, core))
    for partner in partners:
        pl.semaphore_signal(barrier, inc=1, device_id=partner, device_id_type=MESH)
    pl.semaphore_wait(barrier, len(partners))

    copies = Copies(send_sem)

    own0, own1 = pl.ds(0, half), pl.ds(half, half)

    @pl.when(core == 0)
    def _():
        pltpu.make_async_copy(a_ref, a0.at[z], local_sem.at[0]).start()
        copy = pltpu.make_async_remote_copy(
            a_ref, a0.at[z], own_sem, local_sem.at[0], device_id=twin, device_id_type=MESH
        )
        copy.start()

    @pl.when(core == 1)
    def _():
        pltpu.make_async_copy(a_ref.at[own1], a1_own, local_sem.at[1]).start()
        copy = pltpu.make_async_remote_copy(
            a_ref.at[own0], a1_own, own_sem, local_sem.at[1], device_id=twin, device_id_type=MESH
        )
        copy.start()

    deep = (depth // 256 * 128 + 128, depth // 256 * 128)

    def b_slot(stream, k, p, part=None):
        buffer = b1.at[k] if stream == 0 else b0.at[k, stream - 1]
        start, count = p * deep[0], deep[p]
        if part is not None:
            start, count = start + part * (count // 2), count // 2
        return buffer.at[pl.ds(start, count)]

    def a_rows(stream, k, start, count):
        buffer = a0.at[k] if stream == 0 else a1.at[k, stream - 1]
        return buffer.at[pl.ds(start, count)]

    def a_slot(stream, k, p, part=None, of=core):
        start, count = of * half + p * piece, piece
        if part is not None:
            start, count = start + part * (count // 2), count // 2
        return a_rows(stream, k, pl.multiple_of(start, piece // 2), count)

    b_up = [device(y_at[1], xh, z, xl, core), device(y_at[3], xh, z, xl, core)]
    a_up = [device(y, xh, z_at[1], xl, core), device(y, xh, z_at[3], xl, core)]
    A, B = (a_slot, 0, z_at, a_up), (b_slot, 3, y_at, b_up)

    def b_own(p, base=0):
        return b_ref.at[pl.ds(base + p * deep[0], deep[p])]

    inner = xh != xl

    def b_along_x(p):
        def at(role):
            return b0.at[y, role, pl.ds(p * deep[0], deep[p])]

        for j in range(2):
            copies.send_if(inner, b_own(p), at(0), x_sem.at[1, 0, p], device(y, j, z, xh, core))

    def a_along_x(p):
        source = a1_own.at[pl.ds(p * piece, piece)]
        for j in range(2):
            copies.send_if(inner, source, a_slot(1, z, p), x_sem.at[0, 0, p], device(y, xl, z, j, core))

    outer = jnp.logical_not(inner)

    def a_outer_along_x(p):
        source = a1_own.at[pl.ds(p * piece, piece)]
        copies.send_if(outer, source, a_slot(2, z, p), x_sem.at[0, 1, p], device(y, xh, z, 1 - xl, core))

    def b_outer_along_x(p):
        copies.send_if(outer, b_own(p), b_slot(2, y, p), x_sem.at[1, 1, p], device(y, 1 - xh, z, xl, core))

    def outer_keep():
        for p in range(2):
            source = a1_own.at[pl.ds(p * piece, piece)]
            pltpu.make_async_copy(source, a_slot(2, z, p), x_sem.at[0, 1, p]).start()
            pltpu.make_async_copy(b_own(p), b_slot(2, y, p), x_sem.at[1, 1, p]).start()

    def spread(array, stream, p, source=None):
        slot, base, at, to = array
        for side in range(2):
            here = slot(stream, at[0], p)
            copies.send(here if source is None else source, here, near_sem.at[base + stream, side, p], to[side])

    def start_near(wanted, p, source):
        for side in range(2):
            copies.send_if(wanted, source, a_slot(0, z, p), near_sem.at[0, side, p], a_up[side])

    def to_twin(stream, k, p, index):
        here = a_slot(stream, k, p)
        copies.send(here, here, twin_sem.at[stream, index, p], twin)

    def go_on(array, stream, p):
        slot, base, at, to = array
        for side in range(2):
            k = at[3 - 2 * side]
            landed(slot(stream, k, p), near_sem.at[base + stream, side, p])
            half_of = slot(stream, k, p, side)
            copies.send(half_of, half_of, far_sem.at[base + stream, side, p], to[side])
        if base == 0:
            for side in range(2):
                to_twin(stream, at[3 - 2 * side], p, 3 - 2 * side)

    def far(array, stream, p):
        slot, base, at, to = array
        for side in range(2):
            landed(slot(stream, at[2], p, side), far_sem.at[base + stream, side, p])
        if base == 0:
            to_twin(stream, at[2], p, 2)

    def from_twin(stream, p, indices):
        for d in indices:
            landed(a_slot(stream, z_at[d], p, of=1 - core), twin_sem.at[stream, d, p])

    def arrive(s, p):
        landed(a_slot(s, z, p), x_sem.at[0, s - 1, p])
        spread(A, s, p)
        landed(b_slot(s, y, p), x_sem.at[1, s - 1, p])
        spread(B, s, p)
        to_twin(s, z, p, 0)

    def keep_rows(k, p, j):
        lanes = slice(p * deep[0], p * deep[0] + deep[p])

        def body(t, carry):
            at = pl.ds(pl.multiple_of(t * half, half), half)
            total[0, j, at] += jnp.dot(
                a0[k, at, lanes], b0[k, j, lanes], preferred_element_type=jnp.float32
            )
            return carry

        lax.fori_loop(0, 2, body, 0)

    def keep_cols(k, p, j):
        def body(t, carry):
            at = pl.ds(pl.multiple_of(t * half + p * piece, piece), piece)
            total[1, j, at] += jnp.dot(a1[k, j, at], b1[k], preferred_element_type=jnp.float32)
            return carry

        lax.fori_loop(0, 2, body, 0)

    for p in range(2):
        start_near(core == 0, p, a_ref.at[pl.ds(p * piece, piece)])
    b_along_x(0)
    for p in range(2):
        spread(B, 0, p, b_own(p, depth))
    landed(a1_own, local_sem.at[1])
    a_along_x(0)
    b_along_x(1)
    a_along_x(1)
    landed(a0.at[z], local_sem.at[0])
    for p in range(2):
        start_near(core == 1, p, a_slot(0, z, p))
    pl.when(outer)(outer_keep)
    b_local = pltpu.make_async_copy(b_ref.at[pl.ds(depth, depth)], b1.at[y], local_sem.at[2])
    b_local.start()
    total[...] = jnp.zeros_like(total)
    finish_masks()

    panel_steps(0, 6)
    for p in range(2):
        a_outer_along_x(p)
    go_on(B, 0, 0)
    go_on(A, 0, 0)
    panel_steps(6, 12)
    go_on(B, 0, 1)
    go_on(A, 0, 1)
    arrive(1, 0)
    panel_steps(12, 16)
    near_steps(0, 3)
    for p in range(2):
        far(B, 0, p)
        far(A, 0, p)
    arrive(1, 1)
    for p in range(2):
        b_outer_along_x(p)
    go_on(A, 1, 0)
    go_on(B, 1, 0)
    near_steps(3, 8)
    go_on(A, 1, 1)
    go_on(B, 1, 1)
    arrive(2, 0)
    for p in range(2):
        from_twin(0, p, (1, 2, 3))
    b_local.wait()

    def others(p):
        def step(d, carry):
            keep_rows(lax.rem(y + d, 4), p, 0)
            keep_cols(lax.rem(z + d, 4), p, 0)
            return carry

        lax.fori_loop(0, 4, step, 0)

    far(A, 1, 0)
    far(B, 1, 0)
    from_twin(1, 0, (0, 1, 2, 3))
    others(0)
    arrive(2, 1)
    far(A, 1, 1)
    far(B, 1, 1)
    go_on(A, 2, 0)
    go_on(B, 2, 0)
    from_twin(1, 1, (0, 1, 2, 3))
    others(1)
    for i in range(2):
        give[i] = total[i, 0].astype(jnp.bfloat16)
    copies.send(give.at[0], take.at[0], last_sem.at[0], device(y, xh, z, 1 - xl, core))
    copies.send(give.at[1], take.at[1], last_sem.at[1], device(y, 1 - xh, z, xl, core))
    from_twin(2, 0, (0, 1, 3))

    def own(p):
        def step(d):
            keep_rows(y_at[d], p, 1)
            keep_cols(z_at[d], p, 1)

        return step

    for d in (0, 1, 3):
        own(0)(d)
    go_on(A, 2, 1)
    go_on(B, 2, 1)
    from_twin(2, 1, (0, 1, 3))
    for d in (0, 1, 3):
        own(1)(d)
    ahead()
    landed(take.at[0], last_sem.at[0])
    landed(take.at[1], last_sem.at[1])
    total[0, 1] += take[0].astype(jnp.float32) + take[1].astype(jnp.float32)
    far(B, 2, 0)
    far(A, 2, 0)
    keep_rows(y_at[2], 0, 1)
    from_twin(2, 0, (2,))
    keep_cols(z_at[2], 0, 1)
    far(B, 2, 1)
    far(A, 2, 1)
    keep_rows(y_at[2], 1, 1)
    from_twin(2, 1, (2,))
    keep_cols(z_at[2], 1, 1)
    out_ref[...] = (total[0, 1] + total[1, 1]).astype(jnp.bfloat16)

    def finish():
        copies.finish()

        @pl.when(core == 0)
        def _():
            pltpu.make_async_copy(a_ref, a0.at[z], own_sem).wait()

        @pl.when(core == 1)
        def _():
            pltpu.make_async_copy(a_ref.at[own0], a1_own, own_sem).wait()

    return finish


LATE = 1152


def contract_part(
    s_ref,
    panel_t,
    dressed,
    out_ref,
    energy_ref,
    block,
    part,
    far_y,
    near_y,
    cross_y,
    cross_x,
    far_x,
    near_x,
    total,
    other,
    dressed_b,
    tile,
    row_sum,
    tile_row,
    tile_col,
    send_sem,
    block_sem,
    far_sem,
    near_sem,
    cross_sem,
    row_sem,
    col_sem,
):
    y, xh, z, xl, core = place()
    col = (z * 2 + xl) * 2 + core
    f32, bf16 = jnp.float32, jnp.bfloat16

    def in_row(d, j):
        return device(lax.rem(y + d, 4), lax.rem(xh + j, 2), z, xl, core)

    order = [(2, 1), (2, 0), (1, 1), (3, 1), (1, 0), (3, 0), (0, 1), (0, 0)]
    chunk = block.shape[1]

    def fetch(i):
        d, j = order[i // 2]
        share = lax.rem(y + d, 4) * 2 + lax.rem(xh + j, 2)
        return pltpu.make_async_copy(
            panel_t.at[share, pl.ds(i % 2 * chunk, chunk)], block.at[i % 2], block_sem.at[i % 2]
        )

    fetch(0).start()
    fetch(1).start()
    yield

    copies = Copies(send_sem)
    rows = TILE * 32
    early = rows - LATE
    h_late, h_early = LATE // 2, early // 2
    up, down, across = in_row(1, 0), in_row(3, 0), in_row(0, 1)

    def late(d, j, start=0, count=LATE):
        return part.at[d * 2 + j, pl.ds(start, count)]

    def first(d, j, start=0, count=early):
        return part.at[d * 2 + j, pl.ds(LATE + start, count)]

    for i, (d, j) in enumerate(order):
        for h in range(2):
            fetch(i * 2 + h).wait()

            def multiply(t, carry):
                at = pl.ds(pl.multiple_of(t * 256, 256), 256)
                to = pl.ds(pl.multiple_of(h * chunk + t * 256, 256), 256)
                part[d * 2 + j, to] = jnp.dot(
                    block[h, at], s_ref[...], preferred_element_type=f32
                ).astype(bf16)
                return carry

            lax.fori_loop(0, chunk // 256, multiply, 0)
            if i < 7:
                fetch(i * 2 + 2 + h).start()
        if j == 1:
            copies.send(first(d, 1), cross_x.at[d], cross_sem.at[d], across)
        if d == 2:
            copies.send(late(2, j, 0, h_late), far_y.at[j, 0], far_sem.at[j, 0], up)
            copies.send(late(2, j, h_late, h_late), far_y.at[j, 1], far_sem.at[j, 1], down)
        if d == 1:
            copies.send(late(1, j, h_late, h_late), near_y.at[j, 0, pl.ds(h_late, h_late)], near_sem.at[j, 0, 0], up)
        if d == 3:
            copies.send(late(3, j, 0, h_late), near_y.at[j, 1, pl.ds(0, h_late)], near_sem.at[j, 1, 0], down)

    def add(ref, *others):
        result = ref[...].astype(f32)
        for each in others:
            result = result + each[...].astype(f32)
        ref[...] = result.astype(bf16)

    def share(d, j):
        return lax.rem(y + d, 4) * 2 + lax.rem(xh + j, 2)

    turns = [(1, 1), (3, 1), (1, 0), (3, 0), (2, 0), (2, 1), (0, 1), (0, 0)]

    def fetch_dressed(i):
        return pltpu.make_async_copy(dressed.at[share(*turns[i])], dressed_b, block_sem.at[2])

    fetch_dressed(0).start()
    tile[...] = jnp.zeros_like(tile)

    def energy(i):
        d, j = turns[i]
        fetch_dressed(i).wait()
        for h in range(2):
            lanes = slice(h * 128, (h + 1) * 128)
            other[h] = dressed_b[:, lanes].astype(f32)
            total[h] = part[d * 2 + j, :, lanes].astype(f32)
        if i < 7:
            fetch_dressed(i + 1).start()

        def column(ref, l):
            halves = [ref[h, pl.ds(l, TILE, stride=32), :].astype(bf16) for h in range(2)]
            return jnp.concatenate(halves, 1)

        def body(k, carry):
            for l in range(4):
                carry = carry + lax.dot_general(
                    column(total, k * 4 + l),
                    column(other, k * 4 + l),
                    (((1,), (1,)), ((), ())),
                    preferred_element_type=f32,
                )
            return carry

        tile[:, :TILE] += lax.fori_loop(0, 8, body, jnp.zeros((TILE, TILE), f32))

    def forward_y(j):
        landed(far_y.at[j, 0], far_sem.at[j, 0])
        add(late(1, j, 0, h_late), far_y.at[j, 0])
        copies.send(late(1, j, 0, h_late), near_y.at[j, 0, pl.ds(0, h_late)], near_sem.at[j, 0, 1], up)
        landed(far_y.at[j, 1], far_sem.at[j, 1])
        add(late(3, j, h_late, h_late), far_y.at[j, 1])
        copies.send(late(3, j, h_late, h_late), near_y.at[j, 1, pl.ds(h_late, h_late)], near_sem.at[j, 1, 1], down)

    def both_near(j, ref):
        count = ref.shape[1] // 2
        for side in range(2):
            for turn in range(2):
                start = count if (side == 0) == (turn == 0) else 0
                landed(ref.at[side, pl.ds(start, count)], near_sem.at[j, side, turn])

    def share_of(row):
        return pl.ds(pl.multiple_of(row * 8, 8), 8)

    def settle(at, *terms):
        result = terms[0][...].astype(f32)
        for each in terms[1:]:
            result = result + each[...].astype(f32)
        out_ref[at] = result.astype(bf16)

    energy(0)
    energy(1)
    forward_y(1)
    energy(2)
    energy(3)
    forward_y(0)
    energy(4)
    landed(cross_x.at[2], cross_sem.at[2])
    add(first(2, 0), cross_x.at[2])
    copies.send(first(2, 0, 0, h_early), far_x.at[0], far_sem.at[2, 0], up)
    copies.send(first(2, 0, h_early, h_early), far_x.at[1], far_sem.at[2, 1], down)
    energy(5)
    landed(cross_x.at[1], cross_sem.at[1])
    add(first(1, 0), cross_x.at[1])
    copies.send(first(1, 0, h_early, h_early), near_x.at[0, pl.ds(h_early, h_early)], near_sem.at[2, 0, 0], up)
    energy(6)
    energy(7)
    for s in range(1, 8):
        target = in_row(s // 2, s % 2)
        copies.send(tile.at[share_of(target[0])], tile_row.at[s], row_sem.at[s], target)
    landed(cross_x.at[3], cross_sem.at[3])
    add(first(3, 0), cross_x.at[3])
    copies.send(first(3, 0, 0, h_early), near_x.at[1, pl.ds(0, h_early)], near_sem.at[2, 1, 0], down)
    both_near(1, near_y.at[1])
    add(late(0, 1), near_y.at[1, 0], near_y.at[1, 1])
    copies.send(late(0, 1), cross_y, cross_sem.at[4], across)

    landed(far_x.at[0], far_sem.at[2, 0])
    add(first(1, 0, 0, h_early), far_x.at[0])
    copies.send(first(1, 0, 0, h_early), near_x.at[0, pl.ds(0, h_early)], near_sem.at[2, 0, 1], up)
    landed(far_x.at[1], far_sem.at[2, 1])
    add(first(3, 0, h_early, h_early), far_x.at[1])
    copies.send(first(3, 0, h_early, h_early), near_x.at[1, pl.ds(h_early, h_early)], near_sem.at[2, 1, 1], down)

    mine = tile[share_of(y * 2 + xh)]
    for s in range(1, 8):
        landed(tile_row.at[s], row_sem.at[s])
        mine = mine + tile_row[s]
    along_z = [device(y, xh, lax.rem(z + d, 4), xl, core) for d in range(1, 4)]
    close = [device(y, xh, z, xl, 1 - core), device(y, xh, z, 1 - xl, core), device(y, xh, z, 1 - xl, 1 - core)]
    for turn, targets in enumerate((along_z, close)):
        row_sum[turn] = mine
        for d, target in enumerate(targets):
            copies.send(row_sum.at[turn], tile_col.at[turn * 3 + d], col_sem.at[turn * 3 + d], target)
        for d in range(turn * 3, turn * 3 + 3):
            landed(tile_col.at[d], col_sem.at[d])
            mine = mine + tile_col[d]

    copies.finish(but=9)
    yield

    both_near(0, near_y.at[0])
    for h in range(2):
        lanes = slice(h * 128, (h + 1) * 128)
        total[h, :LATE] = (
            part[0, :LATE, lanes].astype(f32) + near_y[0, 0, :, lanes].astype(f32) + near_y[0, 1, :, lanes].astype(f32)
        )
    turned = pltpu.roll(-mine, lax.rem(128 - 4 * col, 128), 1).T
    energy_ref[...] = turned[:4]
    landed(cross_x.at[0], cross_sem.at[0])
    both_near(2, near_x)
    settle(pl.ds(LATE, early), first(0, 0), cross_x.at[0], near_x.at[0], near_x.at[1])
    yield

    landed(cross_y, cross_sem.at[4])
    for h in range(2):
        lanes = slice(h * 128, (h + 1) * 128)
        out_ref[:LATE, lanes] = (total[h, :LATE] + cross_y[:, lanes].astype(f32)).astype(bf16)
    copies.finish()


SCREEN_SCRATCH = 26


def kernel(*refs):
    inputs, (screened_out, contracted_out, energy, panel_t, dressed), scratch = refs[:7], refs[7:12], refs[12:]
    (screened, contracted, out_sem), scratch = scratch[:3], scratch[3:]
    first, second = scratch[:SCREEN_SCRATCH], scratch[SCREEN_SCRATCH:]
    flat = first[9]
    leaving = [
        pltpu.make_async_copy(screened, screened_out, out_sem.at[0]),
        pltpu.make_async_copy(contracted.at[pl.ds(LATE, TILE * 32 - LATE)], contracted_out.at[pl.ds(LATE, TILE * 32 - LATE)], out_sem.at[1]),
        pltpu.make_async_copy(contracted.at[pl.ds(0, LATE)], contracted_out.at[pl.ds(0, LATE)], out_sem.at[2]),
    ]
    steps = contract_part(screened, panel_t, dressed, contracted, energy, *second[:8], flat, *second[8:])
    finish = screen_part(*inputs, screened, panel_t, dressed, lambda: next(steps), *first)
    leaving[0].start()
    next(steps)
    finish()
    next(steps)
    leaving[1].start()
    next(steps, None)
    leaving[2].start()
    for copy in leaving:
        copy.wait()


def tile_terms(a, b, panel, near, panel_mask, near_mask, green):
    rows, depth = a.shape
    cols = b.shape[1]
    long = TILE * 32
    early = long - LATE
    bf16, f32 = jnp.bfloat16, jnp.float32
    dma = pltpu.SemaphoreType.DMA
    hbm, vmem = pl.BlockSpec(memory_space=pl.ANY), pl.BlockSpec(memory_space=pltpu.VMEM)
    first = [
        pltpu.VMEM((4, rows, depth), bf16),
        pltpu.VMEM((4, 2, rows, depth), bf16),
        pltpu.VMEM((4, 2, depth, cols), bf16),
        pltpu.VMEM((4, depth, cols), bf16),
        pltpu.VMEM((rows // 2, depth), bf16),
        pltpu.VMEM((2, 2, rows, cols), f32),
        pltpu.VMEM((2, rows, cols), bf16),
        pltpu.VMEM((2, rows, cols), bf16),
        pltpu.VMEM((2, 128, 16, NL), bf16),
        pltpu.VMEM((2, 128 * 16, 128), f32),
        pltpu.VMEM((2, 8, 16 * 32, 128), bf16),
        pltpu.VMEM(panel_mask.shape, jnp.int32),
        pltpu.VMEM(near_mask.shape, jnp.int32),
        pltpu.VMEM((rows, NL), f32),
        pltpu.VMEM((cols, NL), f32),
        pltpu.VMEM((NL, NL), bf16),
        dma((96,)),
        dma,
        dma((3,)),
        dma((2, 2, 2)),
        dma((6, 2, 2)),
        dma((6, 2, 2)),
        dma((3, 4, 2)),
        dma((2,)),
        dma((4,)),
        dma((3,)),
    ]
    second = [
        pltpu.VMEM((2, long // 2, rows), bf16),
        pltpu.VMEM((8, long, cols), bf16),
        pltpu.VMEM((2, 2, LATE // 2, cols), bf16),
        pltpu.VMEM((2, 2, LATE, cols), bf16),
        pltpu.VMEM((LATE, cols), bf16),
        pltpu.VMEM((4, early, cols), bf16),
        pltpu.VMEM((2, early // 2, cols), bf16),
        pltpu.VMEM((2, early, cols), bf16),
        pltpu.VMEM((2, long, 128), f32),
        pltpu.VMEM((long, cols), bf16),
        pltpu.VMEM((TILE, 128), f32),
        pltpu.VMEM((2, 8, 128), f32),
        pltpu.VMEM((8, 8, 128), f32),
        pltpu.VMEM((6, 8, 128), f32),
        dma((48,)),
        dma((3,)),
        dma((3, 2)),
        dma((3, 2, 2)),
        dma((5,)),
        dma((8,)),
        dma((6,)),
    ]
    assert len(first) == SCREEN_SCRATCH
    return pl.pallas_call(
        kernel,
        out_shape=(
            jax.ShapeDtypeStruct((rows, cols), bf16),
            jax.ShapeDtypeStruct((long, cols), bf16),
            jax.ShapeDtypeStruct((4, 8), f32),
            jax.ShapeDtypeStruct((8, long, rows), bf16),
            jax.ShapeDtypeStruct((8, long, cols), bf16),
        ),
        in_specs=[hbm] * 7,
        out_specs=(hbm, hbm, vmem, hbm, hbm),
        scratch_shapes=[pltpu.VMEM((rows, cols), bf16), pltpu.VMEM((long, cols), bf16), dma((3,))] + first + second,
        compiler_params=pltpu.CompilerParams(
            collective_id=0, has_side_effects=True, vmem_limit_bytes=64 * 2**20 - 2**16
        ),
        name="tile_terms",
    )(a, b, panel, near, panel_mask, near_mask, green)


def hand_over_kernel(*refs):
    sources, results, held, sem = refs[:3], refs[3:6], refs[6:9], refs[9]
    pieces = []
    for k, source in enumerate(sources):
        count = 4 if k == 1 else 1
        size = source.shape[0] // count
        pieces += [(k, pl.ds(i * size, size)) for i in range(count)]
    taken = [pltpu.make_async_copy(sources[k].at[at], held[k].at[at], sem.at[0, i]) for i, (k, at) in enumerate(pieces)]
    given = [pltpu.make_async_copy(held[k].at[at], results[k].at[at], sem.at[1, i]) for i, (k, at) in enumerate(pieces)]
    for copy in taken:
        copy.start()
    for i, copy in enumerate(given):
        taken[i].wait()
        copy.start()
    for copy in given:
        copy.wait()


def hand_over(*arrays):
    hbm = pl.BlockSpec(memory_space=pl.ANY)
    return pl.pallas_call(
        hand_over_kernel,
        out_shape=tuple(jax.ShapeDtypeStruct(array.shape, array.dtype) for array in arrays),
        in_specs=[hbm] * 3,
        out_specs=(hbm,) * 3,
        scratch_shapes=[pltpu.VMEM(array.shape, array.dtype) for array in arrays]
        + [pltpu.SemaphoreType.DMA((2, 6))],
        name="hand_over",
    )(*arrays)


def per_device(
    polarization, metric, three_panel, three_near, green_function, mask_panel, mask_near
):
    near_cols = metric.shape[1]
    screened, contracted, energy, *_ = tile_terms(
        polarization, metric, three_panel, three_near, mask_panel.T, mask_near.T, green_function
    )
    screened, contracted, energy = hand_over(screened, contracted, energy)
    return screened, contracted.T.reshape(near_cols, TILE, contracted.shape[0] // TILE), energy.T


def solution(mesh):
    placed = (
        P("row", "col"),
        P("row", "col"),
        P("row", None, None),
        P("col", None, None),
        P(),
        P(),
        P(),
    )
    return jax.shard_map(
        per_device,
        mesh=mesh,
        in_specs=placed,
        out_specs=(P("row", "col"), P("col", None, "row"), P("row", "col")),
        check_vma=False,
    )
```
